32 devices in a mesh: dir: 2 (over core), seq: 16 (over z, y, x).
Axes of the slice: x: 2, y: 2, z: 4, core: 2. Of those that a mesh axis runs over, the one named last changes fastest.
Arguments:
- tokens: bfloat16 [2048, 256], P('seq'), may hold values from -6 to 6
- gain: float32 [256], replicated, may hold values from 0.5 to 1.5
- w_in: bfloat16 [256, 1024], replicated, may hold values from -0.375 to 0.375
- w_out: bfloat16 [512, 256], replicated, may hold values from -0.25 to 0.25
- conv_w: float32 [2, 4, 512], P('dir'), may hold values from -3 to 3
- conv_b: float32 [2, 512], P('dir'), may hold values from -3 to 3
- w_x: bfloat16 [2, 512, 48], P('dir'), may hold values from -0.25 to 0.25
- w_dt: bfloat16 [2, 16, 512], P('dir'), may hold values from -1.5 to 1.5
- dt_bias: float32 [2, 512], P('dir'), may hold values from -9 to -1
- a_log: float32 [2, 16, 512], P('dir'), may hold values from 0 to 2.77
- d_skip: float32 [2, 512], P('dir'), may hold values from 0.5 to 1.5
- lengths: int32 [8], replicated, may hold values from 1 to 1920, as said below
- cotangent: bfloat16 [2048, 256], P('seq'), may hold values from -6 to 6
Outputs:
- out: bfloat16 [2048, 256], P('seq')
- in_grad: float32 [2048, 256], P('seq')
- grad_gain: float32 [256], replicated
- grad_w_in: float32 [256, 1024], replicated
- grad_w_out: float32 [512, 256], replicated
- grad_conv_w: float32 [2, 4, 512], P('dir')
- grad_conv_b: float32 [2, 512], P('dir')
- grad_w_x: float32 [2, 512, 48], P('dir')
- grad_w_dt: float32 [2, 16, 512], P('dir')
- grad_dt_bias: float32 [2, 512], P('dir')
- grad_a_log: float32 [2, 16, 512], P('dir')
- grad_d_skip: float32 [2, 512], P('dir')
The draws below stay inside these ranges and needn't reach their ends.
Inputs may be any that keep to these rules, and one draw needn't show every extreme that they name: 8 window lengths that sum to 2048; the fourth has length 1920, the other 7 together hold 128 tokens, of which the first three hold at most 124, so the fourth window begins on the first index of seq and ends on the last.
All inputs are finite; a program needn't handle non-finite values.
Results may differ from the reference program's by a relative error of at most 0.011.
The reference program's roundings to bfloat16 on the way count: a program that leaves them out, or rounds other values in their place, can miss the bound.
Values may be sent and summed in bfloat16 or wider, within the bound.
A program may use at most 128 MiB of HBM per device.

```python
import math
import jax
import jax.numpy as jnp
from jax import lax

D = 256
INNER = 512
STATE = 16
RANK = 16
TOK_DEV = 128
NWIN = 8
TOKENS = 2048


def draw_lengths(key, part):
    key = jax.random.fold_in(key, 11)
    shuffled = jax.random.permutation(key, TOK_DEV - 1).astype(jnp.int32) + 1
    cut_points = jnp.sort(shuffled[:NWIN - 2])
    bounds = jnp.concatenate([jnp.zeros((1,), jnp.int32), cut_points, jnp.full((1,), TOK_DEV, jnp.int32)])
    short_len = (bounds[1:] - bounds[:-1]).astype(jnp.int32)
    long_len = jnp.full((1,), TOKENS - TOK_DEV, jnp.int32)
    return jnp.concatenate([short_len[:3], long_len, short_len[3:]]).astype(jnp.int32)


def steps_of(own_key, dims, cuts, low, top_value):
    level = 1.0
    for dim, parts in cuts:
        steps = jax.random.uniform(jax.random.fold_in(jax.random.fold_in(own_key, 6), dim), (parts,), jnp.float32, low / len(cuts), top_value / len(cuts))
        level = level * jnp.repeat(jnp.exp(steps), dims[dim] // parts).reshape((-1,) + (1,) * (len(dims) - 1 - dim))
    return level


def normal_values(stream_key, shape, spread, most, shards=(), kind=jnp.bfloat16):
    values = jax.random.normal(stream_key, shape, jnp.float32) * spread
    if len(shards) > 0:
        values = steps_of(stream_key, shape, shards, -0.22, 0.18) * values
    return jnp.clip(values, min=-most, max=most).astype(kind)


def setup_inputs(seed: int = 0) -> dict:
    seeds = jax.random.split(jax.random.key(seed), 14)
    return {
        "tokens": normal_values(seeds[0], (TOKENS, D), 1.0, 6.0, ((0, 16),)),
        "gain": jnp.clip(1.0 + 0.1 * jax.random.normal(seeds[1], (D,), jnp.float32), 0.5, 1.5),
        "w_in": normal_values(seeds[2], (D, 2 * INNER), D ** -0.5, 0.375),
        "w_out": normal_values(seeds[3], (INNER, D), INNER ** -0.5, 0.25),
        "conv_w": normal_values(seeds[4], (2, 4, INNER), 0.5, 3.0, ((0, 2),), jnp.float32),
        "conv_b": normal_values(seeds[5], (2, INNER), 0.5, 3.0, ((0, 2),), jnp.float32),
        "w_x": normal_values(seeds[6], (2, INNER, RANK + 2 * STATE), INNER ** -0.5, 0.25, ((0, 2),)),
        "w_dt": normal_values(seeds[7], (2, RANK, INNER), RANK ** -0.5, 1.5, ((0, 2),)),
        "dt_bias": jnp.clip(-9.0 + 8.0 * jax.random.uniform(seeds[8], (2, INNER), jnp.float32) ** steps_of(seeds[8], (2, INNER), ((0, 2),), -0.2, 0.2), -9.0, -1.0),
        "a_log": jnp.clip(2.77 * jax.random.uniform(seeds[9], (2, STATE, INNER), jnp.float32) ** steps_of(seeds[9], (2, STATE, INNER), ((0, 2),), -0.2, 0.2), 0.0, 2.77),
        "d_skip": jnp.clip(0.5 + 1.0 * jax.random.uniform(seeds[10], (2, INNER), jnp.float32) ** steps_of(seeds[10], (2, INNER), ((0, 2),), -0.2, 0.2), 0.5, 1.5),
        "lengths": draw_lengths(jax.random.fold_in(seeds[13], 71), 0),
        "cotangent": normal_values(seeds[12], (TOKENS, D), 1.0, 6.0, ((0, 16),)),
    }


NORM_EPS = 1e-05

@jax.custom_vjp
def low(v):
    return lax.optimization_barrier(v.astype(jnp.bfloat16)).astype(jnp.float32)

@jax.custom_vjp
def low_back(v):
    return v

def low_keep(v):
    return (low(v), None)

def low_pass(kept, grad):
    return (grad,)

def back_keep(v):
    return (v, None)

def back_low(kept, grad):
    return (low(grad),)
low.defvjp(low_keep, low_pass)
low_back.defvjp(back_keep, back_low)

def combine(earlier, later):
    return (earlier[0] * later[0], later[0] * earlier[1] + later[1])

def window_dist(lengths, places, slot_index):
    ends_at = jnp.cumsum(lengths)
    starts_at = ends_at - lengths
    below = lax.optimization_barrier(jnp.sum(jnp.where(ends_at[None, :] <= places[:, None], lengths[None, :], 0), axis=1))
    upper = lax.optimization_barrier(jnp.sum(jnp.where(starts_at[None, :] <= places[:, None], lengths[None, :], 0), axis=1))
    return jnp.where(slot_index == 1, upper - 1 - places, places - below).astype(jnp.int32)

def scan_blocks(step_dt, act_out, in_b, out_c, keep_mask, decay_rate):
    total_rows = step_dt.shape[0]
    block_len = math.gcd(total_rows, 512)
    block_count = total_rows // block_len

    def one_block(carry, pieces):
        dt_blk, act_blk, b_blk, c_blk, keep_blk = pieces
        decay_fac = jnp.exp(dt_blk[:, None, :] * decay_rate[None]) * keep_blk[:, None, None]
        drive_term = (dt_blk * act_blk)[:, None, :] * b_blk[:, :, None]
        cum_a, cum_b = lax.associative_scan(combine, (decay_fac, drive_term), axis=0)
        states = cum_b + cum_a * carry[None]
        return (states[-1], lax.optimization_barrier(jnp.sum(states * c_blk[:, :, None], axis=1)))
    shaped = tuple((piece.reshape((block_count, block_len) + piece.shape[1:]) for piece in (step_dt, act_out, in_b, out_c, keep_mask)))
    init_state = jnp.zeros(decay_rate.shape, step_dt.dtype)
    last_state, outputs = lax.scan(jax.checkpoint(one_block), init_state, shaped)
    return outputs.reshape(total_rows, -1)

def branch(rows_in, distance, gain, w_in, w_out, conv_w, conv_b, w_x, w_dt, dt_bias, a_log, d_skip):
    highest = lax.Precision.HIGHEST
    inner_width = w_out.shape[0]
    rank_width = w_dt.shape[0]
    state_count = a_log.shape[0]
    mean_sq = lax.optimization_barrier(jnp.mean(rows_in * rows_in, axis=1, keepdims=True))
    normed = low(rows_in * lax.rsqrt(mean_sq + NORM_EPS) * gain[None, :])
    proj_out = low_back(jnp.dot(normed, w_in, precision=highest))
    xi_low = low(proj_out[:, :inner_width])
    zgate = proj_out[:, inner_width:]
    conv_sum = jnp.zeros_like(xi_low) + conv_b[None, :]
    for offset in range(4):
        tap_rows = jnp.concatenate([jnp.zeros((offset, inner_width), xi_low.dtype), xi_low[:xi_low.shape[0] - offset]], 0)
        conv_sum = conv_sum + jnp.where((distance >= offset)[:, None], tap_rows * conv_w[offset][None, :], 0.0)
    conv_sum = low_back(conv_sum)
    act_out = low(jax.nn.silu(conv_sum))
    proj_x = low_back(jnp.dot(act_out, w_x, precision=highest))
    dt_low = low(proj_x[:, :rank_width])
    in_b = proj_x[:, rank_width:rank_width + state_count]
    out_c = proj_x[:, rank_width + state_count:]
    pre_dt = low_back(jnp.dot(dt_low, w_dt, precision=highest)) + dt_bias[None, :]
    step_dt = jax.nn.softplus(pre_dt)
    decay_rate = -jnp.exp(a_log)
    keep_mask = (distance > 0).astype(step_dt.dtype)
    y_scan = scan_blocks(step_dt, act_out, in_b, out_c, keep_mask, decay_rate)
    y_full = y_scan + d_skip[None, :] * act_out
    mixed_out = low(y_full * jax.nn.silu(zgate))
    return jnp.dot(mixed_out, w_out, precision=highest)

def reference(tokens, gain, w_in, w_out, conv_w, conv_b, w_x, w_dt, dt_bias, a_log, d_skip, lengths, cotangent):
    total_rows = tokens.shape[0]
    places = jnp.arange(total_rows, dtype=jnp.int32)
    dist_fwd = window_dist(lengths, places, 0)
    dist_rev = window_dist(lengths, (total_rows - 1 - places).astype(jnp.int32), 1)

    def forward(rows_f, gain_f, win_f, wout_f, cw_f, cb_f, wx_f, wdt_f, bias_f, alog_f, skip_f):
        first_out = branch(rows_f, dist_fwd, gain_f, win_f, wout_f, cw_f[0], cb_f[0], wx_f[0], wdt_f[0], bias_f[0], alog_f[0], skip_f[0])
        second = branch(rows_f[::-1, ::-1], dist_rev, gain_f, win_f, wout_f, cw_f[1], cb_f[1], wx_f[1], wdt_f[1], bias_f[1], alog_f[1], skip_f[1])
        return rows_f + first_out + second[::-1, ::-1]
    as_f32 = jnp.float32
    primals = (tokens.astype(as_f32), gain.astype(as_f32), w_in.astype(as_f32), w_out.astype(as_f32), conv_w.astype(as_f32), conv_b.astype(as_f32), w_x.astype(as_f32), w_dt.astype(as_f32), dt_bias.astype(as_f32), a_log.astype(as_f32), d_skip.astype(as_f32))
    out_value, pullback = jax.vjp(forward, *primals)
    gradients = pullback(cotangent.astype(as_f32))
    return (out_value.astype(jnp.bfloat16), gradients[0], gradients[1], gradients[2], gradients[3], gradients[4], gradients[5], gradients[6], gradients[7], gradients[8], gradients[9], gradients[10])
```

```python
import functools
import math

import jax
import jax.numpy as jnp
from jax import lax
from jax.experimental import pallas as pl
from jax.experimental.pallas import tpu as pltpu
from jax.sharding import PartitionSpec as P

F32 = jnp.float32
B16 = jnp.bfloat16
MESH = pl.DeviceIdType.MESH
NORM_EPS = 1e-05
LOG2E = 1.4426950408889634
RESET = 1e6
HALO = 16
LANES = 128
GROUP = 16


def dot(a, b, ca=1, cb=0):
    return lax.dot_general(a, b, (((ca,), (cb,)), ((), ())), preferred_element_type=F32)


def silu_grad(v, sigma):
    return sigma * (1.0 + v * (1.0 - sigma))


def softplus(v):
    u = jnp.exp(-jnp.abs(v))
    s = u / (2.0 + u)
    q = s * s
    p = 1.0 / 15.0
    for k in (13.0, 11.0, 9.0, 7.0, 5.0, 3.0):
        p = p * q + 1.0 / k
    return jnp.maximum(v, 0.0) + 2.0 * s * (p * q + 1.0)


def log_split(n):
    inner = 1
    while inner * inner * 4 <= n:
        inner *= 2
    return inner, n // inner


class Ring:
    def __init__(self, ssem, rsem, size):
        self.ssem, self.rsem, self.next, self.size, self.sent = ssem, rsem, 0, size, []

    def take(self, count):
        base = self.next
        self.next += count
        assert self.next <= self.size
        return base

    def copy(self, src, dst, s, r, dev):
        return pltpu.make_async_remote_copy(
            src_ref=src, dst_ref=dst, send_sem=self.ssem.at[s], recv_sem=self.rsem.at[r],
            device_id=dev, device_id_type=MESH,
        )


class Exchange:
    def __init__(self, ring, size, me, dev):
        self.ring, self.size, self.me, self.dev = ring, size, me, dev
        self.base = ring.take(size)

    def start(self, src, dst):
        self.src, self.dst = src, dst
        for r in range(1, self.size):
            peer = lax.rem(self.me + r, self.size)
            c = self.ring.copy(src(peer), dst(self.me), self.base + r, self.base + self.me, self.dev(peer))
            c.start()
            self.ring.sent.append(c)

    def wait(self):
        for r in range(1, self.size):
            peer = lax.rem(self.me + r, self.size)
            self.ring.copy(
                self.src(peer), self.dst(peer), self.base + r, self.base + peer, self.dev(peer)
            ).wait_recv()


class Reduce:
    def __init__(self, ring, n, seq, dirn, part, total, send1, recv1, send2, recv2, buf3):
        g1, g2 = 4, 4
        g3 = n // (g1 * g2)
        self.g = (g1, g2, g3)
        lo = lax.rem(seq, g1)
        mid = lax.rem(seq // g1, g2)
        hi = seq // (g1 * g2)
        self.ids = (lo, mid, hi)
        dev1 = lambda p: (dirn, seq - lo + p)
        dev2 = lambda p: (dirn, seq + (p - mid) * g1)
        dev3 = lambda p: (dirn, seq + (p - hi) * g1 * g2)
        self.ex = [Exchange(ring, g1, lo, dev1), Exchange(ring, g2, mid, dev2)]
        self.top = Exchange(ring, g3, hi, dev3) if g3 > 1 else None
        self.back = [Exchange(ring, g2, mid, dev2), Exchange(ring, g1, lo, dev1)]
        self.part, self.total = part, total
        self.send1, self.recv1, self.send2, self.recv2, self.buf3 = send1, recv1, send2, recv2, buf3
        self.q = part.shape[0] // g1
        self.p = self.q // g2

    def scatter1(self):
        q = self.q
        self.send1[...] = self.part[...].astype(B16)
        self.ex[0].start(
            lambda p: self.send1.at[pl.ds(pl.multiple_of(p * q, q), q)], lambda s: self.recv1.at[s]
        )

    def scatter2(self):
        q, p_ = self.q, self.p
        lo, mid, _ = self.ids
        self.recv1[lo] = jnp.zeros(self.recv1.shape[1:], B16)
        self.ex[0].wait()
        acc = self.part[pl.ds(pl.multiple_of(lo * q, q), q)]
        for j in range(self.g[0]):
            acc = acc + self.recv1[j].astype(F32)
        self.part[pl.ds(0, q)] = acc
        self.send2[...] = acc.astype(B16)
        self.ex[1].start(
            lambda p: self.send2.at[pl.ds(pl.multiple_of(p * p_, p_), p_)],
            lambda s: self.recv2.at[s],
        )

    def gather2(self):
        q, p_ = self.q, self.p
        lo, mid, hi = self.ids
        self.recv2[mid] = jnp.zeros(self.recv2.shape[1:], B16)
        self.ex[1].wait()
        acc = self.part[pl.ds(pl.multiple_of(mid * p_, p_), p_)]
        for j in range(self.g[1]):
            acc = acc + self.recv2[j].astype(F32)
        if self.top is not None:
            self.buf3[hi] = acc.astype(B16)
            self.top.start(lambda p: self.buf3.at[hi], lambda s: self.buf3.at[s])
            self.top.wait()
            acc = self.buf3[0].astype(F32)
            for j in range(1, self.g[2]):
                acc = acc + self.buf3[j].astype(F32)
        at = lambda s: pl.ds(pl.multiple_of(lo * q + s * p_, p_), p_)
        self.total[at(mid)] = acc.astype(B16)
        self.back[0].start(lambda p: self.total.at[at(mid)], lambda s: self.total.at[at(s)])

    def gather1(self):
        q = self.q
        lo = self.ids[0]
        self.back[0].wait()
        at = lambda s: pl.ds(pl.multiple_of(s * q, q), q)
        self.back[1].start(lambda p: self.total.at[at(lo)], lambda s: self.total.at[at(s)])

    def finish(self):
        self.back[1].wait()


def kernel(n, nsem, *refs):
    (tok_r, gain_r, win_r, wout_r, cw_r, cb_r, wx_r, wdt_r, bias_r, alog_r, skip_r, len_r, cot_r,
     out_r, ing_r, ggain_r, gwin_r, gwout_r, gcw_r, gcb_r, gwx_r, gwdt_r, gbias_r, galog_r, gskip_r,
     thalo, brep, crep, dref, hs, lamr, rar, sdr, sar, gyr, xpad, gpad, gext, ghalo, ghsend, ghrecv,
     xin1, xsend2, xin2, yr, mgr, mbr, adjr, dtar, bsend, brecv, vsend, vrecv,
     epair, eprecv, epart, etotal, es1, er1, es2, er2, eb3,
     lpair, lprecv, lpart, ltotal, ls1, lr1, ls2, lr2, lb3, esib, lsib,
     ssem, rsem) = refs
    rows, width = tok_r.shape
    inner = wout_r.shape[0]
    state = alog_r.shape[1]
    chunks = inner // LANES
    groups = rows // GROUP
    blk = GROUP * state
    dirn = lax.axis_index("dir")
    seq = lax.axis_index("seq")
    place = seq + dirn * (n - 1 - 2 * seq)
    seq_at = lambda p: p + dirn * (n - 1 - 2 * p)
    dev_at = lambda p: (dirn, seq_at(p))
    sibling = (1 - dirn, seq)
    g_in, g_out = log_split(n)
    lo = lax.rem(place, g_in)
    hi = place // g_in
    ring = Ring(ssem, rsem, nsem)
    up = lax.rem(place + 1, n)
    down = lax.rem(place + n - 1, n)

    barrier = pltpu.get_barrier_semaphore()
    peers = [sibling, dev_at(up), dev_at(down)]
    peers += [dev_at(hi * g_in + lax.rem(lo + r, g_in)) for r in range(1, g_in)]
    peers += [dev_at(lax.rem(hi + r, g_out) * g_in + lo) for r in range(1, g_out)]
    s_lo, s_mid, s_hi = lax.rem(seq, 4), lax.rem(seq // 4, 4), seq // 16
    if n != 16:
        peers += [(dirn, seq - s_lo + lax.rem(s_lo + r, 4)) for r in range(1, 4)]
        peers += [(dirn, seq + (lax.rem(s_mid + r, 4) - s_mid) * 4) for r in range(1, 4)]
        peers += [(dirn, seq + (lax.rem(s_hi + r, n // 16) - s_hi) * 16) for r in range(1, n // 16)]
    for dev in peers:
        pl.semaphore_signal(barrier, inc=1, device_id=dev, device_id_type=MESH)
    pl.semaphore_wait(barrier, len(peers))

    edge = pl.multiple_of((1 - dirn) * (rows - HALO), HALO)
    b0 = ring.take(1)
    tok_copy = ring.copy(tok_r.at[pl.ds(edge, HALO)], thalo, b0, b0, dev_at(up))

    @pl.when(place < n - 1)
    def _():
        tok_copy.start()

    @pl.when(place == 0)
    def _():
        thalo[...] = jnp.zeros(thalo.shape, B16)

    def turn(size):
        r = lax.broadcasted_iota(jnp.int32, (size, size), 0)
        c = lax.broadcasted_iota(jnp.int32, (size, size), 1)
        return jnp.where(c == r + dirn * (size - 1 - 2 * r), 1.0, 0.0).astype(B16)

    turn_t, turn_f, turn_h = turn(rows), turn(width), turn(HALO)
    turned = lambda v, tt: dot(dot(tt, v).astype(B16), turn_f)

    def normalise(v):
        inv = lax.rsqrt(jnp.mean(v * v, axis=1, keepdims=True) + NORM_EPS)
        vr = v * inv
        return inv, vr, (vr * gain_r[...]).astype(B16)

    inv, vr, normed = normalise(turned(tok_r[...], turn_t))
    cot = turned(cot_r[...], turn_t).astype(B16)
    proj = dot(normed, win_r[...])
    xi = proj[:, :inner].astype(B16).astype(F32)
    zgate = proj[:, inner:]
    xpad[pl.ds(HALO, rows)] = xi
    sig_z = jax.nn.sigmoid(zgate)
    gate = zgate * sig_z
    gmix = dot(cot, wout_r[...], 1, 1)
    gy = gmix * gate
    gyr[...] = gy

    total = n * rows
    q = lax.broadcasted_iota(jnp.int32, (rows + 2 * HALO, LANES), 0) + (place * rows - HALO)
    dist = jnp.full(q.shape, 1 << 30, jnp.int32)
    before = jnp.int32(0)
    for w in range(len_r.shape[0]):
        after = before + len_r[w]
        delta = q - (before + dirn * (total - after - before))
        dist = jnp.where((delta >= 0) & (delta < dist), delta, dist)
        before = after
    dist = jnp.concatenate([dist] * chunks, axis=1)
    q_all = jnp.concatenate([q] * chunks, axis=1)
    dist_own = dist[HALO:HALO + rows]

    @pl.when(place > 0)
    def _():
        tok_copy.wait_recv()

    _, vr_h, normed_h = normalise(turned(thalo[...], turn_h))
    xpad[pl.ds(0, HALO)] = dot(normed_h, win_r[:, :inner]).astype(B16).astype(F32)
    conv = jnp.zeros((rows, inner), F32) + cb_r[...]
    for k in range(4):
        tap = xpad[pl.ds(HALO - k, rows)] * cw_r[0, k:k + 1]
        conv = conv + jnp.where(dist_own >= k, tap, 0.0)
    sig_c = jax.nn.sigmoid(conv)
    act_b = (conv * sig_c).astype(B16)
    act = act_b.astype(F32)
    px = dot(wx_r[0], act_b, 0, 1)
    dt_low = px[:state].astype(B16)
    b_t = px[state:2 * state]
    c_t = px[2 * state:]
    pre = dot(dt_low, wdt_r[0], 0, 0) + bias_r[...]
    step = softplus(pre)
    sd = jnp.where(dist_own == 0, RESET, step)
    sdr[...] = sd
    sar[...] = step * act
    rate = -jnp.exp(alog_r[0])
    rate2 = rate * LOG2E
    cut = lambda v: [v[:, c * LANES:(c + 1) * LANES] for c in range(chunks)]
    a2 = cut(rate2)
    a1 = cut(rate)

    def spread(g, carry):
        shift = lax.rem(LANES - g * 8, LANES)
        br = pltpu.roll(b_t, shift, 1)
        cr = pltpu.roll(c_t, shift, 1)
        for j in range(8):
            at = pl.ds(pl.multiple_of((g * 8 + j) * state, state), state)
            brep[at] = jnp.broadcast_to(br[:, j:j + 1], (state, LANES))
            crep[at] = jnp.broadcast_to(cr[:, j:j + 1], (state, LANES))
        return carry

    lax.fori_loop(0, rows // 8, spread, 0)

    def summarise(g, carry):
        h, p, l = [list(x) for x in carry]
        at8 = pl.ds(pl.multiple_of(g * 8, 8), 8)
        sd8, sa8, gy8 = sdr[at8], sar[at8], gyr[at8]
        for j in range(8):
            at = pl.ds(pl.multiple_of((g * 8 + j) * state, state), state)
            br, cr = brep[at], crep[at]
            for c in range(chunks):
                lane = slice(c * LANES, (c + 1) * LANES)
                d = jnp.exp2(sd8[j:j + 1, lane] * a2[c])
                dref[at, lane] = d
                h[c] = d * h[c] + sa8[j:j + 1, lane] * br
                p[c] = p[c] * d
                l[c] = l[c] + p[c] * (gy8[j:j + 1, lane] * cr)
        return tuple(h), tuple(p), tuple(l)

    zero = tuple(jnp.zeros((state, LANES), F32) for _ in range(chunks))
    one = tuple(jnp.ones((state, LANES), F32) for _ in range(chunks))
    h_sum, _, l_sum = lax.fori_loop(0, rows // 8, summarise, (zero, one, zero))
    join = lambda v: jnp.concatenate(v, axis=1)

    def pair_rows(v):
        top = v.astype(B16)
        rest = (v - top.astype(F32)).astype(B16)
        r = lax.broadcasted_iota(jnp.int32, (16, v.shape[1]), 0)
        both = jnp.where(r == 0, top.astype(F32), jnp.where(r == 1, rest.astype(F32), 0.0))
        return both.astype(B16)

    unpair = lambda v: v[0:1].astype(F32) + v[1:2].astype(F32)
    xin1[lo, pl.ds(0, state)] = join(h_sum).astype(B16)
    xin1[lo, pl.ds(state, state)] = join(l_sum).astype(B16)
    xin1[lo, pl.ds(2 * state, 16)] = pair_rows(jnp.sum(sd, axis=0, keepdims=True))
    ex1 = Exchange(ring, g_in, lo, lambda p: dev_at(hi * g_in + p))
    ex1.start(lambda p: xin1.at[lo], lambda s: xin1.at[s])
    ex1.wait()
    sums = [unpair(xin1[j, pl.ds(2 * state, 16)]) for j in range(g_in)]
    fwd = bwd = fwd_all = bwd_all = jnp.zeros((state, inner), F32)
    s_fwd = s_bwd = s_all = jnp.zeros((1, inner), F32)
    for j in range(g_in):
        fade = jnp.exp2(rate2 * sums[j])
        fwd_all = fade * fwd_all + xin1[j, pl.ds(0, state)].astype(F32)
        fwd = jnp.where(j < lo, fwd_all, fwd)
        s_all = s_all + sums[j]
        s_fwd = jnp.where(j < lo, s_all, s_fwd)
    for j in reversed(range(g_in)):
        fade = jnp.exp2(rate2 * sums[j])
        bwd_all = fade * bwd_all + xin1[j, pl.ds(state, state)].astype(F32)
        bwd = jnp.where(j > lo, bwd_all, bwd)
        s_bwd = jnp.where(j > lo, s_bwd + sums[j], s_bwd)
    s_pair = pair_rows(s_all)
    xsend2[0, pl.ds(0, state)] = fwd_all.astype(B16)
    xsend2[0, pl.ds(state, 16)] = s_pair
    xsend2[1, pl.ds(0, state)] = bwd_all.astype(B16)
    xsend2[1, pl.ds(state, 16)] = s_pair
    xin2[hi] = jnp.zeros(xin2.shape[1:], B16)
    ex2 = Exchange(ring, g_out, hi, lambda p: dev_at(p * g_in + lo))
    ex2.start(lambda p: xsend2.at[jnp.where(p > hi, 0, 1)], lambda s: xin2.at[s])
    ex2.wait()
    h_in = l_in = jnp.zeros((state, inner), F32)
    for k in range(g_out):
        new = jnp.exp2(rate2 * unpair(xin2[k, pl.ds(state, 16)])) * h_in
        h_in = jnp.where(k < hi, new + xin2[k, pl.ds(0, state)].astype(F32), h_in)
    for k in reversed(range(g_out)):
        new = jnp.exp2(rate2 * unpair(xin2[k, pl.ds(state, 16)])) * l_in
        l_in = jnp.where(k > hi, new + xin2[k, pl.ds(0, state)].astype(F32), l_in)
    h_in = jnp.exp2(rate2 * s_fwd) * h_in + fwd
    l_in = jnp.exp2(rate2 * s_bwd) * l_in + bwd

    hs[pl.ds(0, state)] = h_in

    def forward(g, h):
        h = list(h)
        at8 = pl.ds(pl.multiple_of(g * 8, 8), 8)
        sa8 = sar[at8]
        for j in range(8):
            at = pl.ds(pl.multiple_of((g * 8 + j) * state, state), state)
            nxt = pl.ds(pl.multiple_of((g * 8 + j + 1) * state, state), state)
            br = brep[at]
            for c in range(chunks):
                lane = slice(c * LANES, (c + 1) * LANES)
                h[c] = dref[at, lane] * h[c] + sa8[j:j + 1, lane] * br
                hs[nxt, lane] = h[c]
        return tuple(h)

    lax.fori_loop(0, rows // 8, forward, tuple(cut(h_in)))

    lane_n = lax.broadcasted_iota(jnp.int32, (state, blk), 1)
    row_n = lax.broadcasted_iota(jnp.int32, (state, blk), 0)
    rep = jnp.where(lax.rem(lane_n, state) == row_n, 1.0, 0.0).astype(B16)
    lane_t = lax.broadcasted_iota(jnp.int32, (rows, blk), 1) // state
    row_t = lax.rem(lax.broadcasted_iota(jnp.int32, (rows, blk), 0), GROUP)
    on = lane_t == row_t
    bdiag = jnp.where(on, dot(b_t.astype(B16), rep, 0, 0), 0.0).astype(B16)
    cdiag = jnp.where(on, dot(c_t.astype(B16), rep, 0, 0), 0.0).astype(B16)
    odiag = jnp.where(on, 1.0, 0.0).astype(B16)
    gy_b = gy.astype(B16)
    sa_b = (step * act).astype(B16)
    for g in range(groups):
        t = slice(g * GROUP, (g + 1) * GROUP)
        xh = hs[pl.ds(g * blk + state, blk)].astype(B16)
        yr[pl.ds(g * GROUP, GROUP)] = dot(cdiag[t], xh)
        mgr[pl.ds(g * GROUP, GROUP)] = dot(gy_b[t], xh, 1, 1)
    y = yr[...] + skip_r[...] * act
    mixed = (y * gate).astype(B16)
    bsend[...] = dot(dot(turn_t, mixed).astype(B16), dot(wout_r[...], turn_f).astype(B16))
    bb = ring.take(1)
    b_copy = ring.copy(bsend, brecv, bb, bb, sibling)
    b_copy.start()
    ring.sent.append(b_copy)
    gz = (gmix * y * silu_grad(zgate, sig_z)).astype(B16)
    gskip = jnp.sum(gy * act, axis=0, keepdims=True)

    half = width
    gwz = dot(normed, gz, 0, 0)
    gwo = dot(mixed, cot, 0, 0)
    gwo = jnp.concatenate([gwo[:width], gwo[width:]], axis=1)
    epair[0] = gwz.astype(B16)
    epair[1] = gwo.astype(B16)
    epart[...] = jnp.where(dirn == 0, gwz, gwo)
    be = ring.take(1)
    e_copy = ring.copy(epair.at[1 - dirn], eprecv, be, be, sibling)
    e_copy.start()
    ring.sent.append(e_copy)

    def backward(i, carry):
        m, acc = [list(x) for x in carry]
        g = rows // 8 - 1 - i
        at8 = pl.ds(pl.multiple_of(g * 8, 8), 8)
        sd8, gy8 = sdr[at8], gyr[at8]
        for j in reversed(range(8)):
            at = pl.ds(pl.multiple_of((g * 8 + j) * state, state), state)
            cr = crep[at]
            for c in range(chunks):
                lane = slice(c * LANES, (c + 1) * LANES)
                lam = m[c] + gy8[j:j + 1, lane] * cr
                lamr[at, lane] = lam
                m[c] = dref[at, lane] * lam
                r = m[c] * hs[at, lane] * a1[c]
                rar[at, lane] = r
                acc[c] = acc[c] + r * sd8[j:j + 1, lane]
        return tuple(m), tuple(acc)

    _, galog = lax.fori_loop(0, rows // 8, backward, (tuple(cut(l_in)), zero))
    galog = join(galog)

    early = Reduce(ring, n, seq, dirn, epart, etotal, es1, er1, es2, er2, eb3)
    e_copy.wait_recv()
    epart[...] = epart[...] + eprecv[...].astype(F32)
    early.scatter1()

    for g in range(groups):
        t = slice(g * GROUP, (g + 1) * GROUP)
        at = pl.ds(g * blk, blk)
        xl = lamr[at].astype(B16)
        adjr[pl.ds(g * GROUP, GROUP)] = dot(bdiag[t], xl)
        mbr[pl.ds(g * GROUP, GROUP)] = dot(sa_b[t], xl, 1, 1)
        dtar[pl.ds(g * GROUP, GROUP)] = dot(odiag[t], rar[at].astype(B16))
    adj = adjr[...]
    gpre = (dtar[...] + adj * act) * jax.nn.sigmoid(pre)
    gbias = jnp.sum(gpre, axis=0, keepdims=True)
    gpre = gpre.astype(B16)
    gwdt = dot(dt_low, gpre)
    pick = jnp.where(on, 1.0, 0.0)
    sel = lambda m: dot(rep, jnp.where(on, m, 0.0).astype(B16), 1, 1)
    gpx = jnp.concatenate([dot(wdt_r[0], gpre, 1, 1), sel(mbr[...]), sel(mgr[...])], axis=0).astype(B16)
    gwx_t = dot(gpx, act_b)
    gact = gy * skip_r[...] + adj * step + dot(gpx, wx_r[0], 0, 1)
    gconv_b = (gact * silu_grad(conv, sig_c)).astype(B16)
    ghsend[...] = gconv_b[:HALO]
    bh = ring.take(1)
    h_copy = ring.copy(ghsend, ghrecv, bh, bh, dev_at(down))

    @pl.when(place > 0)
    def _():
        h_copy.start()

    early.scatter2()

    gconv = gconv_b.astype(F32)
    gcb = jnp.sum(gconv, axis=0, keepdims=True)
    gcw = [
        jnp.sum(jnp.where(dist_own >= k, gconv * xpad[pl.ds(HALO - k, rows)], 0.0), axis=0, keepdims=True)
        for k in range(4)
    ]
    gpad[pl.ds(0, rows)] = gconv
    gpad[pl.ds(rows, HALO)] = jnp.zeros((HALO, inner), F32)
    gext[pl.ds(0, HALO)] = jnp.zeros((HALO, inner), F32)
    gext[pl.ds(HALO, HALO)] = gconv[:HALO]
    gxi = jnp.zeros((rows, inner), F32)
    gxe = jnp.zeros((HALO, inner), F32)
    for k in range(4):
        w = cw_r[0, k:k + 1]
        gxi = gxi + jnp.where(dist[HALO + k:HALO + k + rows] >= k, gpad[pl.ds(k, rows)] * w, 0.0)
        if k > 0:
            gxe = gxe + jnp.where(dist[k:k + HALO] >= k, gext[pl.ds(k, HALO)] * w, 0.0)
    gxi_b = jnp.concatenate([gxe, gxi], axis=0).astype(B16)
    normed_x = jnp.concatenate([normed_h, normed], axis=0)
    vr_x = jnp.concatenate([vr_h, vr], axis=0)
    gwx_half = dot(normed_x, gxi_b, 0, 0)
    gn_x = dot(gxi_b, win_r[:, :inner], 1, 1)
    gn_z = dot(gz, win_r[:, inner:], 1, 1)
    ggain = jnp.sum(gn_x * vr_x, axis=0, keepdims=True) + jnp.sum(gn_z * vr, axis=0, keepdims=True)

    own_rows = lpart.shape[0] - width // 2
    lpair[...] = gwx_half.astype(B16)
    bl = ring.take(1)
    hw = width // 2
    l_copy = ring.copy(
        lpair.at[pl.ds(pl.multiple_of((1 - dirn) * hw, hw), hw)], lprecv, bl, bl, sibling
    )
    l_copy.start()
    ring.sent.append(l_copy)
    lpart[pl.ds(0, hw)] = jnp.where(dirn == 0, gwx_half[:hw], gwx_half[hw:])
    nx = gwx_t.shape[0]
    ns = gwdt.shape[0]
    lpart[pl.ds(hw, nx)] = gwx_t
    lpart[pl.ds(hw + nx, ns)] = gwdt
    lpart[pl.ds(hw + nx + ns, state)] = galog
    pad_gain = jnp.concatenate([ggain, jnp.zeros((1, inner - width), F32)], axis=1)
    lasts = gcw + [gcb, gbias, gskip, pad_gain]
    lpart[pl.ds(hw + nx + ns + state, 8)] = jnp.concatenate(lasts, axis=0)
    spare = own_rows - nx - ns - state - 8
    lpart[pl.ds(lpart.shape[0] - spare, spare)] = jnp.zeros((spare, inner), F32)

    out_r[...] = (tok_r[...].astype(F32) + (bsend[...] + _recv(b_copy, brecv))).astype(B16)

    late = Reduce(ring, n, seq, dirn, lpart, ltotal, ls1, lr1, ls2, lr2, lb3)
    early.gather2()
    l_copy.wait_recv()
    lpart[pl.ds(0, hw)] = lpart[pl.ds(0, hw)] + lprecv[...].astype(F32)
    late.scatter1()

    @pl.when(place < n - 1)
    def _():
        h_copy.wait_recv()
        gpad[pl.ds(rows, HALO)] = ghrecv[...].astype(F32)

    edge_x = jnp.zeros((HALO, inner), F32)
    for k in range(4):
        at = HALO + rows - HALO + k
        ok = (dist[at:at + HALO] >= k) & (q_all[at:at + HALO] < total)
        edge_x = edge_x + jnp.where(ok, gpad[pl.ds(rows - HALO + k, HALO)] * cw_r[0, k:k + 1], 0.0)
    gn_edge = dot(edge_x.astype(B16), win_r[:, :inner], 1, 1)
    gn = jnp.concatenate([gn_x[HALO:rows], gn_edge], axis=0) + gn_z
    scaled = gn * gain_r[...]
    gv = inv * (scaled - vr * jnp.mean(scaled * vr, axis=1, keepdims=True))
    vsend[...] = turned(gv.astype(B16), turn_t).astype(B16)
    bv = ring.take(1)
    v_copy = ring.copy(vsend, vrecv, bv, bv, sibling)
    v_copy.start()
    ring.sent.append(v_copy)
    early.gather1()
    late.scatter2()
    early.finish()
    v_copy.wait_recv()
    ing_r[...] = cot_r[...].astype(F32) + (vsend[...].astype(F32) + vrecv[...].astype(F32))
    bs = ring.take(1)
    es_copy = ring.copy(etotal, esib, bs, bs, sibling)
    es_copy.start()
    ring.sent.append(es_copy)
    late.gather2()
    late.gather1()
    es_copy.wait_recv()

    def halves(mine, other):
        a, b = mine.astype(F32), other.astype(F32)
        return jnp.where(dirn == 0, a, b), jnp.where(dirn == 0, b, a)

    gwz_all, gwo_all = halves(etotal[...], esib[...])
    gwin_r[:, inner:] = gwz_all
    gwout_r[pl.ds(0, width)] = gwo_all[:, :width]
    gwout_r[pl.ds(width, width)] = gwo_all[:, width:]
    late.finish()
    bs2 = ring.take(1)
    ls_copy = ring.copy(ltotal, lsib, bs2, bs2, sibling)
    ls_copy.start()
    ring.sent.append(ls_copy)
    own = ltotal[pl.ds(hw, own_rows)].astype(F32)
    gwx_r[0] = own[:nx].T
    gwdt_r[0] = own[nx:nx + ns]
    galog_r[0] = own[nx + ns:nx + ns + state]
    tail = own[nx + ns + state:]
    gcw_r[0] = tail[0:4]
    gcb_r[...] = tail[4:5]
    gbias_r[...] = tail[5:6]
    gskip_r[...] = tail[6:7]
    ls_copy.wait_recv()
    low, high = halves(ltotal[pl.ds(0, hw)], lsib[pl.ds(0, hw)])
    gwin_r[pl.ds(0, hw), :inner] = low
    gwin_r[pl.ds(hw, hw), :inner] = high
    gain_at = hw + nx + ns + state
    both = ltotal[pl.ds(gain_at, 16)].astype(F32) + lsib[pl.ds(gain_at, 16)].astype(F32)
    ggain_r[...] = both[7:8, :width]

    @pl.when(place < n - 1)
    def _():
        tok_copy.wait_send()

    @pl.when(place > 0)
    def _():
        h_copy.wait_send()

    for c in ring.sent:
        c.wait_send()


def _recv(copy, ref):
    copy.wait_recv()
    return ref[...]


def on_device(n, tokens, gain, w_in, w_out, conv_w, conv_b, w_x, w_dt, dt_bias, a_log, d_skip, lengths, cotangent):
    rows, width = tokens.shape
    inner = w_out.shape[0]
    state = a_log.shape[1]
    rank = w_dt.shape[1]
    g_in, g_out = log_split(n)
    g3 = n // 16
    early_rows = width
    late_rows = -(-(width // 2 + w_x.shape[2] + rank + state + 16) // 256) * 256
    nsem = 16 + g_in + g_out + 2 * (16 + (g3 if g3 > 1 else 0))
    vm = pltpu.VMEM
    sds = jax.ShapeDtypeStruct
    half_bufs = lambda r: [
        vm((r, inner), F32), vm((r, inner), B16),
        vm((r, inner), B16), vm((4, r // 4, inner), B16),
        vm((r // 4, inner), B16), vm((4, r // 16, inner), B16),
        vm((max(g3, 1), r // 16, inner), B16),
    ]
    scratch = [
        vm((HALO, width), B16),
        vm((rows * state, LANES), F32), vm((rows * state, LANES), F32),
        vm((rows * state, inner), F32), vm(((rows + 1) * state, inner), F32),
        vm((rows * state, inner), F32), vm((rows * state, inner), F32),
        vm((rows, inner), F32), vm((rows, inner), F32), vm((rows, inner), F32),
        vm((HALO + rows, inner), F32), vm((rows + HALO, inner), F32), vm((2 * HALO, inner), F32),
        vm((HALO, inner), B16), vm((HALO, inner), B16), vm((HALO, inner), B16),
        vm((g_in, 2 * state + 16, inner), B16), vm((2, state + 16, inner), B16),
        vm((g_out, state + 16, inner), B16),
        vm((rows, inner), F32), vm((rows, GROUP * state), F32), vm((rows, GROUP * state), F32),
        vm((rows, inner), F32), vm((rows, inner), F32),
        vm((rows, width), F32), vm((rows, width), F32),
        vm((rows, width), B16), vm((rows, width), B16),
        vm((2, early_rows, inner), B16), vm((early_rows, inner), B16),
        *half_bufs(early_rows),
        vm((width, inner), B16), vm((width // 2, inner), B16),
        *half_bufs(late_rows),
        vm((early_rows, inner), B16), vm((late_rows, inner), B16),
        pltpu.SemaphoreType.DMA((nsem,)), pltpu.SemaphoreType.DMA((nsem,)),
    ]
    outs = (
        sds((rows, width), B16), sds((rows, width), F32), sds((1, width), F32),
        sds(w_in.shape, F32), sds(w_out.shape, F32), sds(conv_w.shape, F32), sds(conv_b.shape, F32),
        sds(w_x.shape, F32), sds(w_dt.shape, F32), sds(dt_bias.shape, F32), sds(a_log.shape, F32),
        sds(d_skip.shape, F32),
    )
    specs = [pl.BlockSpec(memory_space=pltpu.VMEM)] * 13
    specs[11] = pl.BlockSpec(memory_space=pltpu.SMEM)
    res = pl.pallas_call(
        functools.partial(kernel, n, nsem),
        out_shape=outs,
        in_specs=specs,
        out_specs=[pl.BlockSpec(memory_space=pltpu.VMEM)] * len(outs),
        scratch_shapes=scratch,
        compiler_params=pltpu.CompilerParams(
            collective_id=0, has_side_effects=True, vmem_limit_bytes=56 * 2**20
        ),
    )(tokens, gain.reshape(1, width), w_in, w_out, conv_w, conv_b, w_x, w_dt, dt_bias, a_log, d_skip, lengths, cotangent)
    return (res[0], res[1], res[2].reshape(width)) + tuple(res[3:])


def solution(mesh):
    d1, d2 = P("dir", None), P("dir", None, None)
    return jax.shard_map(
        functools.partial(on_device, mesh.shape["seq"]),
        mesh=mesh,
        in_specs=(P("seq", None), P(), P(), P(), d2, d1, d2, d2, d1, d2, d1, P(), P("seq", None)),
        out_specs=(P("seq", None), P("seq", None), P(), P(), P(), d2, d1, d2, d2, d1, d2, d1),
        check_vma=False,
    )
```

```python
import functools

import jax
import jax.numpy as jnp
from jax import lax
from jax.experimental import pallas as pl
from jax.experimental.pallas import tpu as pltpu
from jax.sharding import PartitionSpec as P

F32 = jnp.float32
B16 = jnp.bfloat16
MESH = pl.DeviceIdType.MESH
NORM_EPS = 1e-05
LOG2E = 1.4426950408889634
RESET = 1e6
HALO = 16
LANES = 128
GROUP = 16


def dot(a, b, ca=1, cb=0):
    return lax.dot_general(a, b, (((ca,), (cb,)), ((), ())), preferred_element_type=F32)


def silu_grad(v, sigma):
    return sigma * (1.0 + v * (1.0 - sigma))


def softplus(v):
    u = jnp.exp(-jnp.abs(v))
    s = u / (2.0 + u)
    q = s * s
    p = 1.0 / 15.0
    for k in (13.0, 11.0, 9.0, 7.0, 5.0, 3.0):
        p = p * q + 1.0 / k
    return jnp.maximum(v, 0.0) + 2.0 * s * (p * q + 1.0)


def log_split(n):
    inner = 1
    while inner * inner * 4 <= n:
        inner *= 2
    return inner, n // inner


class Ring:
    def __init__(self, ssem, rsem, size):
        self.ssem, self.rsem, self.next, self.size = ssem, rsem, 0, size
        self.sent, self.edges = [], []

    def take(self, count):
        base = self.next
        self.next += count
        assert self.next <= self.size
        return base

    def copy(self, src, dst, s, r, dev):
        return pltpu.make_async_remote_copy(
            src_ref=src, dst_ref=dst, send_sem=self.ssem.at[s], recv_sem=self.rsem.at[r],
            device_id=dev, device_id_type=MESH,
        )


class Exchange:
    def __init__(self, ring, size, me, dev):
        self.ring, self.size, self.me, self.dev = ring, size, me, dev
        self.base = ring.take(size)

    def start(self, src, dst):
        self.src, self.dst = src, dst
        for r in range(1, self.size):
            peer = lax.rem(self.me + r, self.size)
            c = self.ring.copy(src(peer), dst(self.me), self.base + r, self.base + self.me, self.dev(peer))
            c.start()
            self.ring.sent.append(c)

    def wait(self):
        for r in range(1, self.size):
            peer = lax.rem(self.me + r, self.size)
            self.ring.copy(
                self.src(peer), self.dst(peer), self.base + r, self.base + peer, self.dev(peer)
            ).wait_recv()


class Reduce:
    def __init__(self, ring, n, seq, dirn, part, total, send1, recv1, send2, recv2, buf3):
        g1, g2 = 4, 4
        g3 = n // (g1 * g2)
        self.g = (g1, g2, g3)
        lo = lax.rem(seq, g1)
        mid = lax.rem(seq // g1, g2)
        hi = seq // (g1 * g2)
        self.ids = (lo, mid, hi)
        dev1 = lambda p: (dirn, seq - lo + p)
        dev2 = lambda p: (dirn, seq + (p - mid) * g1)
        dev3 = lambda p: (dirn, seq + (p - hi) * g1 * g2)
        self.ex = [Exchange(ring, g1, lo, dev1), Exchange(ring, g2, mid, dev2)]
        self.top = Exchange(ring, g3, hi, dev3) if g3 > 1 else None
        self.back = [Exchange(ring, g2, mid, dev2), Exchange(ring, g1, lo, dev1)]
        self.part, self.total = part, total
        self.send1, self.recv1, self.send2, self.recv2, self.buf3 = send1, recv1, send2, recv2, buf3
        self.q = part.shape[0] // g1
        self.p = self.q // g2

    def scatter1(self):
        q = self.q
        self.send1[...] = self.part[...].astype(B16)
        self.ex[0].start(
            lambda p: self.send1.at[pl.ds(pl.multiple_of(p * q, q), q)], lambda s: self.recv1.at[s]
        )

    def scatter2(self):
        q, p_ = self.q, self.p
        lo, mid, _ = self.ids
        self.recv1[lo] = jnp.zeros(self.recv1.shape[1:], B16)
        self.ex[0].wait()
        acc = self.part[pl.ds(pl.multiple_of(lo * q, q), q)]
        for j in range(self.g[0]):
            acc = acc + self.recv1[j].astype(F32)
        self.part[pl.ds(0, q)] = acc
        self.send2[...] = acc.astype(B16)
        self.ex[1].start(
            lambda p: self.send2.at[pl.ds(pl.multiple_of(p * p_, p_), p_)],
            lambda s: self.recv2.at[s],
        )

    def gather2(self):
        q, p_ = self.q, self.p
        lo, mid, hi = self.ids
        self.recv2[mid] = jnp.zeros(self.recv2.shape[1:], B16)
        self.ex[1].wait()
        acc = self.part[pl.ds(pl.multiple_of(mid * p_, p_), p_)]
        for j in range(self.g[1]):
            acc = acc + self.recv2[j].astype(F32)
        if self.top is not None:
            self.buf3[hi] = acc.astype(B16)
            self.top.start(lambda p: self.buf3.at[hi], lambda s: self.buf3.at[s])
            self.top.wait()
            acc = self.buf3[0].astype(F32)
            for j in range(1, self.g[2]):
                acc = acc + self.buf3[j].astype(F32)
        at = lambda s: pl.ds(pl.multiple_of(lo * q + s * p_, p_), p_)
        self.total[at(mid)] = acc.astype(B16)
        self.back[0].start(lambda p: self.total.at[at(mid)], lambda s: self.total.at[at(s)])

    def gather1(self):
        q = self.q
        lo = self.ids[0]
        self.back[0].wait()
        at = lambda s: pl.ds(pl.multiple_of(s * q, q), q)
        self.back[1].start(lambda p: self.total.at[at(lo)], lambda s: self.total.at[at(s)])

    def finish(self):
        self.back[1].wait()


class Direct:
    def __init__(self, ring, n, seq, dirn, part, total, send, recv, buf3, pieces):
        self.ring, self.part, self.total = ring, part, total
        self.send, self.recv, self.buf3, self.pieces = send, recv, buf3, pieces
        self.me, self.hi, self.g3 = lax.rem(seq, 16), seq // 16, n // 16
        self.dev = lambda p: (dirn, seq - self.me + p)
        self.s1, self.s2 = ring.take(16), ring.take(16)
        self.top = Exchange(ring, self.g3, self.hi, lambda p: (dirn, seq + (p - self.hi) * 16)) if self.g3 > 1 else None
        self.peers = [lax.rem(self.me + r, 16) for r in range(1, 16)]

    def piece(self, p):
        return lax.rem(p + 12, 16) if self.pieces < 16 else p

    def at(self, p):
        return pl.ds(pl.multiple_of(self.piece(p) * 16, 16), 16)

    def owns(self, p, body):
        if self.pieces < 16:
            pl.when(self.piece(p) < self.pieces)(body)
        else:
            body()

    def go(self, c, owner):
        self.owns(owner, c.start)
        if self.pieces < 16:
            self.ring.edges.append((c, self.piece(owner) < self.pieces))
        else:
            self.ring.sent.append(c)

    def scatter(self):
        self.send[...] = self.part[...].astype(B16)
        for r, p in enumerate(self.peers):
            c = self.ring.copy(self.send.at[self.at(p)], self.recv.at[self.me], self.s1 + r, self.s1 + self.me, self.dev(p))
            self.go(c, p)

    def gather(self):
        def add():
            self.recv[self.me] = jnp.zeros(self.recv.shape[1:], B16)
            for r, p in enumerate(self.peers):
                self.ring.copy(
                    self.send.at[pl.ds(0, 16)], self.recv.at[p], self.s1 + r, self.s1 + p, self.dev(p)
                ).wait_recv()
            acc = self.part[self.at(self.me)]
            for j in range(16):
                acc = acc + self.recv[j].astype(F32)
            if self.top is not None:
                self.buf3[self.hi] = acc.astype(B16)
                self.top.start(lambda p: self.buf3.at[self.hi], lambda s: self.buf3.at[s])
                self.top.wait()
                for _ in range(1, self.g3):
                    self.ring.sent.pop().wait_send()
                acc = self.buf3[0].astype(F32)
                for j in range(1, self.g3):
                    acc = acc + self.buf3[j].astype(F32)
            self.total[self.at(self.me)] = acc.astype(B16)

        self.owns(self.me, add)
        mine = self.total.at[self.at(self.me)]
        for r, p in enumerate(self.peers):
            self.go(self.ring.copy(mine, mine, self.s2 + r, self.s2 + self.me, self.dev(p)), self.me)

    def finish(self):
        for r, p in enumerate(self.peers):
            there = self.total.at[self.at(p)]
            c = self.ring.copy(there, there, self.s2 + r, self.s2 + p, self.dev(p))
            self.owns(p, c.wait_recv)


def kernel(n, nsem, *refs):
    (tok_h, gain_h, win_h, wout_h, cw_h, cb_h, wx_h, wdt_h, bias_h, alog_h, skip_h, cot_h, len_r,
     out_r, ing_r, etotal, esib, xtotal, xsib, ototal, gsib,
     tok_r, gain_r, win_r, wout_r, cw_r, cb_r, wx_r, wdt_r, bias_r, alog_r, skip_r, cot_r, lsem,
     thalo, brep, crep, dref, hs, lamr, rar, sdr, sar, gyr, xpad, gpad, gext, ghsend, ghrecv,
     xin1, xsend2, xin2, yr, mgr, mbr, adjr, dtar, bsend, brecv, vsend, vrecv,
     epair, eprecv, epart, es1, er1, es2, er2, eb3,
     xpair, xprecv, xpart, xs1, xr1, xb3, opart, os1, or1, ob3,
     ssem, rsem) = refs
    rows, width = tok_r.shape
    inner = wout_r.shape[0]
    state = alog_r.shape[1]
    chunks = inner // LANES
    groups = rows // GROUP
    blk = GROUP * state
    dirn = lax.axis_index("dir")
    seq = lax.axis_index("seq")
    place = seq + dirn * (n - 1 - 2 * seq)
    seq_at = lambda p: p + dirn * (n - 1 - 2 * p)
    dev_at = lambda p: (dirn, seq_at(p))
    sibling = (1 - dirn, seq)
    g_in, g_out = log_split(n)
    lo = lax.rem(place, g_in)
    hi = place // g_in
    ring = Ring(ssem, rsem, nsem)
    up = lax.rem(place + 1, n)
    down = lax.rem(place + n - 1, n)

    barrier = pltpu.get_barrier_semaphore()
    s_lo, s_hi = lax.rem(seq, 16), seq // 16
    peers = [sibling] + [(dirn, seq - s_lo + lax.rem(s_lo + r, 16)) for r in range(1, 16)]
    if n != 16:
        peers += [dev_at(up), dev_at(down)]
        peers += [(dirn, seq + (lax.rem(s_hi + r, n // 16) - s_hi) * 16) for r in range(1, n // 16)]
        peers += [dev_at(hi * g_in + lax.rem(lo + r, g_in)) for r in range(1, g_in)]
        peers += [dev_at(lax.rem(hi + r, g_out) * g_in + lo) for r in range(1, g_out)]
    for dev in peers:
        pl.semaphore_signal(barrier, inc=1, device_id=dev, device_id_type=MESH)

    loads = {}
    pairs = [(tok_h, tok_r), (gain_h, gain_r), (win_h, win_r), (cot_h, cot_r), (wout_h, wout_r), (cw_h, cw_r),
             (cb_h, cb_r), (wx_h, wx_r), (wdt_h, wdt_r), (bias_h, bias_r), (alog_h, alog_r), (skip_h, skip_r)]
    for i, (a, b) in enumerate(pairs):
        loads[i] = pltpu.make_async_copy(a, b, lsem.at[i])
        loads[i].start()

    def turn(size):
        r = lax.broadcasted_iota(jnp.int32, (size, size), 0)
        c = lax.broadcasted_iota(jnp.int32, (size, size), 1)
        return jnp.where(c == r + dirn * (size - 1 - 2 * r), 1.0, 0.0).astype(B16)

    turn_t, turn_f, turn_h = turn(rows), turn(width), turn(HALO)
    turned = lambda v, tt: dot(dot(tt, v).astype(B16), turn_f)

    total = n * rows
    q = lax.broadcasted_iota(jnp.int32, (rows + 2 * HALO, LANES), 0) + (place * rows - HALO)
    dist = jnp.full(q.shape, 1 << 30, jnp.int32)
    before = jnp.int32(0)
    for w in range(len_r.shape[0]):
        after = before + len_r[w]
        delta = q - (before + dirn * (total - after - before))
        dist = jnp.where((delta >= 0) & (delta < dist), delta, dist)
        before = after
    dist = jnp.concatenate([dist] * chunks, axis=1)
    q_all = jnp.concatenate([q] * chunks, axis=1)
    dist_own = dist[HALO:HALO + rows]

    def normalise(v):
        inv = lax.rsqrt(jnp.mean(v * v, axis=1, keepdims=True) + NORM_EPS)
        vr = v * inv
        return inv, vr, (vr * gain_r[...]).astype(B16)

    for i in range(3):
        loads[i].wait()
    inv, vr, normed = normalise(turned(tok_r[...], turn_t))
    proj = dot(normed, win_r[...])
    xi = proj[:, :inner].astype(B16).astype(F32)
    zgate = proj[:, inner:]
    xpad[pl.ds(0, HALO)] = jnp.zeros((HALO, inner), F32)
    xpad[pl.ds(HALO, rows)] = xi

    pl.semaphore_wait(barrier, len(peers))
    edge = pl.multiple_of((1 - dirn) * (rows - HALO), HALO)
    b0 = ring.take(1)
    tok_copy = ring.copy(tok_r.at[pl.ds(edge, HALO)], thalo, b0, b0, dev_at(up))
    ring.edges.append((tok_copy, place < n - 1))

    @pl.when(place < n - 1)
    def _():
        tok_copy.start()

    @pl.when(place == 0)
    def _():
        thalo[...] = jnp.zeros(thalo.shape, B16)

    for i in range(3, len(pairs)):
        loads[i].wait()
    cot = turned(cot_r[...], turn_t).astype(B16)
    sig_z = jax.nn.sigmoid(zgate)
    gate = zgate * sig_z
    gmix = dot(cot, wout_r[...], 1, 1)
    gy = gmix * gate
    gyr[...] = gy
    rate = -jnp.exp(alog_r[0])
    rate2 = rate * LOG2E
    cut = lambda v: [v[:, c * LANES:(c + 1) * LANES] for c in range(chunks)]
    a2 = cut(rate2)
    a1 = cut(rate)

    def drive(count):
        conv = jnp.zeros((count, inner), F32) + cb_r[...]
        for k in range(4):
            tap = xpad[pl.ds(HALO - k, count)] * cw_r[0, k:k + 1]
            conv = conv + jnp.where(dist_own[:count] >= k, tap, 0.0)
        sig_c = jax.nn.sigmoid(conv)
        act_b = (conv * sig_c).astype(B16)
        px = dot(wx_r[0], act_b, 1, 1)
        pre = dot(px[:state].astype(B16), wdt_r[0], 0, 0) + bias_r[...]
        step = softplus(pre)
        sd = jnp.where(dist_own[:count] == 0, RESET, step)
        sdr[pl.ds(0, count)] = sd
        sar[pl.ds(0, count)] = step * act_b.astype(F32)
        return conv, sig_c, act_b, px, pre, step, sd

    def spread(b_t, c_t, first, last):
        def body(g, carry):
            shift = lax.rem(LANES - g * 8, LANES)
            br = pltpu.roll(b_t, shift, 1)
            cr = pltpu.roll(c_t, shift, 1)
            for j in range(8):
                at = pl.ds(pl.multiple_of((g * 8 + j) * state, state), state)
                brep[at] = jnp.broadcast_to(br[:, j:j + 1], (state, LANES))
                crep[at] = jnp.broadcast_to(cr[:, j:j + 1], (state, LANES))
            return carry

        lax.fori_loop(first, last, body, 0)

    def summarise(g, carry):
        h, p, l = [list(x) for x in carry]
        at8 = pl.ds(pl.multiple_of(g * 8, 8), 8)
        sd8, sa8, gy8 = sdr[at8], sar[at8], gyr[at8]
        for j in range(8):
            at = pl.ds(pl.multiple_of((g * 8 + j) * state, state), state)
            br, cr = brep[at], crep[at]
            for c in range(chunks):
                lane = slice(c * LANES, (c + 1) * LANES)
                d = jnp.exp2(sd8[j:j + 1, lane] * a2[c])
                dref[at, lane] = d
                h[c] = d * h[c] + sa8[j:j + 1, lane] * br
                p[c] = p[c] * d
                l[c] = l[c] + p[c] * (gy8[j:j + 1, lane] * cr)
        return tuple(h), tuple(p), tuple(l)

    zero = tuple(jnp.zeros((state, LANES), F32) for _ in range(chunks))
    one = tuple(jnp.ones((state, LANES), F32) for _ in range(chunks))
    join = lambda v: jnp.concatenate(v, axis=1)
    head = HALO // 8

    whole = drive(rows)
    spread(whole[3][state:2 * state], whole[3][2 * state:], head, rows // 8)
    h_late, p_late, l_late = lax.fori_loop(head, rows // 8, summarise, (zero, one, zero))

    @pl.when(place > 0)
    def _():
        tok_copy.wait_recv()

    _, vr_h, normed_h = normalise(turned(thalo[...], turn_h))
    xpad[pl.ds(0, HALO)] = dot(normed_h, win_r[:, :inner]).astype(B16).astype(F32)
    start = drive(HALO)
    first_px = jnp.concatenate([start[3], jnp.zeros((start[3].shape[0], rows - HALO), F32)], axis=1)
    lane_px = lax.broadcasted_iota(jnp.int32, first_px.shape, 1)
    px = jnp.where(lane_px < HALO, first_px, whole[3])
    patch = lambda i: jnp.concatenate([start[i], whole[i][HALO:]], axis=0)
    conv, sig_c, act_b, pre, step, sd = [patch(i) for i in (0, 1, 2, 4, 5, 6)]
    act = act_b.astype(F32)
    dt_low = px[:state].astype(B16)
    b_t = px[state:2 * state]
    c_t = px[2 * state:]
    spread(b_t, c_t, 0, head)
    h_first, p_first, l_first = lax.fori_loop(0, head, summarise, (zero, one, zero))
    h_sum = join(h_late) + join(p_late) * join(h_first)
    l_sum = join(l_first) + join(p_first) * join(l_late)

    def pair_rows(v):
        top = v.astype(B16)
        rest = (v - top.astype(F32)).astype(B16)
        r = lax.broadcasted_iota(jnp.int32, (16, v.shape[1]), 0)
        both = jnp.where(r == 0, top.astype(F32), jnp.where(r == 1, rest.astype(F32), 0.0))
        return both.astype(B16)

    unpair = lambda v: v[0:1].astype(F32) + v[1:2].astype(F32)
    xin1[lo, pl.ds(0, state)] = h_sum.astype(B16)
    xin1[lo, pl.ds(state, state)] = l_sum.astype(B16)
    xin1[lo, pl.ds(2 * state, 16)] = pair_rows(jnp.sum(sd, axis=0, keepdims=True))
    ex1 = Exchange(ring, g_in, lo, lambda p: dev_at(hi * g_in + p))
    ex1.start(lambda p: xin1.at[lo], lambda s: xin1.at[s])
    ex1.wait()
    sums = [unpair(xin1[j, pl.ds(2 * state, 16)]) for j in range(g_in)]
    fwd = bwd = fwd_all = bwd_all = jnp.zeros((state, inner), F32)
    s_fwd = s_bwd = s_all = jnp.zeros((1, inner), F32)
    for j in range(g_in):
        fade = jnp.exp2(rate2 * sums[j])
        fwd_all = fade * fwd_all + xin1[j, pl.ds(0, state)].astype(F32)
        fwd = jnp.where(j < lo, fwd_all, fwd)
        s_all = s_all + sums[j]
        s_fwd = jnp.where(j < lo, s_all, s_fwd)
    for j in reversed(range(g_in)):
        fade = jnp.exp2(rate2 * sums[j])
        bwd_all = fade * bwd_all + xin1[j, pl.ds(state, state)].astype(F32)
        bwd = jnp.where(j > lo, bwd_all, bwd)
        s_bwd = jnp.where(j > lo, s_bwd + sums[j], s_bwd)
    s_pair = pair_rows(s_all)
    xsend2[0, pl.ds(0, state)] = fwd_all.astype(B16)
    xsend2[0, pl.ds(state, 16)] = s_pair
    xsend2[1, pl.ds(0, state)] = bwd_all.astype(B16)
    xsend2[1, pl.ds(state, 16)] = s_pair
    xin2[hi] = jnp.zeros(xin2.shape[1:], B16)
    ex2 = Exchange(ring, g_out, hi, lambda p: dev_at(p * g_in + lo))
    ex2.start(lambda p: xsend2.at[jnp.where(p > hi, 0, 1)], lambda s: xin2.at[s])
    ex2.wait()
    h_in = l_in = jnp.zeros((state, inner), F32)
    for k in range(g_out):
        new = jnp.exp2(rate2 * unpair(xin2[k, pl.ds(state, 16)])) * h_in
        h_in = jnp.where(k < hi, new + xin2[k, pl.ds(0, state)].astype(F32), h_in)
    for k in reversed(range(g_out)):
        new = jnp.exp2(rate2 * unpair(xin2[k, pl.ds(state, 16)])) * l_in
        l_in = jnp.where(k > hi, new + xin2[k, pl.ds(0, state)].astype(F32), l_in)
    h_in = jnp.exp2(rate2 * s_fwd) * h_in + fwd
    l_in = jnp.exp2(rate2 * s_bwd) * l_in + bwd

    hs[pl.ds(0, state)] = h_in

    def forward(g, h):
        h = list(h)
        at8 = pl.ds(pl.multiple_of(g * 8, 8), 8)
        sa8 = sar[at8]
        for j in range(8):
            at = pl.ds(pl.multiple_of((g * 8 + j) * state, state), state)
            nxt = pl.ds(pl.multiple_of((g * 8 + j + 1) * state, state), state)
            br = brep[at]
            for c in range(chunks):
                lane = slice(c * LANES, (c + 1) * LANES)
                h[c] = dref[at, lane] * h[c] + sa8[j:j + 1, lane] * br
                hs[nxt, lane] = h[c]
        return tuple(h)

    lax.fori_loop(0, rows // 8, forward, tuple(cut(h_in)))

    lane_n = lax.broadcasted_iota(jnp.int32, (state, blk), 1)
    row_n = lax.broadcasted_iota(jnp.int32, (state, blk), 0)
    rep = jnp.where(lax.rem(lane_n, state) == row_n, 1.0, 0.0).astype(B16)
    lane_t = lax.broadcasted_iota(jnp.int32, (rows, blk), 1) // state
    row_t = lax.rem(lax.broadcasted_iota(jnp.int32, (rows, blk), 0), GROUP)
    on = lane_t == row_t
    bdiag = jnp.where(on, dot(b_t.astype(B16), rep, 0, 0), 0.0).astype(B16)
    cdiag = jnp.where(on, dot(c_t.astype(B16), rep, 0, 0), 0.0).astype(B16)
    odiag = jnp.where(on, 1.0, 0.0).astype(B16)
    gy_b = gy.astype(B16)
    sa_b = (step * act).astype(B16)
    for g in range(groups):
        t = slice(g * GROUP, (g + 1) * GROUP)
        xh = hs[pl.ds(g * blk + state, blk)].astype(B16)
        yr[pl.ds(g * GROUP, GROUP)] = dot(cdiag[t], xh)
        mgr[pl.ds(g * GROUP, GROUP)] = dot(gy_b[t], xh, 1, 1)
    y = yr[...] + skip_r[...] * act
    mixed = (y * gate).astype(B16)
    gz = (gmix * y * silu_grad(zgate, sig_z)).astype(B16)
    gskip = jnp.sum(gy * act, axis=0, keepdims=True)

    gwz = dot(normed, gz, 0, 0)
    gwo = dot(mixed, cot, 0, 0)
    gwo = jnp.concatenate([gwo[:width], gwo[width:]], axis=1)
    epair[0] = gwz.astype(B16)
    epair[1] = gwo.astype(B16)
    epart[...] = jnp.where(dirn == 0, gwz, gwo)
    be = ring.take(1)
    e_copy = ring.copy(epair.at[1 - dirn], eprecv, be, be, sibling)
    e_copy.start()
    ring.sent.append(e_copy)
    bsend[...] = dot(dot(turn_t, mixed).astype(B16), dot(wout_r[...], turn_f).astype(B16))
    bb = ring.take(1)
    b_copy = ring.copy(bsend, brecv, bb, bb, sibling)
    b_copy.start()
    ring.sent.append(b_copy)

    def backward(i, carry):
        m, acc = [list(x) for x in carry]
        g = rows // 8 - 1 - i
        at8 = pl.ds(pl.multiple_of(g * 8, 8), 8)
        sd8, gy8 = sdr[at8], gyr[at8]
        for j in reversed(range(8)):
            at = pl.ds(pl.multiple_of((g * 8 + j) * state, state), state)
            cr = crep[at]
            for c in range(chunks):
                lane = slice(c * LANES, (c + 1) * LANES)
                lam = m[c] + gy8[j:j + 1, lane] * cr
                lamr[at, lane] = lam
                m[c] = dref[at, lane] * lam
                r = m[c] * hs[at, lane] * a1[c]
                rar[at, lane] = r
                acc[c] = acc[c] + r * sd8[j:j + 1, lane]
        return tuple(m), tuple(acc)

    _, galog = lax.fori_loop(0, rows // 8, backward, (tuple(cut(l_in)), zero))
    galog = join(galog)

    early = Reduce(ring, n, seq, dirn, epart, etotal, es1, er1, es2, er2, eb3)
    e_copy.wait_recv()
    epart[...] = epart[...] + eprecv[...].astype(F32)
    early.scatter1()

    for g in range(groups):
        t = slice(g * GROUP, (g + 1) * GROUP)
        at = pl.ds(g * blk, blk)
        xl = lamr[at].astype(B16)
        adjr[pl.ds(g * GROUP, GROUP)] = dot(bdiag[t], xl)
        mbr[pl.ds(g * GROUP, GROUP)] = dot(sa_b[t], xl, 1, 1)
        dtar[pl.ds(g * GROUP, GROUP)] = dot(odiag[t], rar[at].astype(B16))
    adj = adjr[...]
    gpre = (dtar[...] + adj * act) * jax.nn.sigmoid(pre)
    gbias = jnp.sum(gpre, axis=0, keepdims=True)
    gpre = gpre.astype(B16)
    gwdt = dot(dt_low, gpre)
    sel = lambda m: dot(rep, jnp.where(on, m, 0.0).astype(B16), 1, 1)
    gpx = jnp.concatenate([dot(wdt_r[0], gpre, 1, 1), sel(mbr[...]), sel(mgr[...])], axis=0).astype(B16)
    gwx_t = dot(gpx, act_b)
    gact = gy * skip_r[...] + adj * step + dot(gpx, wx_r[0], 0, 0)
    gconv_b = (gact * silu_grad(conv, sig_c)).astype(B16)
    gconv = gconv_b.astype(F32)

    gpad[pl.ds(0, rows)] = gconv
    gpad[pl.ds(rows, HALO)] = jnp.zeros((HALO, inner), F32)
    gext[pl.ds(0, HALO)] = jnp.zeros((HALO, inner), F32)
    gext[pl.ds(HALO, HALO)] = gconv[:HALO]
    gxi = jnp.zeros((rows, inner), F32)
    gxe = jnp.zeros((HALO, inner), F32)
    for k in range(4):
        w = cw_r[0, k:k + 1]
        gxi = gxi + jnp.where(dist[HALO + k:HALO + k + rows] >= k, gpad[pl.ds(k, rows)] * w, 0.0)
        if k > 0:
            gxe = gxe + jnp.where(dist[k:k + HALO] >= k, gext[pl.ds(k, HALO)] * w, 0.0)
    gxi_b = jnp.concatenate([gxe, gxi], axis=0).astype(B16)
    normed_x = jnp.concatenate([normed_h, normed], axis=0)
    vr_x = jnp.concatenate([vr_h, vr], axis=0)
    gwx_half = dot(normed_x, gxi_b, 0, 0)
    hw = inner // 2
    left, right = gwx_half[:, :hw], gwx_half[:, hw:]
    xpair[0] = left.astype(B16)
    xpair[1] = right.astype(B16)
    bx = ring.take(1)
    x_copy = ring.copy(xpair.at[1 - dirn], xprecv, bx, bx, sibling)
    x_copy.start()
    ring.sent.append(x_copy)
    xpart[...] = jnp.where(dirn == 0, left, right)
    ghsend[...] = gconv_b[:HALO]
    bh = ring.take(1)
    h_copy = ring.copy(ghsend, ghrecv, bh, bh, dev_at(down))
    ring.edges.append((h_copy, place > 0))

    @pl.when(place > 0)
    def _():
        h_copy.start()

    gn_x = dot(gxi_b, win_r[:, :inner], 1, 1)
    gn_z = dot(gz, win_r[:, inner:], 1, 1)
    ggain = jnp.sum(gn_x * vr_x, axis=0, keepdims=True) + jnp.sum(gn_z * vr, axis=0, keepdims=True)
    gcb = jnp.sum(gconv, axis=0, keepdims=True)
    gcw = [
        jnp.sum(jnp.where(dist_own >= k, gconv * xpad[pl.ds(HALO - k, rows)], 0.0), axis=0, keepdims=True)
        for k in range(4)
    ]
    pad_gain = jnp.concatenate([ggain, jnp.zeros((1, inner - width), F32)], axis=1)
    tail = jnp.concatenate(gcw + [gcb, gbias, gskip, pad_gain], axis=0)
    row = 0
    for part in (gwx_t, gwdt, galog, tail):
        k = part.shape[0]
        opart[pl.ds(row, k)] = part[:, :hw]
        opart[pl.ds(row + k, k)] = part[:, hw:]
        row += 2 * k
    opart[pl.ds(row, opart.shape[0] - row)] = jnp.zeros((opart.shape[0] - row, hw), F32)
    own = Direct(ring, n, seq, dirn, opart, ototal, os1, or1, ob3, -(-row // 16))
    own.scatter()
    xlate = Direct(ring, n, seq, dirn, xpart, xtotal, xs1, xr1, xb3, 16)
    x_copy.wait_recv()
    xpart[...] = xpart[...] + xprecv[...].astype(F32)
    xlate.scatter()
    early.scatter2()
    b_copy.wait_recv()
    out_r[...] = (tok_r[...].astype(F32) + (bsend[...] + brecv[...])).astype(B16)

    @pl.when(place < n - 1)
    def _():
        h_copy.wait_recv()
        gpad[pl.ds(rows, HALO)] = ghrecv[...].astype(F32)

    edge_x = jnp.zeros((HALO, inner), F32)
    for k in range(4):
        at = HALO + rows - HALO + k
        ok = (dist[at:at + HALO] >= k) & (q_all[at:at + HALO] < total)
        edge_x = edge_x + jnp.where(ok, gpad[pl.ds(rows - HALO + k, HALO)] * cw_r[0, k:k + 1], 0.0)
    gn_edge = dot(edge_x.astype(B16), win_r[:, :inner], 1, 1)
    gn = jnp.concatenate([gn_x[HALO:rows], gn_edge], axis=0) + gn_z
    scaled = gn * gain_r[...]
    gv = inv * (scaled - vr * jnp.mean(scaled * vr, axis=1, keepdims=True))
    vsend[...] = turned(gv.astype(B16), turn_t).astype(B16)
    bv = ring.take(1)
    v_copy = ring.copy(vsend, vrecv, bv, bv, sibling)
    v_copy.start()
    ring.sent.append(v_copy)
    early.gather2()
    own.gather()
    xlate.gather()
    early.gather1()
    v_copy.wait_recv()
    ing_r[...] = cot_r[...].astype(F32) + (vsend[...].astype(F32) + vrecv[...].astype(F32))
    early.finish()
    bs = ring.take(1)
    es_copy = ring.copy(etotal, esib, bs, bs, sibling)
    es_copy.start()
    ring.sent.append(es_copy)
    own.finish()
    bo = ring.take(1)
    gat = pl.ds(row - 16, 16)
    os_copy = ring.copy(ototal.at[gat], gsib, bo, bo, sibling)
    os_copy.start()
    ring.sent.append(os_copy)
    xlate.finish()
    bs2 = ring.take(1)
    xs_copy = ring.copy(xtotal, xsib, bs2, bs2, sibling)
    xs_copy.start()
    ring.sent.append(xs_copy)
    es_copy.wait_recv()
    os_copy.wait_recv()
    xs_copy.wait_recv()
    done_edges(ring)
    for c in ring.sent:
        c.wait_send()


def finish(sizes, *refs):
    (out_v, ing_v, etotal, esib, xtotal, xsib, ototal, gsib,
     out_h, ing_h, ggain_h, gwin_h, gwout_h, gcw_h, gcb_h, gwx_h, gwdt_h, gbias_h, galog_h, gskip_h,
     ggain, gwin, gwout, gcw, gcb, gwx, gwdt, gbias, galog, gskip, sems) = refs
    nx, ns, state = sizes
    dirn = lax.axis_index("dir")
    width = ing_v.shape[1]
    hw = xtotal.shape[1]
    inner = 2 * hw
    started = []

    def write(src, dst):
        c = pltpu.make_async_copy(src, dst, sems.at[len(started)])
        c.start()
        started.append(c)

    write(out_v, out_h)
    write(ing_v, ing_h)

    def halves(mine, other):
        a, b = mine[...].astype(F32), other[...].astype(F32)
        return jnp.where(dirn == 0, a, b), jnp.where(dirn == 0, b, a)

    gz, go = halves(etotal, esib)
    gwout[pl.ds(0, width)] = go[:, :width]
    gwout[pl.ds(width, width)] = go[:, width:]
    write(gwout, gwout_h)
    gwin[:, inner:] = gz
    left, right = halves(xtotal, xsib)
    gwin[:, :hw] = left
    gwin[:, hw:inner] = right
    write(gwin, gwin_h)
    row = 0
    parts = []
    for k in (nx, ns, state, 8):
        parts.append(jnp.concatenate([ototal[pl.ds(row, k)], ototal[pl.ds(row + k, k)]], axis=1).astype(F32))
        row += 2 * k
    tail = parts[3]
    gwx[0], gwdt[0], galog[0] = parts[:3]
    gcw[0] = tail[0:4]
    gcb[...], gbias[...], gskip[...] = tail[4:5], tail[5:6], tail[6:7]
    both = ototal[pl.ds(row - 16, 16)].astype(F32) + gsib[...].astype(F32)
    ggain[...] = both[7:8, :width]
    for a, b in ((gwx, gwx_h), (gwdt, gwdt_h), (galog, galog_h), (gcw, gcw_h), (gcb, gcb_h),
                 (gbias, gbias_h), (gskip, gskip_h), (ggain, ggain_h)):
        write(a, b)
    for c in started:
        c.wait()


def done_edges(ring):
    for c, cond in ring.edges:
        @pl.when(cond)
        def _():
            c.wait_send()


def on_device(n, tokens, gain, w_in, w_out, conv_w, conv_b, w_x, w_dt, dt_bias, a_log, d_skip, lengths, cotangent):
    rows, width = tokens.shape
    inner = w_out.shape[0]
    state = a_log.shape[1]
    rank = w_dt.shape[1]
    g_in, g_out = log_split(n)
    g3 = max(n // 16, 1)
    hw = inner // 2
    gain = gain.reshape(1, width)
    w_xt = jnp.swapaxes(w_x, 1, 2)
    nsem = 16 + g_in + g_out + 16 + 4 * 16 + 3 * g3
    vm = pltpu.VMEM
    sds = jax.ShapeDtypeStruct
    ins = (tokens, gain, w_in, w_out, conv_w, conv_b, w_xt, w_dt, dt_bias, a_log, d_skip, cotangent)
    direct = [vm((256, hw), F32), vm((256, hw), B16), vm((16, 16, hw), B16), vm((g3, 16, hw), B16)]
    scratch = [vm(x.shape, x.dtype) for x in ins] + [
        pltpu.SemaphoreType.DMA((len(ins),)),
        vm((HALO, width), B16),
        vm((rows * state, LANES), F32), vm((rows * state, LANES), F32),
        vm((rows * state, inner), F32), vm(((rows + 1) * state, inner), F32),
        vm((rows * state, inner), F32), vm((rows * state, inner), F32),
        vm((rows, inner), F32), vm((rows, inner), F32), vm((rows, inner), F32),
        vm((HALO + rows, inner), F32), vm((rows + HALO, inner), F32), vm((2 * HALO, inner), F32),
        vm((HALO, inner), B16), vm((HALO, inner), B16),
        vm((g_in, 2 * state + 16, inner), B16), vm((2, state + 16, inner), B16),
        vm((g_out, state + 16, inner), B16),
        vm((rows, inner), F32), vm((rows, GROUP * state), F32), vm((rows, GROUP * state), F32),
        vm((rows, inner), F32), vm((rows, inner), F32),
        vm((rows, width), F32), vm((rows, width), F32),
        vm((rows, width), B16), vm((rows, width), B16),
        vm((2, width, inner), B16), vm((width, inner), B16), vm((width, inner), F32),
        vm((width, inner), B16), vm((4, width // 4, inner), B16),
        vm((width // 4, inner), B16), vm((4, width // 16, inner), B16), vm((g3, width // 16, inner), B16),
        vm((2, width, hw), B16), vm((width, hw), B16), *direct, *direct,
        pltpu.SemaphoreType.DMA((nsem,)), pltpu.SemaphoreType.DMA((nsem,)),
    ]
    mids = [
        vm((rows, width), B16), vm((rows, width), F32), vm((width, inner), B16), vm((width, inner), B16),
        vm((width, hw), B16), vm((width, hw), B16), vm((256, hw), B16), vm((16, hw), B16),
    ]
    in_vmem = pl.BlockSpec(memory_space=pltpu.VMEM)
    in_hbm = pl.BlockSpec(memory_space=pltpu.HBM)
    sums = pl.pallas_call(
        functools.partial(kernel, n, nsem),
        out_shape=mids,
        in_specs=[in_hbm] * len(ins) + [pl.BlockSpec(memory_space=pltpu.SMEM)],
        out_specs=[in_vmem] * len(mids),
        scratch_shapes=scratch,
        compiler_params=pltpu.CompilerParams(
            collective_id=0, has_side_effects=True, vmem_limit_bytes=40 * 2**20
        ),
    )(*ins, lengths)
    outs = (
        sds((rows, width), B16), sds((rows, width), F32), sds((1, width), F32),
        sds(w_in.shape, F32), sds(w_out.shape, F32), sds(conv_w.shape, F32), sds(conv_b.shape, F32),
        sds(w_xt.shape, F32), sds(w_dt.shape, F32), sds(dt_bias.shape, F32), sds(a_log.shape, F32),
        sds(d_skip.shape, F32),
    )
    res = pl.pallas_call(
        functools.partial(finish, (w_xt.shape[1], rank, state)),
        out_shape=outs,
        in_specs=[in_vmem] * len(mids),
        out_specs=[in_hbm] * len(outs),
        scratch_shapes=[vm(x.shape, x.dtype) for x in outs[2:]] + [pltpu.SemaphoreType.DMA((len(outs),))],
        compiler_params=pltpu.CompilerParams(vmem_limit_bytes=8 * 2**20),
    )(*sums)
    return (res[0], res[1], res[2].reshape(width)) + tuple(res[3:7]) + (jnp.swapaxes(res[7], 1, 2),) + tuple(res[8:])


def solution(mesh):
    d1, d2 = P("dir", None), P("dir", None, None)
    return jax.shard_map(
        functools.partial(on_device, mesh.shape["seq"]),
        mesh=mesh,
        in_specs=(P("seq", None), P(), P(), P(), d2, d1, d2, d2, d1, d2, d1, P(), P("seq", None)),
        out_specs=(P("seq", None), P("seq", None), P(), P(), P(), d2, d1, d2, d2, d1, d2, d1),
        check_vma=False,
    )
```

```python
import functools

import jax
import jax.numpy as jnp
from jax import lax
from jax.experimental import pallas as pl
from jax.experimental.pallas import tpu as pltpu
from jax.sharding import PartitionSpec as P

F32 = jnp.float32
B16 = jnp.bfloat16
MESH = pl.DeviceIdType.MESH
NORM_EPS = 1e-05
LOG2E = 1.4426950408889634
RESET = 1e6
HALO = 16
LANES = 128


def dot(a, b, ca=1, cb=0):
    return lax.dot_general(a, b, (((ca,), (cb,)), ((), ())), preferred_element_type=F32)


def silu_grad(v, sigma):
    return sigma * (1.0 + v * (1.0 - sigma))


def softplus(v):
    u = jnp.exp(-jnp.abs(v))
    s = u / (2.0 + u)
    q = s * s
    p = 1.0 / 13.0
    for k in (11.0, 9.0, 7.0, 5.0, 3.0):
        p = p * q + 1.0 / k
    return jnp.maximum(v, 0.0) + 2.0 * s * (p * q + 1.0)


def log_split(n):
    inner = 1
    while inner * inner * 4 <= n:
        inner *= 2
    return inner, n // inner


class Ring:
    def __init__(self, ssem, rsem, size):
        self.ssem, self.rsem, self.next, self.size = ssem, rsem, 0, size
        self.sent, self.edges = [], []

    def take(self, count):
        base = self.next
        self.next += count
        assert self.next <= self.size
        return base

    def copy(self, src, dst, s, r, dev):
        return pltpu.make_async_remote_copy(
            src_ref=src, dst_ref=dst, send_sem=self.ssem.at[s], recv_sem=self.rsem.at[r],
            device_id=dev, device_id_type=MESH,
        )


class Exchange:
    def __init__(self, ring, size, me, dev):
        self.ring, self.size, self.me, self.dev = ring, size, me, dev
        self.base = ring.take(size)

    def start(self, src, dst):
        self.src, self.dst = src, dst
        for r in range(1, self.size):
            peer = lax.rem(self.me + r, self.size)
            c = self.ring.copy(src(peer), dst(self.me), self.base + r, self.base + self.me, self.dev(peer))
            c.start()
            self.ring.sent.append(c)

    def wait(self):
        for r in range(1, self.size):
            peer = lax.rem(self.me + r, self.size)
            self.ring.copy(
                self.src(peer), self.dst(peer), self.base + r, self.base + peer, self.dev(peer)
            ).wait_recv()


class Reduce:
    def __init__(self, ring, n, seq, dirn, part, total, send1, recv1, send2, recv2, buf3):
        g1, g2 = 4, 4
        g3 = n // (g1 * g2)
        self.g = (g1, g2, g3)
        lo = lax.rem(seq, g1)
        mid = lax.rem(seq // g1, g2)
        hi = seq // (g1 * g2)
        self.ids = (lo, mid, hi)
        dev1 = lambda p: (dirn, seq - lo + p)
        dev2 = lambda p: (dirn, seq + (p - mid) * g1)
        dev3 = lambda p: (dirn, seq + (p - hi) * g1 * g2)
        self.ex = [Exchange(ring, g1, lo, dev1), Exchange(ring, g2, mid, dev2)]
        self.top = Exchange(ring, g3, hi, dev3) if g3 > 1 else None
        self.back = [Exchange(ring, g2, mid, dev2), Exchange(ring, g1, lo, dev1)]
        self.part, self.total = part, total
        self.send1, self.recv1, self.send2, self.recv2, self.buf3 = send1, recv1, send2, recv2, buf3
        self.q = part.shape[0] // g1
        self.p = self.q // g2

    def scatter1(self):
        q = self.q
        self.send1[...] = self.part[...].astype(B16)
        self.ex[0].start(
            lambda p: self.send1.at[pl.ds(pl.multiple_of(p * q, q), q)], lambda s: self.recv1.at[s]
        )

    def scatter2(self):
        q, p_ = self.q, self.p
        lo, mid, _ = self.ids
        self.recv1[lo] = jnp.zeros(self.recv1.shape[1:], B16)
        self.ex[0].wait()
        acc = self.part[pl.ds(pl.multiple_of(lo * q, q), q)]
        for j in range(self.g[0]):
            acc = acc + self.recv1[j].astype(F32)
        self.part[pl.ds(0, q)] = acc
        self.send2[...] = acc.astype(B16)
        self.ex[1].start(
            lambda p: self.send2.at[pl.ds(pl.multiple_of(p * p_, p_), p_)],
            lambda s: self.recv2.at[s],
        )

    def gather2(self):
        q, p_ = self.q, self.p
        lo, mid, hi = self.ids
        self.recv2[mid] = jnp.zeros(self.recv2.shape[1:], B16)
        self.ex[1].wait()
        acc = self.part[pl.ds(pl.multiple_of(mid * p_, p_), p_)]
        for j in range(self.g[1]):
            acc = acc + self.recv2[j].astype(F32)
        if self.top is not None:
            self.buf3[hi] = acc.astype(B16)
            self.top.start(lambda p: self.buf3.at[hi], lambda s: self.buf3.at[s])
            self.top.wait()
            acc = self.buf3[0].astype(F32)
            for j in range(1, self.g[2]):
                acc = acc + self.buf3[j].astype(F32)
        at = lambda s: pl.ds(pl.multiple_of(lo * q + s * p_, p_), p_)
        self.total[at(mid)] = acc.astype(B16)
        self.back[0].start(lambda p: self.total.at[at(mid)], lambda s: self.total.at[at(s)])

    def gather1(self):
        q = self.q
        lo = self.ids[0]
        self.back[0].wait()
        at = lambda s: pl.ds(pl.multiple_of(s * q, q), q)
        self.back[1].start(lambda p: self.total.at[at(lo)], lambda s: self.total.at[at(s)])

    def finish(self):
        self.back[1].wait()


class Direct:
    def __init__(self, ring, n, seq, dirn, part, total, send, recv, buf3, pieces):
        self.ring, self.part, self.total = ring, part, total
        self.send, self.recv, self.buf3, self.pieces = send, recv, buf3, pieces
        self.me, self.hi, self.g3 = lax.rem(seq, 16), seq // 16, n // 16
        self.dev = lambda p: (dirn, seq - self.me + p)
        self.s1, self.s2 = ring.take(16), ring.take(16)
        self.top = Exchange(ring, self.g3, self.hi, lambda p: (dirn, seq + (p - self.hi) * 16)) if self.g3 > 1 else None
        self.peers = [lax.rem(self.me + r, 16) for r in range(1, 16)]

    def piece(self, p):
        return lax.rem(p + 12, 16) if self.pieces < 16 else p

    def at(self, p):
        return pl.ds(pl.multiple_of(self.piece(p) * 16, 16), 16)

    def owns(self, p, body):
        if self.pieces < 16:
            pl.when(self.piece(p) < self.pieces)(body)
        else:
            body()

    def go(self, c, owner):
        self.owns(owner, c.start)
        if self.pieces < 16:
            self.ring.edges.append((c, self.piece(owner) < self.pieces))
        else:
            self.ring.sent.append(c)

    def scatter(self):
        self.send[...] = self.part[...].astype(B16)
        for r, p in enumerate(self.peers):
            c = self.ring.copy(self.send.at[self.at(p)], self.recv.at[self.me], self.s1 + r, self.s1 + self.me, self.dev(p))
            self.go(c, p)

    def gather(self):
        def add():
            self.recv[self.me] = jnp.zeros(self.recv.shape[1:], B16)
            for r, p in enumerate(self.peers):
                self.ring.copy(
                    self.send.at[pl.ds(0, 16)], self.recv.at[p], self.s1 + r, self.s1 + p, self.dev(p)
                ).wait_recv()
            acc = self.part[self.at(self.me)]
            for j in range(16):
                acc = acc + self.recv[j].astype(F32)
            if self.top is not None:
                self.buf3[self.hi] = acc.astype(B16)
                self.top.start(lambda p: self.buf3.at[self.hi], lambda s: self.buf3.at[s])
                self.top.wait()
                for _ in range(1, self.g3):
                    self.ring.sent.pop().wait_send()
                acc = self.buf3[0].astype(F32)
                for j in range(1, self.g3):
                    acc = acc + self.buf3[j].astype(F32)
            self.total[self.at(self.me)] = acc.astype(B16)

        self.owns(self.me, add)
        mine = self.total.at[self.at(self.me)]
        for r, p in enumerate(self.peers):
            self.go(self.ring.copy(mine, mine, self.s2 + r, self.s2 + self.me, self.dev(p)), self.me)

    def finish(self):
        for r, p in enumerate(self.peers):
            there = self.total.at[self.at(p)]
            c = self.ring.copy(there, there, self.s2 + r, self.s2 + p, self.dev(p))
            self.owns(p, c.wait_recv)


def kernel(n, nsem, *refs):
    (tok_h, gain_h, win_h, wout_h, cw_h, cb_h, wx_h, wdt_h, bias_h, alog_h, skip_h, cot_h, len_r,
     out_r, ing_r, etotal, esib, xtotal, xsib, ototal, gsib,
     tok_r, gain_r, win_r, wout_r, cw_r, cb_r, wx_r, wdt_r, bias_r, alog_r, skip_r, cot_r, lsem,
     thalo, picked, bcr, dref, hs, sdr, sar, gyr, xpad, gpad, gext, ghsend, ghrecv,
     xin1, xsend2, xin2, yr, adjr, dtar, bsend, brecv, vsend, vrecv,
     epair, eprecv, epart, es1, er1, es2, er2, eb3,
     xpair, xprecv, xpart, xs1, xr1, xb3, opart, os1, or1, ob3,
     ssem, rsem) = refs
    rows, width = tok_r.shape
    inner = wout_r.shape[0]
    state = alog_r.shape[1]
    chunks = inner // LANES
    dirn = lax.axis_index("dir")
    seq = lax.axis_index("seq")
    place = seq + dirn * (n - 1 - 2 * seq)
    seq_at = lambda p: p + dirn * (n - 1 - 2 * p)
    dev_at = lambda p: (dirn, seq_at(p))
    sibling = (1 - dirn, seq)
    g_in, g_out = log_split(n)
    lo = lax.rem(place, g_in)
    hi = place // g_in
    ring = Ring(ssem, rsem, nsem)
    up = lax.rem(place + 1, n)
    down = lax.rem(place + n - 1, n)

    barrier = pltpu.get_barrier_semaphore()
    s_lo, s_hi = lax.rem(seq, 16), seq // 16
    peers = [sibling] + [(dirn, seq - s_lo + lax.rem(s_lo + r, 16)) for r in range(1, 16)]
    if n != 16:
        peers += [dev_at(up), dev_at(down)]
        peers += [(dirn, seq + (lax.rem(s_hi + r, n // 16) - s_hi) * 16) for r in range(1, n // 16)]
        peers += [dev_at(hi * g_in + lax.rem(lo + r, g_in)) for r in range(1, g_in)]
        peers += [dev_at(lax.rem(hi + r, g_out) * g_in + lo) for r in range(1, g_out)]
    for dev in peers:
        pl.semaphore_signal(barrier, inc=1, device_id=dev, device_id_type=MESH)

    loads = {}
    pairs = [(tok_h, tok_r), (gain_h, gain_r), (win_h, win_r), (cot_h, cot_r), (wout_h, wout_r), (cw_h, cw_r),
             (cb_h, cb_r), (wx_h, wx_r), (wdt_h, wdt_r), (bias_h, bias_r), (alog_h, alog_r), (skip_h, skip_r)]
    for i, (a, b) in enumerate(pairs):
        loads[i] = pltpu.make_async_copy(a, b, lsem.at[i])
        loads[i].start()

    def turn(size):
        r = lax.broadcasted_iota(jnp.int32, (size, size), 0)
        c = lax.broadcasted_iota(jnp.int32, (size, size), 1)
        return jnp.where(c == r + dirn * (size - 1 - 2 * r), 1.0, 0.0).astype(B16)

    turn_t, turn_f, turn_h = turn(rows), turn(width), turn(HALO)
    turned = lambda v, tt: dot(dot(tt, v).astype(B16), turn_f)

    total = n * rows
    q = lax.broadcasted_iota(jnp.int32, (rows + 2 * HALO, LANES), 0) + (place * rows - HALO)
    dist = jnp.full(q.shape, 1 << 30, jnp.int32)
    before = jnp.int32(0)
    for w in range(len_r.shape[0]):
        after = before + len_r[w]
        delta = q - (before + dirn * (total - after - before))
        dist = jnp.where((delta >= 0) & (delta < dist), delta, dist)
        before = after
    dist = jnp.concatenate([dist] * chunks, axis=1)
    q_all = jnp.concatenate([q] * chunks, axis=1)
    dist_own = dist[HALO:HALO + rows]

    def normalise(v):
        inv = lax.rsqrt(jnp.mean(v * v, axis=1, keepdims=True) + NORM_EPS)
        vr = v * inv
        return inv, vr, (vr * gain_r[...]).astype(B16)

    for i in range(3):
        loads[i].wait()
    inv, vr, normed = normalise(turned(tok_r[...], turn_t))
    proj = dot(normed, win_r[...])
    xi = proj[:, :inner].astype(B16).astype(F32)
    zgate = proj[:, inner:]
    xpad[pl.ds(0, HALO)] = jnp.zeros((HALO, inner), F32)
    xpad[pl.ds(HALO, rows)] = xi

    pl.semaphore_wait(barrier, len(peers))
    edge = pl.multiple_of((1 - dirn) * (rows - HALO), HALO)
    b0 = ring.take(1)
    tok_copy = ring.copy(tok_r.at[pl.ds(edge, HALO)], thalo, b0, b0, dev_at(up))
    ring.edges.append((tok_copy, place < n - 1))

    @pl.when(place < n - 1)
    def _():
        tok_copy.start()

    @pl.when(place == 0)
    def _():
        thalo[...] = jnp.zeros(thalo.shape, B16)

    for i in range(3, len(pairs)):
        loads[i].wait()
    cot = turned(cot_r[...], turn_t).astype(B16)
    sig_z = jax.nn.sigmoid(zgate)
    gate = zgate * sig_z
    gmix = dot(cot, wout_r[...], 1, 1)
    gy = gmix * gate
    gyr[...] = gy
    rate = -jnp.exp(alog_r[0])
    rate2 = rate * LOG2E
    cut = lambda v: [v[:, c * LANES:(c + 1) * LANES] for c in range(chunks)]
    a2 = cut(rate2)
    a1 = cut(rate)

    def drive(count):
        conv = jnp.zeros((count, inner), F32) + cb_r[...]
        for k in range(4):
            tap = xpad[pl.ds(HALO - k, count)] * cw_r[0, k:k + 1]
            conv = conv + jnp.where(dist_own[:count] >= k, tap, 0.0)
        sig_c = jax.nn.sigmoid(conv)
        act_b = (conv * sig_c).astype(B16)
        low_t = dot(wx_r[0, pl.ds(0, state)], act_b, 1, 1).astype(B16)
        bc = dot(act_b, wx_r[0, pl.ds(state, 2 * state)], 1, 1)
        pre = dot(low_t, wdt_r[0], 0, 0) + bias_r[...]
        step = softplus(pre)
        sd = jnp.where(dist_own[:count] == 0, RESET, step)
        sdr[pl.ds(0, count)] = sd
        sar[pl.ds(0, count)] = step * act_b.astype(F32)
        return conv, sig_c, act_b, low_t, pre, step, sd, bc

    wide = 2 * state
    lane_k = lax.broadcasted_iota(jnp.int32, (state, LANES), 1)
    row_k = lax.broadcasted_iota(jnp.int32, (state, LANES), 0)
    own_k = jnp.where((lane_k < 2 * wide) & (lax.rem(lane_k, state) == row_k), 1.0, 0.0)
    fan_r = lax.rem(lax.broadcasted_iota(jnp.int32, (LANES, 2 * LANES), 0), wide) // state
    fan_c = lax.broadcasted_iota(jnp.int32, (LANES, 2 * LANES), 1) // LANES
    fan = jnp.where(fan_r == fan_c, 1.0, 0.0).astype(B16)

    def spread(bc, first):
        count = bc.shape[0]
        top = bc.astype(B16).astype(F32)
        none = jnp.zeros((count, LANES - 2 * wide), F32)
        both = jnp.concatenate([top, bc - top, none], axis=1)
        for t in range(count):
            picked[pl.ds((first + t) * state, state)] = (both[t:t + 1] * own_k).astype(B16)
        at = pl.ds(first * state, count * state)
        bcr[at] = dot(picked[at], fan)

    def summarise(g, carry):
        h, p, l = [list(x) for x in carry]
        at8 = pl.ds(pl.multiple_of(g * 8, 8), 8)
        sd8, sa8, gy8 = sdr[at8], sar[at8], gyr[at8]
        for j in range(8):
            at = pl.ds(pl.multiple_of((g * 8 + j) * state, state), state)
            br, cr = bcr[at, :LANES], bcr[at, LANES:]
            for c in range(chunks):
                lane = slice(c * LANES, (c + 1) * LANES)
                d = jnp.exp2(sd8[j:j + 1, lane] * a2[c])
                dref[at, lane] = d
                h[c] = d * h[c] + sa8[j:j + 1, lane] * br
                p[c] = p[c] * d
                l[c] = l[c] + p[c] * (gy8[j:j + 1, lane] * cr)
        return tuple(h), tuple(p), tuple(l)

    zero = tuple(jnp.zeros((state, LANES), F32) for _ in range(chunks))
    one = tuple(jnp.ones((state, LANES), F32) for _ in range(chunks))
    join = lambda v: jnp.concatenate(v, axis=1)
    head = HALO // 8

    whole = drive(rows)
    spread(whole[7][HALO:], HALO)
    h_late, p_late, l_late = lax.fori_loop(head, rows // 8, summarise, (zero, one, zero), unroll=1)

    @pl.when(place > 0)
    def _():
        tok_copy.wait_recv()

    _, vr_h, normed_h = normalise(turned(thalo[...], turn_h))
    xpad[pl.ds(0, HALO)] = dot(normed_h, win_r[:, :inner]).astype(B16).astype(F32)
    start = drive(HALO)
    low_first = jnp.concatenate([start[3].astype(F32), jnp.zeros((state, rows - HALO), F32)], axis=1)
    lane_low = lax.broadcasted_iota(jnp.int32, low_first.shape, 1)
    dt_low = jnp.where(lane_low < HALO, low_first, whole[3].astype(F32)).astype(B16)
    patch = lambda i: jnp.concatenate([start[i], whole[i][HALO:]], axis=0)
    conv, sig_c, act_b, pre, step, sd = [patch(i) for i in (0, 1, 2, 4, 5, 6)]
    act = act_b.astype(F32)
    spread(start[7], 0)
    h_first, p_first, l_first = lax.fori_loop(0, head, summarise, (zero, one, zero))
    h_sum = join(h_late) + join(p_late) * join(h_first)
    l_sum = join(l_first) + join(p_first) * join(l_late)

    def pair_rows(v):
        top = v.astype(B16).astype(F32)
        both = cut(top) + cut(v - top) + [jnp.zeros((16 - 2 * chunks, LANES), F32)]
        return jnp.concatenate(both, axis=0).astype(B16)

    blk_s = chunks * state
    stack = lambda v: jnp.concatenate(cut(v), axis=0).astype(B16)
    unstack = lambda v, at: join([v[at + c * state:at + (c + 1) * state].astype(F32) for c in range(chunks)])
    def unpair1(v):
        r = v[blk_s:blk_s + 16].astype(F32)
        return join([r[c:c + 1] + r[chunks + c:chunks + c + 1] for c in range(chunks)])
    xin1[lo, pl.ds(0, blk_s)] = stack(h_sum)
    xin1[lo, pl.ds(blk_s, 16)] = pair_rows(jnp.sum(sd, axis=0, keepdims=True))
    xin1[lo, pl.ds(blk_s + 16, blk_s)] = stack(l_sum)
    ex1 = Exchange(ring, g_in, lo, lambda p: dev_at(hi * g_in + p))
    ex1.start(lambda p: xin1.at[lo], lambda s: xin1.at[s])

    ex1.wait()
    sums = [unpair1(xin1[j]) for j in range(g_in)]
    fwd = bwd = fwd_all = bwd_all = jnp.zeros((state, inner), F32)
    s_fwd = s_bwd = s_all = jnp.zeros((1, inner), F32)
    for j in range(g_in):
        fade = jnp.exp2(rate2 * sums[j])
        fwd_all = fade * fwd_all + unstack(xin1[j], 0)
        fwd = jnp.where(j < lo, fwd_all, fwd)
        s_all = s_all + sums[j]
        s_fwd = jnp.where(j < lo, s_all, s_fwd)
    for j in reversed(range(g_in)):
        fade = jnp.exp2(rate2 * sums[j])
        bwd_all = fade * bwd_all + unstack(xin1[j], blk_s + 16)
        bwd = jnp.where(j > lo, bwd_all, bwd)
        s_bwd = jnp.where(j > lo, s_bwd + sums[j], s_bwd)
    s_pair = pair_rows(s_all)
    for k, v in enumerate((fwd_all, bwd_all)):
        xsend2[k, pl.ds(0, blk_s)] = stack(v)
        xsend2[k, pl.ds(blk_s, 16)] = s_pair
    xin2[hi] = jnp.zeros(xin2.shape[1:], B16)
    ex2 = Exchange(ring, g_out, hi, lambda p: dev_at(p * g_in + lo))
    ex2.start(lambda p: xsend2.at[jnp.where(p > hi, 0, 1)], lambda s: xin2.at[s])
    ex2.wait()
    h_in = l_in = jnp.zeros((state, inner), F32)
    for k in range(g_out):
        new = jnp.exp2(rate2 * unpair1(xin2[k])) * h_in
        h_in = jnp.where(k < hi, new + unstack(xin2[k], 0), h_in)
    for k in reversed(range(g_out)):
        new = jnp.exp2(rate2 * unpair1(xin2[k])) * l_in
        l_in = jnp.where(k > hi, new + unstack(xin2[k], 0), l_in)
    h_in = jnp.exp2(rate2 * s_fwd) * h_in + fwd
    l_in = jnp.exp2(rate2 * s_bwd) * l_in + bwd

    sub = lax.broadcasted_iota(jnp.int32, (8, LANES), 0)
    lane_at = lax.broadcasted_iota(jnp.int32, (state, LANES), 1)

    def sum_rows(v):
        for bit in (1, 2, 4):
            mine = lax.rem(sub // bit, 2) == 0
            v = [
                jnp.where(mine, a, b) + pltpu.roll(jnp.where(mine, b, a), bit, 0)
                for a, b in zip(v[::2], v[1::2])
            ]
        return v[0]

    halve = lambda v: v[:8] + v[8:]
    hs[pl.ds(0, state)] = h_in

    def forward(g, carry):
        h, gc = list(carry[0]), carry[1]
        at8 = pl.ds(pl.multiple_of(g * 8, 8), 8)
        sa8, gy8 = sar[at8], gyr[at8]
        over = [None] * 8
        for c in range(chunks):
            lane = slice(c * LANES, (c + 1) * LANES)
            ys = []
            for j in range(8):
                at = pl.ds(pl.multiple_of((g * 8 + j) * state, state), state)
                nxt = pl.ds(pl.multiple_of((g * 8 + j + 1) * state, state), state)
                h[c] = dref[at, lane] * h[c] + sa8[j:j + 1, lane] * bcr[at, :LANES]
                hs[nxt, lane] = h[c]
                ys.append(halve(h[c] * bcr[at, LANES:]))
                new = h[c] * gy8[j:j + 1, lane]
                over[j] = new if c == 0 else over[j] + new
            yr[at8, lane] = sum_rows(ys)
        for j in range(8):
            gc = jnp.where(lane_at == g * 8 + j, jnp.sum(over[j], axis=1, keepdims=True), gc)
        return tuple(h), gc

    none = jnp.zeros((state, rows), F32)
    _, g_c = lax.fori_loop(0, rows // 8, forward, (tuple(cut(h_in)), none))
    y = yr[...] + skip_r[...] * act
    mixed = (y * gate).astype(B16)
    gz = (gmix * y * silu_grad(zgate, sig_z)).astype(B16)
    gskip = jnp.sum(gy * act, axis=0, keepdims=True)

    gwz = dot(normed, gz, 0, 0)
    gwo = dot(mixed, cot, 0, 0)
    gwo = jnp.concatenate([gwo[:width], gwo[width:]], axis=1)
    epair[0] = gwz.astype(B16)
    epair[1] = gwo.astype(B16)
    epart[...] = jnp.where(dirn == 0, gwz, gwo)
    be = ring.take(1)
    e_copy = ring.copy(epair.at[1 - dirn], eprecv, be, be, sibling)
    e_copy.start()
    ring.sent.append(e_copy)
    bsend[...] = dot(dot(turn_t, mixed).astype(B16), dot(wout_r[...], turn_f).astype(B16))
    bb = ring.take(1)
    b_copy = ring.copy(bsend, brecv, bb, bb, sibling)
    b_copy.start()
    ring.sent.append(b_copy)

    def backward(i, carry):
        m, acc, gb = list(carry[0]), list(carry[1]), carry[2]
        g = rows // 8 - 1 - i
        at8 = pl.ds(pl.multiple_of(g * 8, 8), 8)
        sd8, gy8, sa8 = sdr[at8], gyr[at8], sar[at8]
        over = [None] * 8
        for c in range(chunks):
            lane = slice(c * LANES, (c + 1) * LANES)
            adjs, dts = [None] * 8, [None] * 8
            for j in reversed(range(8)):
                at = pl.ds(pl.multiple_of((g * 8 + j) * state, state), state)
                lam = m[c] + gy8[j:j + 1, lane] * bcr[at, LANES:]
                m[c] = dref[at, lane] * lam
                r = m[c] * hs[at, lane] * a1[c]
                acc[c] = acc[c] + r * sd8[j:j + 1, lane]
                adjs[j] = halve(lam * bcr[at, :LANES])
                dts[j] = halve(r)
                new = lam * sa8[j:j + 1, lane]
                over[j] = new if c == 0 else over[j] + new
            adjr[at8, lane] = sum_rows(adjs)
            dtar[at8, lane] = sum_rows(dts)
        for j in range(8):
            gb = jnp.where(lane_at == g * 8 + j, jnp.sum(over[j], axis=1, keepdims=True), gb)
        return tuple(m), tuple(acc), gb

    carry = lax.fori_loop(0, rows // 32, backward, (tuple(cut(l_in)), zero, none))
    early = Reduce(ring, n, seq, dirn, epart, etotal, es1, er1, es2, er2, eb3)
    e_copy.wait_recv()
    epart[...] = epart[...] + eprecv[...].astype(F32)
    early.scatter1()
    _, galog, g_b = lax.fori_loop(rows // 32, rows // 8, backward, carry)
    galog = join(galog)
    adj = adjr[...]
    gpre = (dtar[...] + adj * act) * jax.nn.sigmoid(pre)
    gbias = jnp.sum(gpre, axis=0, keepdims=True)
    gpre = gpre.astype(B16)
    gwdt = dot(dt_low, gpre)
    gpx = jnp.concatenate([dot(wdt_r[0], gpre, 1, 1), g_b, g_c], axis=0).astype(B16)
    gwx_t = dot(gpx, act_b)
    gact = gy * skip_r[...] + adj * step + dot(gpx, wx_r[0], 0, 0)
    gconv_b = (gact * silu_grad(conv, sig_c)).astype(B16)
    gconv = gconv_b.astype(F32)

    gpad[pl.ds(0, rows)] = gconv
    gpad[pl.ds(rows, HALO)] = jnp.zeros((HALO, inner), F32)
    gext[pl.ds(0, HALO)] = jnp.zeros((HALO, inner), F32)
    gext[pl.ds(HALO, HALO)] = gconv[:HALO]
    gxi = jnp.zeros((rows, inner), F32)
    gxe = jnp.zeros((HALO, inner), F32)
    for k in range(4):
        w = cw_r[0, k:k + 1]
        gxi = gxi + jnp.where(dist[HALO + k:HALO + k + rows] >= k, gpad[pl.ds(k, rows)] * w, 0.0)
        if k > 0:
            gxe = gxe + jnp.where(dist[k:k + HALO] >= k, gext[pl.ds(k, HALO)] * w, 0.0)
    gxi_b = jnp.concatenate([gxe, gxi], axis=0).astype(B16)
    normed_x = jnp.concatenate([normed_h, normed], axis=0)
    vr_x = jnp.concatenate([vr_h, vr], axis=0)
    gwx_half = dot(normed_x, gxi_b, 0, 0)
    hw = inner // 2
    left, right = gwx_half[:, :hw], gwx_half[:, hw:]
    xpair[0] = left.astype(B16)
    xpair[1] = right.astype(B16)
    bx = ring.take(1)
    x_copy = ring.copy(xpair.at[1 - dirn], xprecv, bx, bx, sibling)
    x_copy.start()
    ring.sent.append(x_copy)
    xpart[...] = jnp.where(dirn == 0, left, right)
    ghsend[...] = gconv_b[:HALO]
    bh = ring.take(1)
    h_copy = ring.copy(ghsend, ghrecv, bh, bh, dev_at(down))
    ring.edges.append((h_copy, place > 0))

    @pl.when(place > 0)
    def _():
        h_copy.start()

    gn_x = dot(gxi_b, win_r[:, :inner], 1, 1)
    gn_z = dot(gz, win_r[:, inner:], 1, 1)
    ggain = jnp.sum(gn_x * vr_x, axis=0, keepdims=True) + jnp.sum(gn_z * vr, axis=0, keepdims=True)
    gcb = jnp.sum(gconv, axis=0, keepdims=True)
    gcw = [
        jnp.sum(jnp.where(dist_own >= k, gconv * xpad[pl.ds(HALO - k, rows)], 0.0), axis=0, keepdims=True)
        for k in range(4)
    ]
    pad_gain = jnp.concatenate([ggain, jnp.zeros((1, inner - width), F32)], axis=1)
    tail = jnp.concatenate(gcw + [gcb, gbias, gskip, pad_gain], axis=0)
    row = 0
    for part in (gwx_t, gwdt, galog, tail):
        k = part.shape[0]
        opart[pl.ds(row, k)] = part[:, :hw]
        opart[pl.ds(row + k, k)] = part[:, hw:]
        row += 2 * k
    opart[pl.ds(row, opart.shape[0] - row)] = jnp.zeros((opart.shape[0] - row, hw), F32)
    own = Direct(ring, n, seq, dirn, opart, ototal, os1, or1, ob3, -(-row // 16))
    own.scatter()
    xlate = Direct(ring, n, seq, dirn, xpart, xtotal, xs1, xr1, xb3, 16)
    x_copy.wait_recv()
    xpart[...] = xpart[...] + xprecv[...].astype(F32)
    xlate.scatter()
    early.scatter2()
    b_copy.wait_recv()
    out_r[...] = (tok_r[...].astype(F32) + (bsend[...] + brecv[...])).astype(B16)

    @pl.when(place < n - 1)
    def _():
        h_copy.wait_recv()
        gpad[pl.ds(rows, HALO)] = ghrecv[...].astype(F32)

    edge_x = jnp.zeros((HALO, inner), F32)
    for k in range(4):
        at = HALO + rows - HALO + k
        ok = (dist[at:at + HALO] >= k) & (q_all[at:at + HALO] < total)
        edge_x = edge_x + jnp.where(ok, gpad[pl.ds(rows - HALO + k, HALO)] * cw_r[0, k:k + 1], 0.0)
    gn_edge = dot(edge_x.astype(B16), win_r[:, :inner], 1, 1)
    gn = jnp.concatenate([gn_x[HALO:rows], gn_edge], axis=0) + gn_z
    scaled = gn * gain_r[...]
    gv = inv * (scaled - vr * jnp.mean(scaled * vr, axis=1, keepdims=True))
    vsend[...] = turned(gv.astype(B16), turn_t).astype(B16)
    bv = ring.take(1)
    v_copy = ring.copy(vsend, vrecv, bv, bv, sibling)
    v_copy.start()
    ring.sent.append(v_copy)
    own.gather()
    early.gather2()
    xlate.gather()
    v_copy.wait_recv()
    ing_r[...] = cot_r[...].astype(F32) + (vsend[...].astype(F32) + vrecv[...].astype(F32))
    early.gather1()
    own.finish()
    bo = ring.take(1)
    gat = pl.ds(row - 16, 16)
    os_copy = ring.copy(ototal.at[gat], gsib, bo, bo, sibling)
    os_copy.start()
    ring.sent.append(os_copy)
    xlate.finish()
    bs2 = ring.take(1)
    xs_copy = ring.copy(xtotal, xsib, bs2, bs2, sibling)
    xs_copy.start()
    ring.sent.append(xs_copy)
    early.finish()
    bs = ring.take(1)
    es_copy = ring.copy(etotal, esib, bs, bs, sibling)
    es_copy.start()
    ring.sent.append(es_copy)
    es_copy.wait_recv()
    os_copy.wait_recv()
    xs_copy.wait_recv()
    done_edges(ring)
    for c in ring.sent:
        c.wait_send()


def finish(sizes, *refs):
    (out_v, ing_v, etotal, esib, xtotal, xsib, ototal, gsib,
     out_h, ing_h, ggain_h, gwin_h, gwout_h, gcw_h, gcb_h, gwx_h, gwdt_h, gbias_h, galog_h, gskip_h,
     ggain, gwin, gwout, gcw, gcb, gwx, gwdt, gbias, galog, gskip, sems) = refs
    nx, ns, state = sizes
    dirn = lax.axis_index("dir")
    width = ing_v.shape[1]
    hw = xtotal.shape[1]
    inner = 2 * hw
    started = []

    def write(src, dst):
        c = pltpu.make_async_copy(src, dst, sems.at[len(started)])
        c.start()
        started.append(c)

    write(out_v, out_h)
    write(ing_v, ing_h)

    def halves(mine, other):
        a, b = mine[...].astype(F32), other[...].astype(F32)
        return jnp.where(dirn == 0, a, b), jnp.where(dirn == 0, b, a)

    gz, go = halves(etotal, esib)
    gwout[pl.ds(0, width)] = go[:, :width]
    gwout[pl.ds(width, width)] = go[:, width:]
    write(gwout, gwout_h)
    gwin[:, inner:] = gz
    left, right = halves(xtotal, xsib)
    gwin[:, :hw] = left
    gwin[:, hw:inner] = right
    write(gwin, gwin_h)
    row = 0
    parts = []
    for k in (nx, ns, state, 8):
        parts.append(jnp.concatenate([ototal[pl.ds(row, k)], ototal[pl.ds(row + k, k)]], axis=1).astype(F32))
        row += 2 * k
    tail = parts[3]
    gwx[0], gwdt[0], galog[0] = parts[:3]
    gcw[0] = tail[0:4]
    gcb[...], gbias[...], gskip[...] = tail[4:5], tail[5:6], tail[6:7]
    both = ototal[pl.ds(row - 16, 16)].astype(F32) + gsib[...].astype(F32)
    ggain[...] = both[7:8, :width]
    for a, b in ((gwx, gwx_h), (gwdt, gwdt_h), (galog, galog_h), (gcw, gcw_h), (gcb, gcb_h),
                 (gbias, gbias_h), (gskip, gskip_h), (ggain, ggain_h)):
        write(a, b)
    for c in started:
        c.wait()


def done_edges(ring):
    for c, cond in ring.edges:
        @pl.when(cond)
        def _():
            c.wait_send()


def on_device(n, tokens, gain, w_in, w_out, conv_w, conv_b, w_x, w_dt, dt_bias, a_log, d_skip, lengths, cotangent):
    rows, width = tokens.shape
    inner = w_out.shape[0]
    state = a_log.shape[1]
    rank = w_dt.shape[1]
    g_in, g_out = log_split(n)
    g3 = max(n // 16, 1)
    hw = inner // 2
    cells = state * inner // LANES
    gain = gain.reshape(1, width)
    w_xt = jnp.swapaxes(w_x, 1, 2)
    nsem = 16 + g_in + g_out + 16 + 4 * 16 + 3 * g3
    vm = pltpu.VMEM
    sds = jax.ShapeDtypeStruct
    ins = (tokens, gain, w_in, w_out, conv_w, conv_b, w_xt, w_dt, dt_bias, a_log, d_skip, cotangent)
    direct = [vm((256, hw), F32), vm((256, hw), B16), vm((16, 16, hw), B16), vm((g3, 16, hw), B16)]
    scratch = [vm(x.shape, x.dtype) for x in ins] + [
        pltpu.SemaphoreType.DMA((len(ins),)),
        vm((HALO, width), B16),
        vm((rows * state, LANES), B16), vm((rows * state, 2 * LANES), F32),
        vm((rows * state, inner), F32), vm(((rows + 1) * state, inner), F32),
        vm((rows, inner), F32), vm((rows, inner), F32), vm((rows, inner), F32),
        vm((HALO + rows, inner), F32), vm((rows + HALO, inner), F32), vm((2 * HALO, inner), F32),
        vm((HALO, inner), B16), vm((HALO, inner), B16),
        vm((g_in, 2 * cells + 16, LANES), B16), vm((2, cells + 16, LANES), B16),
        vm((g_out, cells + 16, LANES), B16),
        vm((rows, inner), F32), vm((rows, inner), F32), vm((rows, inner), F32),
        vm((rows, width), F32), vm((rows, width), F32),
        vm((rows, width), B16), vm((rows, width), B16),
        vm((2, width, inner), B16), vm((width, inner), B16), vm((width, inner), F32),
        vm((width, inner), B16), vm((4, width // 4, inner), B16),
        vm((width // 4, inner), B16), vm((4, width // 16, inner), B16), vm((g3, width // 16, inner), B16),
        vm((2, width, hw), B16), vm((width, hw), B16), *direct, *direct,
        pltpu.SemaphoreType.DMA((nsem,)), pltpu.SemaphoreType.DMA((nsem,)),
    ]
    mids = [
        vm((rows, width), B16), vm((rows, width), F32), vm((width, inner), B16), vm((width, inner), B16),
        vm((width, hw), B16), vm((width, hw), B16), vm((256, hw), B16), vm((16, hw), B16),
    ]
    in_vmem = pl.BlockSpec(memory_space=pltpu.VMEM)
    in_hbm = pl.BlockSpec(memory_space=pltpu.HBM)
    sums = pl.pallas_call(
        functools.partial(kernel, n, nsem),
        out_shape=mids,
        in_specs=[in_hbm] * len(ins) + [pl.BlockSpec(memory_space=pltpu.SMEM)],
        out_specs=[in_vmem] * len(mids),
        scratch_shapes=scratch,
        compiler_params=pltpu.CompilerParams(
            collective_id=0, has_side_effects=True, vmem_limit_bytes=56 * 2**20
        ),
    )(*ins, lengths)
    outs = (
        sds((rows, width), B16), sds((rows, width), F32), sds((1, width), F32),
        sds(w_in.shape, F32), sds(w_out.shape, F32), sds(conv_w.shape, F32), sds(conv_b.shape, F32),
        sds(w_xt.shape, F32), sds(w_dt.shape, F32), sds(dt_bias.shape, F32), sds(a_log.shape, F32),
        sds(d_skip.shape, F32),
    )
    res = pl.pallas_call(
        functools.partial(finish, (w_xt.shape[1], rank, state)),
        out_shape=outs,
        in_specs=[in_vmem] * len(mids),
        out_specs=[in_hbm] * len(outs),
        scratch_shapes=[vm(x.shape, x.dtype) for x in outs[2:]] + [pltpu.SemaphoreType.DMA((len(outs),))],
        compiler_params=pltpu.CompilerParams(vmem_limit_bytes=8 * 2**20),
    )(*sums)
    return (res[0], res[1], res[2].reshape(width)) + tuple(res[3:7]) + (jnp.swapaxes(res[7], 1, 2),) + tuple(res[8:])


def solution(mesh):
    d1, d2 = P("dir", None), P("dir", None, None)
    return jax.shard_map(
        functools.partial(on_device, mesh.shape["seq"]),
        mesh=mesh,
        in_specs=(P("seq", None), P(), P(), P(), d2, d1, d2, d2, d1, d2, d1, P(), P("seq", None)),
        out_specs=(P("seq", None), P("seq", None), P(), P(), P(), d2, d1, d2, d2, d1, d2, d1),
        check_vma=False,
    )
```

```python
import functools

import jax
import jax.numpy as jnp
from jax import lax
from jax.experimental import pallas as pl
from jax.experimental.pallas import tpu as pltpu
from jax.sharding import PartitionSpec as P

F32 = jnp.float32
B16 = jnp.bfloat16
MESH = pl.DeviceIdType.MESH
NORM_EPS = 1e-05
LOG2E = 1.4426950408889634
RESET = 1e6
HALO = 16
LANES = 128
E_TWO, X_TWO, O_TWO = (True, True, False), (True, False, False), (True, True, True)


def dot(a, b, ca=1, cb=0):
    return lax.dot_general(a, b, (((ca,), (cb,)), ((), ())), preferred_element_type=F32)


def silu_grad(v, sigma):
    return sigma * (1.0 + v * (1.0 - sigma))


def softplus(v):
    u = jnp.exp(-jnp.abs(v))
    s = u / (2.0 + u)
    q = s * s
    p = 1.0 / 13.0
    for k in (11.0, 9.0, 7.0, 5.0, 3.0):
        p = p * q + 1.0 / k
    return jnp.maximum(v, 0.0) + 2.0 * s * (p * q + 1.0)


def log_split(n):
    inner = 1
    while inner * inner * 4 <= n:
        inner *= 2
    return inner, n // inner


class Ring:
    def __init__(self, ssem, rsem, size):
        self.ssem, self.rsem, self.next, self.size = ssem, rsem, 0, size
        self.sent, self.edges = [], []

    def take(self, count):
        base = self.next
        self.next += count
        assert self.next <= self.size
        return base

    def copy(self, src, dst, s, r, dev):
        return pltpu.make_async_remote_copy(
            src_ref=src, dst_ref=dst, send_sem=self.ssem.at[s], recv_sem=self.rsem.at[r],
            device_id=dev, device_id_type=MESH,
        )


class Exchange:
    def __init__(self, ring, size, me, dev):
        self.ring, self.size, self.me, self.dev = ring, size, me, dev
        self.base = ring.take(size)

    def start(self, src, dst):
        self.src, self.dst = src, dst
        for r in range(1, self.size):
            peer = lax.rem(self.me + r, self.size)
            c = self.ring.copy(src(peer), dst(self.me), self.base + r, self.base + self.me, self.dev(peer))
            c.start()
            self.ring.sent.append(c)

    def wait_one(self, r):
        peer = lax.rem(self.me + r, self.size)
        self.ring.copy(
            self.src(peer), self.dst(peer), self.base + r, self.base + peer, self.dev(peer)
        ).wait_recv()

    def wait(self):
        for r in range(1, self.size):
            self.wait_one(r)


def flip(a, mask):
    for b in range(4):
        if mask >> b & 1:
            a = a + (1 << b) * (1 - 2 * lax.rem(a // (1 << b), 2))
    return a


class Sum:
    def __init__(self, ring, n, seq, dirn, own, total, send, recv, over, blocks, two):
        self.ring, self.own, self.total, self.send, self.over = ring, own, total, send, over
        self.blocks, self.k, self.g3 = blocks, total.shape[0] // 16, n // 16
        self.me, hi = lax.rem(seq, 16), seq // 16
        self.hi = hi
        base = seq - self.me
        self.dev = lambda p: (dirn, base + p)
        self.lo, self.mid = lax.rem(self.me, 4), self.me // 4
        self.peers = [flip(self.me, m) for m in range(15, 0, -1)]
        self.out_two, self.back_two, self.far_first = two
        near = lambda p: self.dev(self.me - lax.rem(self.me, 4) + p)
        far = lambda p: self.dev(p * 4 + lax.rem(self.me, 4))
        if self.far_first:
            near, far, self.lo, self.mid = far, near, self.mid, self.lo
        if self.out_two:
            self.recv, self.send2, self.recv2 = recv
            self.ex1, self.ex2 = Exchange(ring, 4, self.lo, near), Exchange(ring, 4, self.mid, far)
        else:
            (self.recv,) = recv
            self.s1 = ring.take(16)
        if self.back_two:
            self.back2, self.back1 = Exchange(ring, 4, self.mid, far), Exchange(ring, 4, self.lo, near)
        else:
            self.s2 = ring.take(16)
        self.top = Exchange(ring, self.g3, hi, lambda p: (dirn, seq + (p - hi) * 16)) if self.g3 > 1 else None

    def block(self, p):
        if (self.out_two or self.back_two) and not self.far_first:
            return lax.rem(p, 4) * 4 + p // 4
        return p if self.blocks == 16 else lax.rem(p + 12, 16)

    def at(self, b, count=1):
        size = self.k * count
        return pl.ds(pl.multiple_of(b * size, size), size)

    def owns(self, p, body):
        if self.blocks < 16:
            pl.when(self.block(p) < self.blocks)(body)
        else:
            body()

    def go(self, c, owner):
        self.owns(owner, c.start)
        if self.blocks < 16:
            self.ring.edges.append((c, self.block(owner) < self.blocks))
        else:
            self.ring.sent.append(c)

    def scatter(self):
        self.send[...] = self.own(slice(None)).astype(B16)
        if self.out_two:
            self.ex1.start(lambda p: self.send.at[self.at(p, 4)], lambda s: self.recv.at[s])
            return
        for r, p in enumerate(self.peers):
            src = self.send.at[self.at(self.block(p))]
            self.go(self.ring.copy(src, self.recv.at[self.me], self.s1 + r, self.s1 + self.me, self.dev(p)), p)

    def scatter2(self):
        self.recv[self.lo] = jnp.zeros(self.recv.shape[1:], B16)
        self.ex1.wait()
        acc = self.own(self.at(self.lo, 4))
        for j in range(4):
            acc = acc + self.recv[j].astype(F32)
        self.send2[...] = acc.astype(B16)
        self.ex2.start(lambda p: self.send2.at[self.at(p)], lambda s: self.recv2.at[s])

    def add(self):
        if self.out_two:
            self.recv2[self.mid] = jnp.zeros(self.recv2.shape[1:], B16)
            self.ex2.wait()
            parts, count = self.recv2, 4
            acc = self.send2[self.at(self.mid)].astype(F32)
        else:
            self.recv[self.me] = jnp.zeros(self.recv.shape[1:], B16)
            for r, p in reversed(list(enumerate(self.peers))):
                there = self.send.at[pl.ds(0, self.k)]
                self.ring.copy(there, self.recv.at[p], self.s1 + r, self.s1 + p, self.dev(p)).wait_recv()
            parts, count = self.recv, 16
            acc = self.own(self.at(self.block(self.me)))
        for j in range(count):
            acc = acc + parts[j].astype(F32)
        if self.top is not None:
            self.over[self.hi] = acc.astype(B16)
            self.top.start(lambda p: self.over.at[self.hi], lambda s: self.over.at[s])
            self.top.wait()
            for _ in range(1, self.g3):
                self.ring.sent.pop().wait_send()
            acc = self.over[0].astype(F32)
            for j in range(1, self.g3):
                acc = acc + self.over[j].astype(F32)
        self.total[self.at(self.block(self.me))] = acc.astype(B16)

    def gather(self):
        self.owns(self.me, self.add)
        mine = self.total.at[self.at(self.block(self.me))]
        if self.back_two:
            there = lambda s: self.total.at[self.at(self.lo * 4 + s)]
            self.back2.start(lambda p: there(self.mid), there)
            return
        for r, p in enumerate(self.peers):
            self.go(self.ring.copy(mine, mine, self.s2 + r, self.s2 + self.me, self.dev(p)), self.me)

    def gather1(self):
        self.back2.wait()
        there = lambda s: self.total.at[self.at(s, 4)]
        self.back1.start(lambda p: there(self.lo), there)

    def took(self, p):
        there = self.total.at[self.at(self.block(p))]
        self.owns(p, self.ring.copy(there, there, self.s2, self.s2 + p, self.dev(p)).wait_recv)

    def finish(self):
        for p in reversed(self.peers):
            self.took(p)

    def mirror(self, other, sibling):
        copies = []

        def on(quarter):
            s = self.ring.take(1)
            rows = self.at(quarter, 4)
            c = self.ring.copy(self.total.at[rows], other.at[rows], s, s, sibling)
            c.start()
            self.ring.sent.append(c)
            copies.append(c)

        if self.back_two:
            for r in range(4):
                p = lax.rem(self.lo + r, 4)
                if r > 0:
                    self.back1.wait_one(r)
                on(p)
        else:
            by_lo = self.out_two and not self.far_first
            for r in range(4):
                quarter = lax.rem((self.lo if by_lo else self.mid) + r, 4)
                for x in range(4):
                    other_at = lax.rem((self.mid if by_lo else self.lo) + x, 4)
                    p = other_at * 4 + quarter if by_lo else quarter * 4 + other_at
                    if r + x > 0:
                        self.took(p)
                on(quarter)
        return copies


def kernel(n, nsem, *refs):
    (tok_h, gain_h, win_h, wout_h, cw_h, cb_h, wx_h, wdt_h, bias_h, alog_h, skip_h, cot_h, len_r,
     out_r, ing_r, etotal, esib, xtotal, xsib, ototal, gsib,
     tok_r, gain_r, win_r, wout_r, cw_r, cb_r, wx_r, wdt_r, bias_r, alog_r, skip_r, cot_r, lsem,
     tail_s, halo, picked, bcr, dref, hs, sdr, sar, gyr, xpad, taps, later, gpad, gext, ghsend, ghrecv,
     sgr, cgr, zgr, gsr, skr, ntx, woutf,
     xin1, xsend2, xin2, yr, adjr, dtar, bsend, brecv, vsend, vrecv,
     epair, eprecv, esend, *rest) = refs
    erecv, rest = rest[:3 if E_TWO[0] else 1], rest[3 if E_TWO[0] else 1:]
    eover, xpair, xprecv, xsend, *rest = rest
    xrecv, rest = rest[:3 if X_TWO[0] else 1], rest[3 if X_TWO[0] else 1:]
    xover, opart, osend, *rest = rest
    orecv, rest = rest[:3 if O_TWO[0] else 1], rest[3 if O_TWO[0] else 1:]
    oover, ssem, rsem = rest
    rows, width = tok_r.shape
    inner = wout_r.shape[0]
    state = alog_r.shape[1]
    chunks = inner // LANES
    dirn = lax.axis_index("dir")
    seq = lax.axis_index("seq")
    place = seq + dirn * (n - 1 - 2 * seq)
    seq_at = lambda p: p + dirn * (n - 1 - 2 * p)
    dev_at = lambda p: (dirn, seq_at(p))
    sibling = (1 - dirn, seq)
    g_in, g_out = log_split(n)
    lo = lax.rem(place, g_in)
    hi = place // g_in
    ring = Ring(ssem, rsem, nsem)
    up = lax.rem(place + 1, n)
    down = lax.rem(place + n - 1, n)

    barrier = pltpu.get_barrier_semaphore()
    line, s_hi = lax.rem(seq, 16), seq // 16
    peers = [sibling, dev_at(up), dev_at(down)]
    if all(E_TWO[:2] + X_TWO[:2] + O_TWO[:2]):
        near, far = lax.rem(line, 4), line // 4
        peers += [(dirn, seq - near + lax.rem(near + r, 4)) for r in range(1, 4)]
        peers += [(dirn, seq + (lax.rem(far + r, 4) - far) * 4) for r in range(1, 4)]
    else:
        peers += [(dirn, seq - line + lax.rem(line + r, 16)) for r in range(1, 16)]
    if n != 16:
        peers += [(dirn, seq + (lax.rem(s_hi + r, n // 16) - s_hi) * 16) for r in range(1, n // 16)]
        peers += [dev_at(hi * g_in + lax.rem(lo + r, g_in)) for r in range(1, g_in)]
        peers += [dev_at(lax.rem(hi + r, g_out) * g_in + lo) for r in range(1, g_out)]
    for dev in peers:
        pl.semaphore_signal(barrier, inc=1, device_id=dev, device_id_type=MESH)

    loads = {}
    pairs = [(tok_h, tok_r), (gain_h, gain_r), (win_h, win_r), (cot_h, cot_r), (wout_h, wout_r), (cw_h, cw_r),
             (cb_h, cb_r), (wx_h, wx_r), (wdt_h, wdt_r), (bias_h, bias_r), (alog_h, alog_r), (skip_h, skip_r)]
    for i, (a, b) in enumerate(pairs):
        loads[i] = pltpu.make_async_copy(a, b, lsem.at[i])
        loads[i].start()

    def turn(size):
        r = lax.broadcasted_iota(jnp.int32, (size, size), 0)
        c = lax.broadcasted_iota(jnp.int32, (size, size), 1)
        return jnp.where(c == r + dirn * (size - 1 - 2 * r), 1.0, 0.0).astype(B16)

    turn_t, turn_f = turn(rows), turn(width)
    turned = lambda v, tt: dot(dot(tt, v).astype(B16), turn_f)

    total = n * rows
    q = lax.broadcasted_iota(jnp.int32, (rows + 2 * HALO, LANES), 0) + (place * rows - HALO)
    dist = jnp.full(q.shape, 1 << 30, jnp.int32)
    before = jnp.int32(0)
    for w in range(len_r.shape[0]):
        after = before + len_r[w]
        delta = q - (before + dirn * (total - after - before))
        dist = jnp.where((delta >= 0) & (delta < dist), delta, dist)
        before = after
    over_lanes = lambda v: jnp.concatenate([v] * (inner // v.shape[1]), axis=1)
    for k in range(1, 4):
        later[k - 1] = jnp.where((dist >= k) & (q < total), 1.0, 0.0)
    dist_own = over_lanes(dist[HALO:HALO + rows])

    def normalise(v):
        inv = lax.rsqrt(jnp.mean(v * v, axis=1, keepdims=True) + NORM_EPS)
        vr = v * inv
        return inv, vr, (vr * gain_r[...]).astype(B16)

    for i in range(3):
        loads[i].wait()
    tok = turned(tok_r[...], turn_t)
    inv, vr, normed = normalise(tok)
    proj = dot(normed, win_r[...])
    xi_b = proj[:, :inner].astype(B16)
    xi = xi_b.astype(F32)
    zgate = proj[:, inner:]
    xpad[pl.ds(0, HALO)] = jnp.zeros((HALO, inner), F32)
    xpad[pl.ds(HALO, rows)] = xi
    tail_s[:, :inner] = xi_b[rows - HALO:]
    tail_s[:, inner:] = tok[rows - HALO:].astype(B16)

    pl.semaphore_wait(barrier, len(peers))
    b0 = ring.take(1)
    tok_copy = ring.copy(tail_s, halo, b0, b0, dev_at(up))
    ring.edges.append((tok_copy, place < n - 1))

    @pl.when(place < n - 1)
    def _():
        tok_copy.start()

    @pl.when(place == 0)
    def _():
        halo[...] = jnp.zeros(halo.shape, B16)

    for i in range(3, len(pairs)):
        loads[i].wait()
    cot = turned(cot_r[...], turn_t).astype(B16)
    sig_z = jax.nn.sigmoid(zgate)
    gate = zgate * sig_z
    gmix = dot(cot, wout_r[...], 1, 1)
    gy = gmix * gate
    gyr[...] = gy
    rate = -jnp.exp(alog_r[0])
    rate2 = rate * LOG2E
    cut = lambda v: [v[:, c * LANES:(c + 1) * LANES] for c in range(chunks)]
    a2 = cut(rate2)
    a1 = cut(rate)

    def drive(count):
        conv = xpad[pl.ds(HALO, count)] * cw_r[0, 0:1] + cb_r[...]
        for k in range(1, 4):
            tap = jnp.where(dist_own[:count] >= k, xpad[pl.ds(HALO - k, count)], 0.0)
            taps[k - 1, pl.ds(0, count)] = tap
            conv = conv + tap * cw_r[0, k:k + 1]
        sig_c = jax.nn.sigmoid(conv)
        act_b = (conv * sig_c).astype(B16)
        low_t = dot(wx_r[0, pl.ds(0, state)], act_b, 1, 1).astype(B16)
        bc = dot(act_b, wx_r[0, pl.ds(state, 2 * state)], 1, 1)
        pre = dot(low_t, wdt_r[0], 0, 0) + bias_r[...]
        step = softplus(pre)
        sd = jnp.where(dist_own[:count] == 0, RESET, step)
        sdr[pl.ds(0, count)] = sd
        sar[pl.ds(0, count)] = step * act_b.astype(F32)
        return conv, sig_c, act_b, low_t, pre, step, sd, bc

    wide = 2 * state
    lane_k = lax.broadcasted_iota(jnp.int32, (state, LANES), 1)
    row_k = lax.broadcasted_iota(jnp.int32, (state, LANES), 0)
    own_k = jnp.where((lane_k < 2 * wide) & (lax.rem(lane_k, state) == row_k), 1.0, 0.0)
    fan_r = lax.rem(lax.broadcasted_iota(jnp.int32, (LANES, 2 * LANES), 0), wide) // state
    fan_c = lax.broadcasted_iota(jnp.int32, (LANES, 2 * LANES), 1) // LANES
    fan = jnp.where(fan_r == fan_c, 1.0, 0.0).astype(B16)

    def spread(bc, first):
        count = bc.shape[0]
        top = bc.astype(B16).astype(F32)
        none = jnp.zeros((count, LANES - 2 * wide), F32)
        both = jnp.concatenate([top, bc - top, none], axis=1)
        for t in range(count):
            picked[pl.ds((first + t) * state, state)] = (both[t:t + 1] * own_k).astype(B16)
        at = pl.ds(first * state, count * state)
        bcr[at] = dot(picked[at], fan)

    def summarise(g, carry):
        h, p, l = [list(x) for x in carry]
        at8 = pl.ds(pl.multiple_of(g * 8, 8), 8)
        sd8, sa8, gy8 = sdr[at8], sar[at8], gyr[at8]
        for c in range(chunks):
            lane = slice(c * LANES, (c + 1) * LANES)
            for j in range(8):
                at = pl.ds(pl.multiple_of((g * 8 + j) * state, state), state)
                br, cr = bcr[at, :LANES], bcr[at, LANES:]
                d = jnp.exp2(sd8[j:j + 1, lane] * a2[c])
                dref[at, lane] = d
                h[c] = d * h[c] + sa8[j:j + 1, lane] * br
                p[c] = p[c] * d
                l[c] = l[c] + p[c] * (gy8[j:j + 1, lane] * cr)
        return tuple(h), tuple(p), tuple(l)

    zero = tuple(jnp.zeros((state, LANES), F32) for _ in range(chunks))
    one = tuple(jnp.ones((state, LANES), F32) for _ in range(chunks))
    join = lambda v: jnp.concatenate(v, axis=1)
    head = HALO // 8

    whole = drive(rows)
    spread(whole[7][HALO:], HALO)
    h_late, p_late, l_late = lax.fori_loop(head, rows // 8, summarise, (zero, one, zero), unroll=2)

    @pl.when(place > 0)
    def _():
        tok_copy.wait_recv()

    xpad[pl.ds(0, HALO)] = halo[:, :inner].astype(F32)
    start = drive(HALO)
    low_first = jnp.concatenate([start[3].astype(F32), jnp.zeros((state, rows - HALO), F32)], axis=1)
    lane_low = lax.broadcasted_iota(jnp.int32, low_first.shape, 1)
    dt_low = jnp.where(lane_low < HALO, low_first, whole[3].astype(F32)).astype(B16)
    patch = lambda i: jnp.concatenate([start[i], whole[i][HALO:]], axis=0)
    conv, sig_c, act_b, pre, step, sd = [patch(i) for i in (0, 1, 2, 4, 5, 6)]
    act = act_b.astype(F32)
    spread(start[7], 0)
    h_first, p_first, l_first = lax.fori_loop(0, head, summarise, (zero, one, zero), unroll=2)
    h_sum = join(h_late) + join(p_late) * join(h_first)
    l_sum = join(l_first) + join(p_first) * join(l_late)

    def pair_rows(v):
        top = v.astype(B16).astype(F32)
        both = cut(top) + cut(v - top) + [jnp.zeros((16 - 2 * chunks, LANES), F32)]
        return jnp.concatenate(both, axis=0).astype(B16)

    blk_s = chunks * state
    stack = lambda v: jnp.concatenate(cut(v), axis=0).astype(B16)
    unstack = lambda v, at: join([v[at + c * state:at + (c + 1) * state].astype(F32) for c in range(chunks)])
    def unpair1(v):
        r = v[blk_s:blk_s + 16].astype(F32)
        return join([r[c:c + 1] + r[chunks + c:chunks + c + 1] for c in range(chunks)])
    xin1[lo, pl.ds(0, blk_s)] = stack(h_sum)
    xin1[lo, pl.ds(blk_s, 16)] = pair_rows(jnp.sum(sd, axis=0, keepdims=True))
    xin1[lo, pl.ds(blk_s + 16, blk_s)] = stack(l_sum)
    ex1 = Exchange(ring, g_in, lo, lambda p: dev_at(hi * g_in + p))
    ex1.start(lambda p: xin1.at[lo], lambda s: xin1.at[s])

    _, vr_h, normed_h = normalise(halo[:, inner:].astype(F32))
    ntx[...] = jnp.concatenate([normed, normed_h], axis=0).T
    sgr[...] = jax.nn.sigmoid(pre)
    cgr[...] = silu_grad(conv, sig_c)
    zgr[...] = gmix * silu_grad(zgate, sig_z)
    gsr[...] = gy * skip_r[...]
    skr[...] = skip_r[...] * act
    woutf[...] = dot(wout_r[...], turn_f).astype(B16)
    gskip = jnp.sum(gy * act, axis=0, keepdims=True)

    ex1.wait()
    sums = [unpair1(xin1[j]) for j in range(g_in)]
    fwd = bwd = fwd_all = bwd_all = jnp.zeros((state, inner), F32)
    s_fwd = s_bwd = s_all = jnp.zeros((1, inner), F32)
    for j in range(g_in):
        fade = jnp.exp2(rate2 * sums[j])
        fwd_all = fade * fwd_all + unstack(xin1[j], 0)
        fwd = jnp.where(j < lo, fwd_all, fwd)
        s_all = s_all + sums[j]
        s_fwd = jnp.where(j < lo, s_all, s_fwd)
    for j in reversed(range(g_in)):
        fade = jnp.exp2(rate2 * sums[j])
        bwd_all = fade * bwd_all + unstack(xin1[j], blk_s + 16)
        bwd = jnp.where(j > lo, bwd_all, bwd)
        s_bwd = jnp.where(j > lo, s_bwd + sums[j], s_bwd)
    s_pair = pair_rows(s_all)
    for k, v in enumerate((fwd_all, bwd_all)):
        xsend2[k, pl.ds(0, blk_s)] = stack(v)
        xsend2[k, pl.ds(blk_s, 16)] = s_pair
    xin2[hi] = jnp.zeros(xin2.shape[1:], B16)
    ex2 = Exchange(ring, g_out, hi, lambda p: dev_at(p * g_in + lo))
    ex2.start(lambda p: xsend2.at[jnp.where(p > hi, 0, 1)], lambda s: xin2.at[s])
    ex2.wait()
    h_in = l_in = jnp.zeros((state, inner), F32)
    for k in range(g_out):
        new = jnp.exp2(rate2 * unpair1(xin2[k])) * h_in
        h_in = jnp.where(k < hi, new + unstack(xin2[k], 0), h_in)
    for k in reversed(range(g_out)):
        new = jnp.exp2(rate2 * unpair1(xin2[k])) * l_in
        l_in = jnp.where(k > hi, new + unstack(xin2[k], 0), l_in)
    h_in = jnp.exp2(rate2 * s_fwd) * h_in + fwd
    l_in = jnp.exp2(rate2 * s_bwd) * l_in + bwd

    sub = lax.broadcasted_iota(jnp.int32, (8, LANES), 0)
    lane_at = lax.broadcasted_iota(jnp.int32, (state, LANES), 1)

    def sum_rows(v):
        for bit in (1, 2, 4):
            mine = lax.rem(sub // bit, 2) == 0
            v = [
                jnp.where(mine, a, b) + pltpu.roll(jnp.where(mine, b, a), bit, 0)
                for a, b in zip(v[::2], v[1::2])
            ]
        return v[0]

    halve = lambda v: v[:8] + v[8:]
    hs[pl.ds(0, state)] = h_in

    def forward(g, carry):
        h, gc = list(carry[0]), carry[1]
        at8 = pl.ds(pl.multiple_of(g * 8, 8), 8)
        sa8, gy8 = sar[at8], gyr[at8]
        over = [None] * 8
        for c in range(chunks):
            lane = slice(c * LANES, (c + 1) * LANES)
            ys = []
            for j in range(8):
                at = pl.ds(pl.multiple_of((g * 8 + j) * state, state), state)
                nxt = pl.ds(pl.multiple_of((g * 8 + j + 1) * state, state), state)
                h[c] = dref[at, lane] * h[c] + sa8[j:j + 1, lane] * bcr[at, :LANES]
                hs[nxt, lane] = h[c]
                ys.append(halve(h[c] * bcr[at, LANES:]))
                new = h[c] * gy8[j:j + 1, lane]
                over[j] = new if c == 0 else over[j] + new
            yr[at8, lane] = sum_rows(ys)
        for j in range(8):
            gc = jnp.where(lane_at == g * 8 + j, jnp.sum(over[j], axis=1, keepdims=True), gc)
        return tuple(h), gc

    none = jnp.zeros((state, rows), F32)
    _, g_c = lax.fori_loop(0, rows // 8, forward, (tuple(cut(h_in)), none), unroll=4)
    y = yr[...] + skr[...]
    mixed = (y * gate).astype(B16)
    gz = (zgr[...] * y).astype(B16)

    epair[0] = dot(ntx[:, :rows], gz).astype(B16)
    gwo = dot(mixed, cot, 0, 0).astype(B16)
    epair[1, :, :width] = gwo[:width]
    epair[1, :, width:] = gwo[width:]
    be = ring.take(1)
    e_copy = ring.copy(epair.at[1 - dirn], eprecv, be, be, sibling)
    e_copy.start()
    ring.sent.append(e_copy)

    def backward(i, carry):
        m, acc, gb = list(carry[0]), list(carry[1]), carry[2]
        g = rows // 8 - 1 - i
        at8 = pl.ds(pl.multiple_of(g * 8, 8), 8)
        sd8, gy8, sa8 = sdr[at8], gyr[at8], sar[at8]
        over = [None] * 8
        for c in range(chunks):
            lane = slice(c * LANES, (c + 1) * LANES)
            adjs, dts = [None] * 8, [None] * 8
            for j in reversed(range(8)):
                at = pl.ds(pl.multiple_of((g * 8 + j) * state, state), state)
                lam = m[c] + gy8[j:j + 1, lane] * bcr[at, LANES:]
                m[c] = dref[at, lane] * lam
                r = m[c] * hs[at, lane] * a1[c]
                acc[c] = acc[c] + r * sd8[j:j + 1, lane]
                adjs[j] = halve(lam * bcr[at, :LANES])
                dts[j] = halve(r)
                new = lam * sa8[j:j + 1, lane]
                over[j] = new if c == 0 else over[j] + new
            adjr[at8, lane] = sum_rows(adjs)
            dtar[at8, lane] = sum_rows(dts)
        for j in range(8):
            gb = jnp.where(lane_at == g * 8 + j, jnp.sum(over[j], axis=1, keepdims=True), gb)
        return tuple(m), tuple(acc), gb

    carry = lax.fori_loop(0, rows // 32, backward, (tuple(cut(l_in)), zero, none), unroll=4)
    e_own = lambda at: epair[dirn, at].astype(F32) + eprecv[at].astype(F32)
    early = Sum(ring, n, seq, dirn, e_own, etotal, esend, erecv, eover, 16, E_TWO)
    e_copy.wait_recv()
    early.scatter()
    _, galog, g_b = lax.fori_loop(rows // 32, rows // 8, backward, carry, unroll=4)
    galog = join(galog)
    adj = adjr[...]
    gpre = (dtar[...] + adj * act) * sgr[...]
    gbias = jnp.sum(gpre, axis=0, keepdims=True)
    gpre = gpre.astype(B16)
    glow = dot(gpre, wdt_r[0], 1, 1).astype(B16)
    gbc = jnp.concatenate([g_b, g_c], axis=0).astype(B16)
    gact = gsr[...] + adj * step + dot(gbc, wx_r[0, pl.ds(state, 2 * state)], 0, 0)
    gact = gact + dot(glow, wx_r[0, pl.ds(0, state)])
    gconv_b = (gact * cgr[...]).astype(B16)
    gconv = gconv_b.astype(F32)

    gpad[pl.ds(0, rows)] = gconv
    gpad[pl.ds(rows, HALO)] = jnp.zeros((HALO, inner), F32)
    gext[pl.ds(0, HALO)] = jnp.zeros((HALO, inner), F32)
    gext[pl.ds(HALO, HALO)] = gconv[:HALO]
    gxi = gconv * cw_r[0, 0:1]
    gxe = jnp.zeros((HALO, inner), F32)
    for k in range(1, 4):
        w = cw_r[0, k:k + 1]
        gxi = gxi + gpad[pl.ds(k, rows)] * over_lanes(later[k - 1, pl.ds(HALO + k, rows)]) * w
        gxe = gxe + gext[pl.ds(k, HALO)] * over_lanes(later[k - 1, pl.ds(k, HALO)]) * w
    gxi_b = jnp.concatenate([gxi, gxe], axis=0).astype(B16)
    gwx_half = dot(ntx[...], gxi_b).astype(B16)
    hw = inner // 2
    xpair[0] = gwx_half[:, :hw]
    xpair[1] = gwx_half[:, hw:]
    bx = ring.take(1)
    x_copy = ring.copy(xpair.at[1 - dirn], xprecv, bx, bx, sibling)
    x_copy.start()
    ring.sent.append(x_copy)
    ghsend[...] = gconv_b[:HALO]
    bh = ring.take(1)
    h_copy = ring.copy(ghsend, ghrecv, bh, bh, dev_at(down))
    ring.edges.append((h_copy, place > 0))

    @pl.when(place > 0)
    def _():
        h_copy.start()

    gwx_t = jnp.concatenate([dot(glow, act_b, 0, 0), dot(gbc, act_b)], axis=0)
    gwdt = dot(dt_low, gpre)
    gn_x = dot(gxi_b, win_r[:, :inner], 1, 1)
    gn_z = dot(gz, win_r[:, inner:], 1, 1)
    ggain = jnp.sum((gn_x[:rows] + gn_z) * vr, axis=0, keepdims=True)
    ggain = ggain + jnp.sum(gn_x[rows:] * vr_h, axis=0, keepdims=True)
    gcb = jnp.sum(gconv, axis=0, keepdims=True)
    gcw = [jnp.sum(gconv * (xi if k == 0 else taps[k - 1]), axis=0, keepdims=True) for k in range(4)]
    pad_gain = jnp.concatenate([ggain, jnp.zeros((1, inner - width), F32)], axis=1)
    tail = jnp.concatenate(gcw + [gcb, gbias, gskip, pad_gain], axis=0)
    row = 0
    for part in (gwx_t, gwdt, galog, tail):
        k = part.shape[0]
        opart[pl.ds(row, k)] = part[:, :hw]
        opart[pl.ds(row + k, k)] = part[:, hw:]
        row += 2 * k
    opart[pl.ds(row, opart.shape[0] - row)] = jnp.zeros((opart.shape[0] - row, hw), F32)
    own = Sum(ring, n, seq, dirn, lambda at: opart[at], ototal, osend, orecv, oover, 16 if any(O_TWO[:2]) else -(-row // 16), O_TWO)
    own.scatter()
    x_own = lambda at: xpair[dirn, at].astype(F32) + xprecv[at].astype(F32)
    xlate = Sum(ring, n, seq, dirn, x_own, xtotal, xsend, xrecv, xover, 16, X_TWO)
    x_copy.wait_recv()
    xlate.scatter()
    if E_TWO[0]:
        early.scatter2()
    bsend[...] = dot(dot(turn_t, mixed).astype(B16), woutf[...])
    bb = ring.take(1)
    b_copy = ring.copy(bsend, brecv, bb, bb, sibling)
    b_copy.start()
    ring.sent.append(b_copy)

    @pl.when(place < n - 1)
    def _():
        h_copy.wait_recv()
        gpad[pl.ds(rows, HALO)] = ghrecv[...].astype(F32)

    edge_x = gpad[pl.ds(rows - HALO, HALO)] * cw_r[0, 0:1]
    for k in range(1, 4):
        ok = over_lanes(later[k - 1, pl.ds(rows + k, HALO)])
        edge_x = edge_x + gpad[pl.ds(rows - HALO + k, HALO)] * ok * cw_r[0, k:k + 1]
    gn_edge = dot(edge_x.astype(B16), win_r[:, :inner], 1, 1)
    gn = jnp.concatenate([gn_x[:rows - HALO], gn_edge], axis=0) + gn_z
    scaled = gn * gain_r[...]
    gv = inv * (scaled - vr * jnp.mean(scaled * vr, axis=1, keepdims=True))
    vsend[...] = turned(gv.astype(B16), turn_t).astype(B16)
    bv = ring.take(1)
    v_copy = ring.copy(vsend, vrecv, bv, bv, sibling)
    v_copy.start()
    ring.sent.append(v_copy)
    if not E_TWO[0]:
        early.gather()
    for v, two in ((own, O_TWO), (xlate, X_TWO)):
        if two[0]:
            v.scatter2()
    if E_TWO[0] and (X_TWO[0] or O_TWO[0]):
        early.gather()
    own.gather()
    if E_TWO[0] and not (X_TWO[0] or O_TWO[0]):
        early.gather()
    xlate.gather()
    b_copy.wait_recv()
    out_r[...] = (tok_r[...].astype(F32) + (bsend[...] + brecv[...])).astype(B16)
    v_copy.wait_recv()
    ing_r[...] = cot_r[...].astype(F32) + (vsend[...].astype(F32) + vrecv[...].astype(F32))
    for v, two in ((early, E_TWO), (own, O_TWO), (xlate, X_TWO)):
        if two[1]:
            v.gather1()
    if O_TWO[1]:
        own.back1.wait()
    else:
        own.finish()
    bo = ring.take(1)
    gat = pl.ds(row - 16, 16)
    os_copy = ring.copy(ototal.at[gat], gsib, bo, bo, sibling)
    os_copy.start()
    ring.sent.append(os_copy)
    copies = xlate.mirror(xsib, sibling)
    copies += early.mirror(esib, sibling)
    for c in copies:
        c.wait_recv()
    os_copy.wait_recv()
    done_edges(ring)
    for c in ring.sent:
        c.wait_send()


def finish(sizes, *refs):
    (out_v, ing_v, etotal, esib, xtotal, xsib, ototal, gsib,
     out_h, ing_h, ggain_h, gwin_h, gwout_h, gcw_h, gcb_h, gwx_h, gwdt_h, gbias_h, galog_h, gskip_h,
     ggain, gwin, gwout, gcw, gcb, gwx, gwdt, gbias, galog, gskip, sems) = refs
    nx, ns, state = sizes
    dirn = lax.axis_index("dir")
    width = ing_v.shape[1]
    hw = xtotal.shape[1]
    inner = 2 * hw
    started = []

    def write(src, dst):
        c = pltpu.make_async_copy(src, dst, sems.at[len(started)])
        c.start()
        started.append(c)

    write(out_v, out_h)
    write(ing_v, ing_h)

    def halves(mine, other):
        a, b = mine[...].astype(F32), other[...].astype(F32)
        return jnp.where(dirn == 0, a, b), jnp.where(dirn == 0, b, a)

    gz, go = halves(etotal, esib)
    gwout[pl.ds(0, width)] = go[:, :width]
    gwout[pl.ds(width, width)] = go[:, width:]
    write(gwout, gwout_h)
    gwin[:, inner:] = gz
    left, right = halves(xtotal, xsib)
    gwin[:, :hw] = left
    gwin[:, hw:inner] = right
    write(gwin, gwin_h)
    row = 0
    parts = []
    for k in (nx, ns, state, 8):
        parts.append(jnp.concatenate([ototal[pl.ds(row, k)], ototal[pl.ds(row + k, k)]], axis=1).astype(F32))
        row += 2 * k
    tail = parts[3]
    gwx[0], gwdt[0], galog[0] = parts[:3]
    gcw[0] = tail[0:4]
    gcb[...], gbias[...], gskip[...] = tail[4:5], tail[5:6], tail[6:7]
    both = ototal[pl.ds(row - 16, 16)].astype(F32) + gsib[...].astype(F32)
    ggain[...] = both[7:8, :width]
    for a, b in ((gwx, gwx_h), (gwdt, gwdt_h), (galog, galog_h), (gcw, gcw_h), (gcb, gcb_h),
                 (gbias, gbias_h), (gskip, gskip_h), (ggain, ggain_h)):
        write(a, b)
    for c in started:
        c.wait()


def done_edges(ring):
    for c, cond in ring.edges:
        @pl.when(cond)
        def _():
            c.wait_send()


def on_device(n, tokens, gain, w_in, w_out, conv_w, conv_b, w_x, w_dt, dt_bias, a_log, d_skip, lengths, cotangent):
    rows, width = tokens.shape
    inner = w_out.shape[0]
    state = a_log.shape[1]
    rank = w_dt.shape[1]
    g_in, g_out = log_split(n)
    g3 = max(n // 16, 1)
    hw = inner // 2
    cells = state * inner // LANES
    gain = gain.reshape(1, width)
    w_xt = jnp.swapaxes(w_x, 1, 2)
    nsem = 24 + g_in + g_out + 3 * 32 + 3 * g3
    vm = pltpu.VMEM
    sds = jax.ShapeDtypeStruct
    ins = (tokens, gain, w_in, w_out, conv_w, conv_b, w_xt, w_dt, dt_bias, a_log, d_skip, cotangent)
    def bufs(two, k, lanes):
        if two[0]:
            return [vm((4, 4 * k, lanes), B16), vm((4 * k, lanes), B16), vm((4, k, lanes), B16)]
        return [vm((16, k, lanes), B16)]

    k = width // 16
    scratch = [vm(x.shape, x.dtype) for x in ins] + [
        pltpu.SemaphoreType.DMA((len(ins),)),
        vm((HALO, inner + width), B16), vm((HALO, inner + width), B16),
        vm((rows * state, LANES), B16), vm((rows * state, 2 * LANES), F32),
        vm((rows * state, inner), F32), vm(((rows + 1) * state, inner), F32),
        vm((rows, inner), F32), vm((rows, inner), F32), vm((rows, inner), F32),
        vm((HALO + rows, inner), F32), vm((3, rows, inner), F32), vm((3, rows + 2 * HALO, LANES), F32),
        vm((rows + HALO, inner), F32), vm((2 * HALO, inner), F32),
        vm((HALO, inner), B16), vm((HALO, inner), B16),
        *[vm((rows, inner), F32)] * 5, vm((width, rows + HALO), B16), vm((inner, width), B16),
        vm((g_in, 2 * cells + 16, LANES), B16), vm((2, cells + 16, LANES), B16),
        vm((g_out, cells + 16, LANES), B16),
        vm((rows, inner), F32), vm((rows, inner), F32), vm((rows, inner), F32),
        vm((rows, width), F32), vm((rows, width), F32),
        vm((rows, width), B16), vm((rows, width), B16),
        vm((2, width, inner), B16), vm((width, inner), B16), vm((width, inner), B16), *bufs(E_TWO, k, inner), vm((g3, k, inner), B16),
        vm((2, width, hw), B16), vm((width, hw), B16),
        vm((width, hw), B16), *bufs(X_TWO, k, hw), vm((g3, k, hw), B16),
        vm((256, hw), F32), vm((256, hw), B16), *bufs(O_TWO, 16, hw), vm((g3, 16, hw), B16),
        pltpu.SemaphoreType.DMA((nsem,)), pltpu.SemaphoreType.DMA((nsem,)),
    ]
    mids = [
        vm((rows, width), B16), vm((rows, width), F32), vm((width, inner), B16), vm((width, inner), B16),
        vm((width, hw), B16), vm((width, hw), B16), vm((256, hw), B16), vm((16, hw), B16),
    ]
    in_vmem = pl.BlockSpec(memory_space=pltpu.VMEM)
    in_hbm = pl.BlockSpec(memory_space=pltpu.HBM)
    sums = pl.pallas_call(
        functools.partial(kernel, n, nsem),
        out_shape=mids,
        in_specs=[in_hbm] * len(ins) + [pl.BlockSpec(memory_space=pltpu.SMEM)],
        out_specs=[in_vmem] * len(mids),
        scratch_shapes=scratch,
        compiler_params=pltpu.CompilerParams(
            collective_id=0, has_side_effects=True, vmem_limit_bytes=56 * 2**20
        ),
    )(*ins, lengths)
    outs = (
        sds((rows, width), B16), sds((rows, width), F32), sds((1, width), F32),
        sds(w_in.shape, F32), sds(w_out.shape, F32), sds(conv_w.shape, F32), sds(conv_b.shape, F32),
        sds(w_xt.shape, F32), sds(w_dt.shape, F32), sds(dt_bias.shape, F32), sds(a_log.shape, F32),
        sds(d_skip.shape, F32),
    )
    res = pl.pallas_call(
        functools.partial(finish, (w_xt.shape[1], rank, state)),
        out_shape=outs,
        in_specs=[in_vmem] * len(mids),
        out_specs=[in_hbm] * len(outs),
        scratch_shapes=[vm(x.shape, x.dtype) for x in outs[2:]] + [pltpu.SemaphoreType.DMA((len(outs),))],
        compiler_params=pltpu.CompilerParams(vmem_limit_bytes=8 * 2**20),
    )(*sums)
    return (res[0], res[1], res[2].reshape(width)) + tuple(res[3:7]) + (jnp.swapaxes(res[7], 1, 2),) + tuple(res[8:])


def solution(mesh):
    d1, d2 = P("dir", None), P("dir", None, None)
    return jax.shard_map(
        functools.partial(on_device, mesh.shape["seq"]),
        mesh=mesh,
        in_specs=(P("seq", None), P(), P(), P(), d2, d1, d2, d2, d1, d2, d1, P(), P("seq", None)),
        out_specs=(P("seq", None), P("seq", None), P(), P(), P(), d2, d1, d2, d2, d1, d2, d1),
        check_vma=False,
    )
```

```python
import functools

import jax
import jax.numpy as jnp
from jax import lax
from jax.experimental import pallas as pl
from jax.experimental.pallas import tpu as pltpu
from jax.sharding import PartitionSpec as P

F32 = jnp.float32
B16 = jnp.bfloat16
MESH = pl.DeviceIdType.MESH
NORM_EPS = 1e-05
LOG2E = 1.4426950408889634
RESET = 1e6
HALO = 16
LANES = 128
E_TWO, X_TWO, O_TWO = (True, True, False), (True, False, False), (True, True, True)


def dot(a, b, ca=1, cb=0):
    return lax.dot_general(a, b, (((ca,), (cb,)), ((), ())), preferred_element_type=F32)


def silu_grad(v, sigma):
    return sigma * (1.0 + v * (1.0 - sigma))


def softplus(v):
    u = jnp.exp(-jnp.abs(v))
    s = u / (2.0 + u)
    q = s * s
    p = 1.0 / 13.0
    for k in (11.0, 9.0, 7.0, 5.0, 3.0):
        p = p * q + 1.0 / k
    return jnp.maximum(v, 0.0) + 2.0 * s * (p * q + 1.0)


def log_split(n):
    inner = 1
    while inner * inner * 4 <= n:
        inner *= 2
    return inner, n // inner


class Ring:
    def __init__(self, ssem, rsem, size):
        self.ssem, self.rsem, self.next, self.size = ssem, rsem, 0, size
        self.sent, self.edges = [], []

    def take(self, count):
        base = self.next
        self.next += count
        assert self.next <= self.size
        return base

    def copy(self, src, dst, s, r, dev):
        return pltpu.make_async_remote_copy(
            src_ref=src, dst_ref=dst, send_sem=self.ssem.at[s], recv_sem=self.rsem.at[r],
            device_id=dev, device_id_type=MESH,
        )


class Exchange:
    def __init__(self, ring, size, me, dev):
        self.ring, self.size, self.me, self.dev = ring, size, me, dev
        self.base = ring.take(size)

    def start(self, src, dst):
        self.src, self.dst = src, dst
        for r in range(1, self.size):
            peer = lax.rem(self.me + r, self.size)
            c = self.ring.copy(src(peer), dst(self.me), self.base + r, self.base + self.me, self.dev(peer))
            c.start()
            self.ring.sent.append(c)

    def wait_one(self, r):
        peer = lax.rem(self.me + r, self.size)
        self.ring.copy(
            self.src(peer), self.dst(peer), self.base + r, self.base + peer, self.dev(peer)
        ).wait_recv()

    def wait(self):
        for r in range(1, self.size):
            self.wait_one(r)


def flip(a, mask):
    for b in range(4):
        if mask >> b & 1:
            a = a + (1 << b) * (1 - 2 * lax.rem(a // (1 << b), 2))
    return a


class Sum:
    def __init__(self, ring, n, seq, dirn, own, total, send, recv, over, blocks, two):
        self.ring, self.own, self.total, self.send, self.over = ring, own, total, send, over
        self.blocks, self.k, self.g3 = blocks, total.shape[0] // 16, n // 16
        self.me, hi = lax.rem(seq, 16), seq // 16
        self.hi = hi
        base = seq - self.me
        self.dev = lambda p: (dirn, base + p)
        self.lo, self.mid = lax.rem(self.me, 4), self.me // 4
        self.peers = [flip(self.me, m) for m in range(15, 0, -1)]
        self.out_two, self.back_two, self.far_first = two
        near = lambda p: self.dev(self.me - lax.rem(self.me, 4) + p)
        far = lambda p: self.dev(p * 4 + lax.rem(self.me, 4))
        if self.far_first:
            near, far, self.lo, self.mid = far, near, self.mid, self.lo
        if self.out_two:
            self.recv, self.send2, self.recv2 = recv
            self.ex1, self.ex2 = Exchange(ring, 4, self.lo, near), Exchange(ring, 4, self.mid, far)
        else:
            (self.recv,) = recv
            self.s1 = ring.take(16)
        if self.back_two:
            self.back2, self.back1 = Exchange(ring, 4, self.mid, far), Exchange(ring, 4, self.lo, near)
        else:
            self.s2 = ring.take(16)
        self.top = Exchange(ring, self.g3, hi, lambda p: (dirn, seq + (p - hi) * 16)) if self.g3 > 1 else None

    def block(self, p):
        if (self.out_two or self.back_two) and not self.far_first:
            return lax.rem(p, 4) * 4 + p // 4
        return p if self.blocks == 16 else lax.rem(p + 12, 16)

    def at(self, b, count=1):
        size = self.k * count
        return pl.ds(pl.multiple_of(b * size, size), size)

    def owns(self, p, body):
        if self.blocks < 16:
            pl.when(self.block(p) < self.blocks)(body)
        else:
            body()

    def go(self, c, owner):
        self.owns(owner, c.start)
        if self.blocks < 16:
            self.ring.edges.append((c, self.block(owner) < self.blocks))
        else:
            self.ring.sent.append(c)

    def scatter(self):
        self.send[...] = self.own(slice(None)).astype(B16)
        if self.out_two:
            self.ex1.start(lambda p: self.send.at[self.at(p, 4)], lambda s: self.recv.at[s])
            return
        for r, p in enumerate(self.peers):
            src = self.send.at[self.at(self.block(p))]
            self.go(self.ring.copy(src, self.recv.at[self.me], self.s1 + r, self.s1 + self.me, self.dev(p)), p)

    def scatter2(self):
        self.recv[self.lo] = jnp.zeros(self.recv.shape[1:], B16)
        self.ex1.wait()
        acc = self.own(self.at(self.lo, 4))
        for j in range(4):
            acc = acc + self.recv[j].astype(F32)
        self.send2[...] = acc.astype(B16)
        self.ex2.start(lambda p: self.send2.at[self.at(p)], lambda s: self.recv2.at[s])

    def add(self):
        if self.out_two:
            self.recv2[self.mid] = jnp.zeros(self.recv2.shape[1:], B16)
            self.ex2.wait()
            parts, count = self.recv2, 4
            acc = self.send2[self.at(self.mid)].astype(F32)
        else:
            self.recv[self.me] = jnp.zeros(self.recv.shape[1:], B16)
            for r, p in reversed(list(enumerate(self.peers))):
                there = self.send.at[pl.ds(0, self.k)]
                self.ring.copy(there, self.recv.at[p], self.s1 + r, self.s1 + p, self.dev(p)).wait_recv()
            parts, count = self.recv, 16
            acc = self.own(self.at(self.block(self.me)))
        for j in range(count):
            acc = acc + parts[j].astype(F32)
        if self.top is not None:
            self.over[self.hi] = acc.astype(B16)
            self.top.start(lambda p: self.over.at[self.hi], lambda s: self.over.at[s])
            self.top.wait()
            for _ in range(1, self.g3):
                self.ring.sent.pop().wait_send()
            acc = self.over[0].astype(F32)
            for j in range(1, self.g3):
                acc = acc + self.over[j].astype(F32)
        self.total[self.at(self.block(self.me))] = acc.astype(B16)

    def gather(self):
        self.owns(self.me, self.add)
        mine = self.total.at[self.at(self.block(self.me))]
        if self.back_two:
            there = lambda s: self.total.at[self.at(self.lo * 4 + s)]
            self.back2.start(lambda p: there(self.mid), there)
            return
        for r, p in enumerate(self.peers):
            self.go(self.ring.copy(mine, mine, self.s2 + r, self.s2 + self.me, self.dev(p)), self.me)

    def gather1(self):
        self.back2.wait()
        there = lambda s: self.total.at[self.at(s, 4)]
        self.back1.start(lambda p: there(self.lo), there)

    def took(self, p):
        there = self.total.at[self.at(self.block(p))]
        self.owns(p, self.ring.copy(there, there, self.s2, self.s2 + p, self.dev(p)).wait_recv)

    def finish(self):
        for p in reversed(self.peers):
            self.took(p)

    def mirror(self, other, sibling):
        copies = []

        def on(quarter):
            s = self.ring.take(1)
            rows = self.at(quarter, 4)
            c = self.ring.copy(self.total.at[rows], other.at[rows], s, s, sibling)
            c.start()
            self.ring.sent.append(c)
            copies.append(c)

        if self.back_two:
            for r in range(4):
                p = lax.rem(self.lo + r, 4)
                if r > 0:
                    self.back1.wait_one(r)
                on(p)
        else:
            by_lo = self.out_two and not self.far_first
            for r in range(4):
                quarter = lax.rem((self.lo if by_lo else self.mid) + r, 4)
                for x in range(4):
                    other_at = lax.rem((self.mid if by_lo else self.lo) + x, 4)
                    p = other_at * 4 + quarter if by_lo else quarter * 4 + other_at
                    if r + x > 0:
                        self.took(p)
                on(quarter)
        return copies


def kernel(n, nsem, *refs):
    (tok_h, gain_h, win_h, wout_h, cw_h, cb_h, wx_h, wdt_h, bias_h, alog_h, skip_h, cot_h, len_r,
     out_r, ing_r, etotal, esib, xtotal, xsib, ototal, gsib,
     tok_r, gain_r, win_r, wout_r, cw_r, cb_r, wx_r, wdt_r, bias_r, alog_r, skip_r, cot_r, lsem,
     tail_s, halo, picked, bcr, dref, cpr, hs, pr, sdr, sar, gyr, xpad, taps, later, gpad, gext, ghsend, ghrecv,
     sgr, cgr, zgr, gsr, skr, gyq, yl, ntx, woutf,
     xin1, xsend2, xin2, yr, adjr, dtar, bsend, brecv, vsend, vrecv,
     epair, eprecv, esend, *rest) = refs
    erecv, rest = rest[:3 if E_TWO[0] else 1], rest[3 if E_TWO[0] else 1:]
    eover, xpair, xprecv, xsend, *rest = rest
    xrecv, rest = rest[:3 if X_TWO[0] else 1], rest[3 if X_TWO[0] else 1:]
    xover, opart, osend, *rest = rest
    orecv, rest = rest[:3 if O_TWO[0] else 1], rest[3 if O_TWO[0] else 1:]
    oover, ssem, rsem = rest
    rows, width = tok_r.shape
    inner = wout_r.shape[0]
    state = alog_r.shape[1]
    chunks = inner // LANES
    dirn = lax.axis_index("dir")
    seq = lax.axis_index("seq")
    place = seq + dirn * (n - 1 - 2 * seq)
    seq_at = lambda p: p + dirn * (n - 1 - 2 * p)
    dev_at = lambda p: (dirn, seq_at(p))
    sibling = (1 - dirn, seq)
    g_in, g_out = log_split(n)
    lo = lax.rem(place, g_in)
    hi = place // g_in
    ring = Ring(ssem, rsem, nsem)
    up = lax.rem(place + 1, n)
    down = lax.rem(place + n - 1, n)

    barrier = pltpu.get_barrier_semaphore()
    line, s_hi = lax.rem(seq, 16), seq // 16
    peers = [sibling, dev_at(up), dev_at(down)]
    if all(E_TWO[:2] + X_TWO[:2] + O_TWO[:2]):
        near, far = lax.rem(line, 4), line // 4
        peers += [(dirn, seq - near + lax.rem(near + r, 4)) for r in range(1, 4)]
        peers += [(dirn, seq + (lax.rem(far + r, 4) - far) * 4) for r in range(1, 4)]
    else:
        peers += [(dirn, seq - line + lax.rem(line + r, 16)) for r in range(1, 16)]
    if n != 16:
        peers += [(dirn, seq + (lax.rem(s_hi + r, n // 16) - s_hi) * 16) for r in range(1, n // 16)]
        peers += [dev_at(hi * g_in + lax.rem(lo + r, g_in)) for r in range(1, g_in)]
        peers += [dev_at(lax.rem(hi + r, g_out) * g_in + lo) for r in range(1, g_out)]
    for dev in peers:
        pl.semaphore_signal(barrier, inc=1, device_id=dev, device_id_type=MESH)

    loads = {}
    pairs = [(tok_h, tok_r), (gain_h, gain_r), (win_h, win_r), (cot_h, cot_r), (wout_h, wout_r), (cw_h, cw_r),
             (cb_h, cb_r), (wx_h, wx_r), (wdt_h, wdt_r), (bias_h, bias_r), (alog_h, alog_r), (skip_h, skip_r)]
    for i, (a, b) in enumerate(pairs):
        loads[i] = pltpu.make_async_copy(a, b, lsem.at[i])
        loads[i].start()

    def turn(size):
        r = lax.broadcasted_iota(jnp.int32, (size, size), 0)
        c = lax.broadcasted_iota(jnp.int32, (size, size), 1)
        return jnp.where(c == r + dirn * (size - 1 - 2 * r), 1.0, 0.0).astype(B16)

    turn_t, turn_f = turn(rows), turn(width)
    turned = lambda v, tt: dot(dot(tt, v).astype(B16), turn_f)

    total = n * rows
    q = lax.broadcasted_iota(jnp.int32, (rows + 2 * HALO, LANES), 0) + (place * rows - HALO)
    dist = jnp.full(q.shape, 1 << 30, jnp.int32)
    before = jnp.int32(0)
    for w in range(len_r.shape[0]):
        after = before + len_r[w]
        delta = q - (before + dirn * (total - after - before))
        dist = jnp.where((delta >= 0) & (delta < dist), delta, dist)
        before = after
    over_lanes = lambda v: jnp.concatenate([v] * (inner // v.shape[1]), axis=1)
    for k in range(1, 4):
        later[k - 1] = jnp.where((dist >= k) & (q < total), 1.0, 0.0)
    dist_own = over_lanes(dist[HALO:HALO + rows])

    def normalise(v):
        inv = lax.rsqrt(jnp.mean(v * v, axis=1, keepdims=True) + NORM_EPS)
        vr = v * inv
        return inv, vr, (vr * gain_r[...]).astype(B16)

    for i in range(3):
        loads[i].wait()
    tok = turned(tok_r[...], turn_t)
    inv, vr, normed = normalise(tok)
    proj = dot(normed, win_r[...])
    xi_b = proj[:, :inner].astype(B16)
    xi = xi_b.astype(F32)
    zgate = proj[:, inner:]
    xpad[pl.ds(0, HALO)] = jnp.zeros((HALO, inner), F32)
    xpad[pl.ds(HALO, rows)] = xi
    tail_s[:, :inner] = xi_b[rows - HALO:]
    tail_s[:, inner:] = tok[rows - HALO:].astype(B16)

    pl.semaphore_wait(barrier, len(peers))
    b0 = ring.take(1)
    tok_copy = ring.copy(tail_s, halo, b0, b0, dev_at(up))
    ring.edges.append((tok_copy, place < n - 1))

    @pl.when(place < n - 1)
    def _():
        tok_copy.start()

    @pl.when(place == 0)
    def _():
        halo[...] = jnp.zeros(halo.shape, B16)

    for i in range(3, len(pairs)):
        loads[i].wait()
    cot = turned(cot_r[...], turn_t).astype(B16)
    sig_z = jax.nn.sigmoid(zgate)
    gate = zgate * sig_z
    gmix = dot(cot, wout_r[...], 1, 1)
    gy = gmix * gate
    gyr[...] = gy
    rate = -jnp.exp(alog_r[0])
    rate2 = rate * LOG2E
    cut = lambda v: [v[:, c * LANES:(c + 1) * LANES] for c in range(chunks)]
    a2 = cut(rate2)
    a1 = cut(rate)

    def drive(count):
        conv = xpad[pl.ds(HALO, count)] * cw_r[0, 0:1] + cb_r[...]
        for k in range(1, 4):
            tap = jnp.where(dist_own[:count] >= k, xpad[pl.ds(HALO - k, count)], 0.0)
            conv = conv + tap * cw_r[0, k:k + 1]
        sig_c = jax.nn.sigmoid(conv)
        act_b = (conv * sig_c).astype(B16)
        low_t = dot(wx_r[0, pl.ds(0, state)], act_b, 1, 1).astype(B16)
        bc = dot(act_b, wx_r[0, pl.ds(state, 2 * state)], 1, 1)
        pre = dot(low_t, wdt_r[0], 0, 0) + bias_r[...]
        step = softplus(pre)
        sd = jnp.where(dist_own[:count] == 0, RESET, step)
        sdr[pl.ds(0, count)] = sd
        sar[pl.ds(0, count)] = step * act_b.astype(F32)
        return conv, sig_c, act_b, low_t, pre, step, sd, bc

    wide = 2 * state
    lane_k = lax.broadcasted_iota(jnp.int32, (state, LANES), 1)
    row_k = lax.broadcasted_iota(jnp.int32, (state, LANES), 0)
    own_k = jnp.where((lane_k < 2 * wide) & (lax.rem(lane_k, state) == row_k), 1.0, 0.0)
    fan_r = lax.rem(lax.broadcasted_iota(jnp.int32, (LANES, 2 * LANES), 0), wide) // state
    fan_c = lax.broadcasted_iota(jnp.int32, (LANES, 2 * LANES), 1) // LANES
    fan = jnp.where(fan_r == fan_c, 1.0, 0.0).astype(B16)

    def spread(bc, first):
        count = bc.shape[0]
        top = bc.astype(B16).astype(F32)
        none = jnp.zeros((count, LANES - 2 * wide), F32)
        both = jnp.concatenate([top, bc - top, none], axis=1)
        for t in range(count):
            picked[pl.ds((first + t) * state, state)] = (both[t:t + 1] * own_k).astype(B16)
        at = pl.ds(first * state, count * state)
        bcr[at] = dot(picked[at], fan)

    def summarise(g, carry):
        h, p, l = [list(x) for x in carry]
        at8 = pl.ds(pl.multiple_of(g * 8, 8), 8)
        sd8, sa8, gy8 = sdr[at8], sar[at8], gyr[at8]
        for c in range(chunks):
            lane = slice(c * LANES, (c + 1) * LANES)
            for j in range(8):
                at = pl.ds(pl.multiple_of((g * 8 + j) * state, state), state)
                br, cr = bcr[at, :LANES], bcr[at, LANES:]
                d = jnp.exp2(sd8[j:j + 1, lane] * a2[c])
                dref[at, lane] = d
                h[c] = d * h[c] + sa8[j:j + 1, lane] * br
                p[c] = p[c] * d
                l[c] = l[c] + p[c] * (gy8[j:j + 1, lane] * cr)
        return tuple(h), tuple(p), tuple(l)

    zero = tuple(jnp.zeros((state, LANES), F32) for _ in range(chunks))
    one = tuple(jnp.ones((state, LANES), F32) for _ in range(chunks))
    join = lambda v: jnp.concatenate(v, axis=1)
    head = HALO // 8

    whole = drive(rows)
    spread(whole[7][HALO:], HALO)
    h_late, p_late, l_late = lax.fori_loop(head, rows // 8, summarise, (zero, one, zero), unroll=2)

    @pl.when(place > 0)
    def _():
        tok_copy.wait_recv()

    xpad[pl.ds(0, HALO)] = halo[:, :inner].astype(F32)
    start = drive(HALO)
    low_first = jnp.concatenate([start[3].astype(F32), jnp.zeros((state, rows - HALO), F32)], axis=1)
    lane_low = lax.broadcasted_iota(jnp.int32, low_first.shape, 1)
    dt_low = jnp.where(lane_low < HALO, low_first, whole[3].astype(F32)).astype(B16)
    patch = lambda i: jnp.concatenate([start[i], whole[i][HALO:]], axis=0)
    conv, sig_c, act_b, pre, step, sd = [patch(i) for i in (0, 1, 2, 4, 5, 6)]
    act = act_b.astype(F32)
    spread(start[7], 0)
    h_first, p_first, l_first = lax.fori_loop(0, head, summarise, (zero, one, zero), unroll=2)
    h_sum = join(h_late) + join(p_late) * join(h_first)
    l_sum = join(l_first) + join(p_first) * join(l_late)

    def pair_rows(v):
        top = v.astype(B16).astype(F32)
        both = cut(top) + cut(v - top) + [jnp.zeros((16 - 2 * chunks, LANES), F32)]
        return jnp.concatenate(both, axis=0).astype(B16)

    blk_s = chunks * state
    stack = lambda v: jnp.concatenate(cut(v), axis=0).astype(B16)
    unstack = lambda v, at: join([v[at + c * state:at + (c + 1) * state].astype(F32) for c in range(chunks)])
    def unpair1(v):
        r = v[blk_s:blk_s + 16].astype(F32)
        return join([r[c:c + 1] + r[chunks + c:chunks + c + 1] for c in range(chunks)])
    xin1[lo, pl.ds(0, blk_s)] = stack(h_sum)
    xin1[lo, pl.ds(blk_s, 16)] = pair_rows(jnp.sum(sd, axis=0, keepdims=True))
    xin1[lo, pl.ds(blk_s + 16, blk_s)] = stack(l_sum)
    ex1 = Exchange(ring, g_in, lo, lambda p: dev_at(hi * g_in + p))
    ex1.start(lambda p: xin1.at[lo], lambda s: xin1.at[s])

    sub = lax.broadcasted_iota(jnp.int32, (8, LANES), 0)
    lane_at = lax.broadcasted_iota(jnp.int32, (state, LANES), 1)

    def sum_rows(v):
        for bit in (1, 2, 4):
            mine = lax.rem(sub // bit, 2) == 0
            v = [
                jnp.where(mine, a, b) + pltpu.roll(jnp.where(mine, b, a), bit, 0)
                for a, b in zip(v[::2], v[1::2])
            ]
        return v[0]

    halve = lambda v: v[:8] + v[8:]
    hs[pl.ds(0, state)] = jnp.zeros((state, inner), F32)
    pr[pl.ds(0, state)] = jnp.ones((state, inner), F32)

    def prepare(g, carry):
        h, p = list(carry[0]), list(carry[1])
        at8 = pl.ds(pl.multiple_of(g * 8, 8), 8)
        sa8 = sar[at8]
        for c in range(chunks):
            lane = slice(c * LANES, (c + 1) * LANES)
            ys = []
            for j in range(8):
                at = pl.ds(pl.multiple_of((g * 8 + j) * state, state), state)
                nxt = pl.ds(pl.multiple_of((g * 8 + j + 1) * state, state), state)
                d, cr = dref[at, lane], bcr[at, LANES:]
                h[c] = d * h[c] + sa8[j:j + 1, lane] * bcr[at, :LANES]
                p[c] = p[c] * d
                hs[nxt, lane] = h[c]
                pr[nxt, lane] = p[c]
                cpr[at, lane] = p[c] * cr
                ys.append(halve(h[c] * cr))
            yl[at8, lane] = sum_rows(ys)
        return tuple(h), tuple(p)

    lax.fori_loop(0, rows // 8, prepare, (zero, one), unroll=2)

    ex1.wait()
    sums = [unpair1(xin1[j]) for j in range(g_in)]
    fwd = bwd = fwd_all = bwd_all = jnp.zeros((state, inner), F32)
    s_fwd = s_bwd = s_all = jnp.zeros((1, inner), F32)
    for j in range(g_in):
        fade = jnp.exp2(rate2 * sums[j])
        fwd_all = fade * fwd_all + unstack(xin1[j], 0)
        fwd = jnp.where(j < lo, fwd_all, fwd)
        s_all = s_all + sums[j]
        s_fwd = jnp.where(j < lo, s_all, s_fwd)
    for j in reversed(range(g_in)):
        fade = jnp.exp2(rate2 * sums[j])
        bwd_all = fade * bwd_all + unstack(xin1[j], blk_s + 16)
        bwd = jnp.where(j > lo, bwd_all, bwd)
        s_bwd = jnp.where(j > lo, s_bwd + sums[j], s_bwd)
    s_pair = pair_rows(s_all)
    for k, v in enumerate((fwd_all, bwd_all)):
        xsend2[k, pl.ds(0, blk_s)] = stack(v)
        xsend2[k, pl.ds(blk_s, 16)] = s_pair
    xin2[hi] = jnp.zeros(xin2.shape[1:], B16)
    ex2 = Exchange(ring, g_out, hi, lambda p: dev_at(p * g_in + lo))
    ex2.start(lambda p: xsend2.at[jnp.where(p > hi, 0, 1)], lambda s: xin2.at[s])
    _, vr_h, normed_h = normalise(halo[:, inner:].astype(F32))
    for k in range(1, 4):
        taps[k - 1] = jnp.where(dist_own >= k, xpad[pl.ds(HALO - k, rows)], 0.0)
    ntx[...] = jnp.concatenate([normed, normed_h], axis=0).T
    sgr[...] = jax.nn.sigmoid(pre)
    cgr[...] = silu_grad(conv, sig_c)
    zgr[...] = gmix * silu_grad(zgate, sig_z)
    gsr[...] = gy * skip_r[...]
    skr[...] = skip_r[...] * act
    woutf[...] = dot(wout_r[...], turn_f).astype(B16)
    gskip = jnp.sum(gy * act, axis=0, keepdims=True)
    gpad[pl.ds(0, 8)] = jnp.zeros((8, inner), F32)
    gpad[pl.ds(8, rows)] = gy
    gyq[...] = gpad[pl.ds(7, rows)]

    ex2.wait()
    h_in = l_in = jnp.zeros((state, inner), F32)
    for k in range(g_out):
        new = jnp.exp2(rate2 * unpair1(xin2[k])) * h_in
        h_in = jnp.where(k < hi, new + unstack(xin2[k], 0), h_in)
    for k in reversed(range(g_out)):
        new = jnp.exp2(rate2 * unpair1(xin2[k])) * l_in
        l_in = jnp.where(k > hi, new + unstack(xin2[k], 0), l_in)
    h_in = jnp.exp2(rate2 * s_fwd) * h_in + fwd
    l_in = jnp.exp2(rate2 * s_bwd) * l_in + bwd

    hin = cut(h_in)

    def forward(g, carry):
        at8 = pl.ds(pl.multiple_of(g * 8, 8), 8)
        for c in range(chunks):
            lane = slice(c * LANES, (c + 1) * LANES)
            ys = []
            for j in range(8):
                at = pl.ds(pl.multiple_of((g * 8 + j) * state, state), state)
                ys.append(halve(cpr[at, lane] * hin[c]))
            yr[at8, lane] = yl[at8, lane] + sum_rows(ys)
        return carry

    lax.fori_loop(0, rows // 8, forward, 0, unroll=4)
    none = jnp.zeros((state, rows), F32)
    y = yr[...] + skr[...]
    mixed = (y * gate).astype(B16)
    gz = (zgr[...] * y).astype(B16)

    epair[0] = dot(ntx[:, :rows], gz).astype(B16)
    gwo = dot(mixed, cot, 0, 0).astype(B16)
    epair[1, :, :width] = gwo[:width]
    epair[1, :, width:] = gwo[width:]
    be = ring.take(1)
    e_copy = ring.copy(epair.at[1 - dirn], eprecv, be, be, sibling)
    e_copy.start()
    ring.sent.append(e_copy)

    def backward(i, carry):
        m, acc, gb, gc = list(carry[0]), list(carry[1]), carry[2], carry[3]
        g = rows // 8 - 1 - i
        at8 = pl.ds(pl.multiple_of(g * 8, 8), 8)
        sd8, gy8, sa8, gq8 = sdr[at8], gyr[at8], sar[at8], gyq[at8]
        over_b, over_c = [None] * 8, [None] * 8
        for c in range(chunks):
            lane = slice(c * LANES, (c + 1) * LANES)
            adjs, dts = [None] * 8, [None] * 8
            for j in reversed(range(8)):
                at = pl.ds(pl.multiple_of((g * 8 + j) * state, state), state)
                lam = m[c] + gy8[j:j + 1, lane] * bcr[at, LANES:]
                m[c] = dref[at, lane] * lam
                h = hs[at, lane] + pr[at, lane] * hin[c]
                r = m[c] * h * a1[c]
                acc[c] = acc[c] + r * sd8[j:j + 1, lane]
                adjs[j] = halve(lam * bcr[at, :LANES])
                dts[j] = halve(r)
                new_b, new_c = lam * sa8[j:j + 1, lane], h * gq8[j:j + 1, lane]
                over_b[j] = new_b if c == 0 else over_b[j] + new_b
                over_c[j] = new_c if c == 0 else over_c[j] + new_c
            adjr[at8, lane] = sum_rows(adjs)
            dtar[at8, lane] = sum_rows(dts)
        for j in range(8):
            t = g * 8 + j
            gb = jnp.where(lane_at == t, jnp.sum(over_b[j], axis=1, keepdims=True), gb)
            gc = jnp.where(lane_at == t - 1, jnp.sum(over_c[j], axis=1, keepdims=True), gc)
        return tuple(m), tuple(acc), gb, gc

    h_out = hs[pl.ds(rows * state, state)] + pr[pl.ds(rows * state, state)] * h_in
    g_last = jnp.sum(h_out * gyr[pl.ds(rows - 1, 1)], axis=1, keepdims=True)
    none_c = jnp.where(lane_at == rows - 1, g_last, none)
    carry = lax.fori_loop(0, 6, backward, (tuple(cut(l_in)), zero, none, none_c), unroll=6)
    e_own = lambda at: epair[dirn, at].astype(F32) + eprecv[at].astype(F32)
    early = Sum(ring, n, seq, dirn, e_own, etotal, esend, erecv, eover, 16, E_TWO)
    e_copy.wait_recv()
    early.scatter()
    _, galog, g_b, g_c = lax.fori_loop(6, rows // 8, backward, carry, unroll=5)
    galog = join(galog)
    adj = adjr[...]
    gpre = (dtar[...] + adj * act) * sgr[...]
    gbias = jnp.sum(gpre, axis=0, keepdims=True)
    gpre = gpre.astype(B16)
    glow = dot(gpre, wdt_r[0], 1, 1).astype(B16)
    gbc = jnp.concatenate([g_b, g_c], axis=0).astype(B16)
    gact = gsr[...] + adj * step + dot(gbc, wx_r[0, pl.ds(state, 2 * state)], 0, 0)
    gact = gact + dot(glow, wx_r[0, pl.ds(0, state)])
    gconv_b = (gact * cgr[...]).astype(B16)
    gconv = gconv_b.astype(F32)

    gpad[pl.ds(0, rows)] = gconv
    gpad[pl.ds(rows, HALO)] = jnp.zeros((HALO, inner), F32)
    gext[pl.ds(0, HALO)] = jnp.zeros((HALO, inner), F32)
    gext[pl.ds(HALO, HALO)] = gconv[:HALO]
    gxi = gconv * cw_r[0, 0:1]
    gxe = jnp.zeros((HALO, inner), F32)
    for k in range(1, 4):
        w = cw_r[0, k:k + 1]
        gxi = gxi + gpad[pl.ds(k, rows)] * over_lanes(later[k - 1, pl.ds(HALO + k, rows)]) * w
        gxe = gxe + gext[pl.ds(k, HALO)] * over_lanes(later[k - 1, pl.ds(k, HALO)]) * w
    gxi_b = jnp.concatenate([gxi, gxe], axis=0).astype(B16)
    gwx_half = dot(ntx[...], gxi_b).astype(B16)
    hw = inner // 2
    xpair[0] = gwx_half[:, :hw]
    xpair[1] = gwx_half[:, hw:]
    bx = ring.take(1)
    x_copy = ring.copy(xpair.at[1 - dirn], xprecv, bx, bx, sibling)
    x_copy.start()
    ring.sent.append(x_copy)
    ghsend[...] = gconv_b[:HALO]
    bh = ring.take(1)
    h_copy = ring.copy(ghsend, ghrecv, bh, bh, dev_at(down))
    ring.edges.append((h_copy, place > 0))

    @pl.when(place > 0)
    def _():
        h_copy.start()

    gwx_t = jnp.concatenate([dot(glow, act_b, 0, 0), dot(gbc, act_b)], axis=0)
    gwdt = dot(dt_low, gpre)
    gn_x = dot(gxi_b, win_r[:, :inner], 1, 1)
    gn_z = dot(gz, win_r[:, inner:], 1, 1)
    ggain = jnp.sum((gn_x[:rows] + gn_z) * vr, axis=0, keepdims=True)
    ggain = ggain + jnp.sum(gn_x[rows:] * vr_h, axis=0, keepdims=True)
    gcb = jnp.sum(gconv, axis=0, keepdims=True)
    gcw = [jnp.sum(gconv * (xi if k == 0 else taps[k - 1]), axis=0, keepdims=True) for k in range(4)]
    pad_gain = jnp.concatenate([ggain, jnp.zeros((1, inner - width), F32)], axis=1)
    tail = jnp.concatenate(gcw + [gcb, gbias, gskip, pad_gain], axis=0)
    row = 0
    for part in (gwx_t, gwdt, galog, tail):
        k = part.shape[0]
        opart[pl.ds(row, k)] = part[:, :hw]
        opart[pl.ds(row + k, k)] = part[:, hw:]
        row += 2 * k
    opart[pl.ds(row, opart.shape[0] - row)] = jnp.zeros((opart.shape[0] - row, hw), F32)
    own = Sum(ring, n, seq, dirn, lambda at: opart[at], ototal, osend, orecv, oover, 16 if any(O_TWO[:2]) else -(-row // 16), O_TWO)
    own.scatter()
    x_own = lambda at: xpair[dirn, at].astype(F32) + xprecv[at].astype(F32)
    xlate = Sum(ring, n, seq, dirn, x_own, xtotal, xsend, xrecv, xover, 16, X_TWO)
    x_copy.wait_recv()
    xlate.scatter()
    if E_TWO[0]:
        early.scatter2()
    for v, two in ((own, O_TWO), (xlate, X_TWO)):
        if two[0]:
            v.scatter2()
    bsend[...] = dot(dot(turn_t, mixed).astype(B16), woutf[...])
    bb = ring.take(1)
    b_copy = ring.copy(bsend, brecv, bb, bb, sibling)
    b_copy.start()
    ring.sent.append(b_copy)

    early.gather()

    @pl.when(place < n - 1)
    def _():
        h_copy.wait_recv()
        gpad[pl.ds(rows, HALO)] = ghrecv[...].astype(F32)

    edge_x = gpad[pl.ds(rows - HALO, HALO)] * cw_r[0, 0:1]
    for k in range(1, 4):
        ok = over_lanes(later[k - 1, pl.ds(rows + k, HALO)])
        edge_x = edge_x + gpad[pl.ds(rows - HALO + k, HALO)] * ok * cw_r[0, k:k + 1]
    gn_edge = dot(edge_x.astype(B16), win_r[:, :inner], 1, 1)
    gn = jnp.concatenate([gn_x[:rows - HALO], gn_edge], axis=0) + gn_z
    scaled = gn * gain_r[...]
    gv = inv * (scaled - vr * jnp.mean(scaled * vr, axis=1, keepdims=True))
    vsend[...] = turned(gv.astype(B16), turn_t).astype(B16)
    bv = ring.take(1)
    v_copy = ring.copy(vsend, vrecv, bv, bv, sibling)
    v_copy.start()
    ring.sent.append(v_copy)

    own.gather()
    xlate.gather()
    b_copy.wait_recv()
    out_r[...] = (tok_r[...].astype(F32) + (bsend[...] + brecv[...])).astype(B16)
    v_copy.wait_recv()
    ing_r[...] = cot_r[...].astype(F32) + (vsend[...].astype(F32) + vrecv[...].astype(F32))
    for v, two in ((early, E_TWO), (own, O_TWO), (xlate, X_TWO)):
        if two[1]:
            v.gather1()
    if O_TWO[1]:
        own.back1.wait()
    else:
        own.finish()
    bo = ring.take(1)
    gat = pl.ds(row - 16, 16)
    os_copy = ring.copy(ototal.at[gat], gsib, bo, bo, sibling)
    os_copy.start()
    ring.sent.append(os_copy)
    copies = xlate.mirror(xsib, sibling)
    copies += early.mirror(esib, sibling)
    for c in copies:
        c.wait_recv()
    os_copy.wait_recv()
    done_edges(ring)
    for c in ring.sent:
        c.wait_send()


def finish(sizes, *refs):
    (out_v, ing_v, etotal, esib, xtotal, xsib, ototal, gsib,
     out_h, ing_h, ggain_h, gwin_h, gwout_h, gcw_h, gcb_h, gwx_h, gwdt_h, gbias_h, galog_h, gskip_h,
     ggain, gwin, gwout, gcw, gcb, gwx, gwdt, gbias, galog, gskip, sems) = refs
    nx, ns, state = sizes
    dirn = lax.axis_index("dir")
    width = ing_v.shape[1]
    hw = xtotal.shape[1]
    inner = 2 * hw
    started = []

    def write(src, dst):
        c = pltpu.make_async_copy(src, dst, sems.at[len(started)])
        c.start()
        started.append(c)

    write(out_v, out_h)
    write(ing_v, ing_h)

    def halves(mine, other):
        a, b = mine[...].astype(F32), other[...].astype(F32)
        return jnp.where(dirn == 0, a, b), jnp.where(dirn == 0, b, a)

    gz, go = halves(etotal, esib)
    gwout[pl.ds(0, width)] = go[:, :width]
    gwout[pl.ds(width, width)] = go[:, width:]
    write(gwout, gwout_h)
    gwin[:, inner:] = gz
    left, right = halves(xtotal, xsib)
    gwin[:, :hw] = left
    gwin[:, hw:inner] = right
    write(gwin, gwin_h)
    row = 0
    parts = []
    for k in (nx, ns, state, 8):
        parts.append(jnp.concatenate([ototal[pl.ds(row, k)], ototal[pl.ds(row + k, k)]], axis=1).astype(F32))
        row += 2 * k
    tail = parts[3]
    gwx[0], gwdt[0], galog[0] = parts[:3]
    gcw[0] = tail[0:4]
    gcb[...], gbias[...], gskip[...] = tail[4:5], tail[5:6], tail[6:7]
    both = ototal[pl.ds(row - 16, 16)].astype(F32) + gsib[...].astype(F32)
    ggain[...] = both[7:8, :width]
    for a, b in ((gwx, gwx_h), (gwdt, gwdt_h), (galog, galog_h), (gcw, gcw_h), (gcb, gcb_h),
                 (gbias, gbias_h), (gskip, gskip_h), (ggain, ggain_h)):
        write(a, b)
    for c in started:
        c.wait()


def done_edges(ring):
    for c, cond in ring.edges:
        @pl.when(cond)
        def _():
            c.wait_send()


def on_device(n, tokens, gain, w_in, w_out, conv_w, conv_b, w_x, w_dt, dt_bias, a_log, d_skip, lengths, cotangent):
    rows, width = tokens.shape
    inner = w_out.shape[0]
    state = a_log.shape[1]
    rank = w_dt.shape[1]
    g_in, g_out = log_split(n)
    g3 = max(n // 16, 1)
    hw = inner // 2
    cells = state * inner // LANES
    gain = gain.reshape(1, width)
    w_xt = jnp.swapaxes(w_x, 1, 2)
    nsem = 24 + g_in + g_out + 3 * 32 + 3 * g3
    vm = pltpu.VMEM
    sds = jax.ShapeDtypeStruct
    ins = (tokens, gain, w_in, w_out, conv_w, conv_b, w_xt, w_dt, dt_bias, a_log, d_skip, cotangent)
    def bufs(two, k, lanes):
        if two[0]:
            return [vm((4, 4 * k, lanes), B16), vm((4 * k, lanes), B16), vm((4, k, lanes), B16)]
        return [vm((16, k, lanes), B16)]

    k = width // 16
    scratch = [vm(x.shape, x.dtype) for x in ins] + [
        pltpu.SemaphoreType.DMA((len(ins),)),
        vm((HALO, inner + width), B16), vm((HALO, inner + width), B16),
        vm((rows * state, LANES), B16), vm((rows * state, 2 * LANES), F32),
        *[vm((rows * state, inner), F32)] * 2, *[vm(((rows + 1) * state, inner), F32)] * 2,
        vm((rows, inner), F32), vm((rows, inner), F32), vm((rows, inner), F32),
        vm((HALO + rows, inner), F32), vm((3, rows, inner), F32), vm((3, rows + 2 * HALO, LANES), F32),
        vm((rows + HALO, inner), F32), vm((2 * HALO, inner), F32),
        vm((HALO, inner), B16), vm((HALO, inner), B16),
        *[vm((rows, inner), F32)] * 7, vm((width, rows + HALO), B16), vm((inner, width), B16),
        vm((g_in, 2 * cells + 16, LANES), B16), vm((2, cells + 16, LANES), B16),
        vm((g_out, cells + 16, LANES), B16),
        vm((rows, inner), F32), vm((rows, inner), F32), vm((rows, inner), F32),
        vm((rows, width), F32), vm((rows, width), F32),
        vm((rows, width), B16), vm((rows, width), B16),
        vm((2, width, inner), B16), vm((width, inner), B16), vm((width, inner), B16), *bufs(E_TWO, k, inner), vm((g3, k, inner), B16),
        vm((2, width, hw), B16), vm((width, hw), B16),
        vm((width, hw), B16), *bufs(X_TWO, k, hw), vm((g3, k, hw), B16),
        vm((256, hw), F32), vm((256, hw), B16), *bufs(O_TWO, 16, hw), vm((g3, 16, hw), B16),
        pltpu.SemaphoreType.DMA((nsem,)), pltpu.SemaphoreType.DMA((nsem,)),
    ]
    mids = [
        vm((rows, width), B16), vm((rows, width), F32), vm((width, inner), B16), vm((width, inner), B16),
        vm((width, hw), B16), vm((width, hw), B16), vm((256, hw), B16), vm((16, hw), B16),
    ]
    in_vmem = pl.BlockSpec(memory_space=pltpu.VMEM)
    in_hbm = pl.BlockSpec(memory_space=pltpu.HBM)
    sums = pl.pallas_call(
        functools.partial(kernel, n, nsem),
        out_shape=mids,
        in_specs=[in_hbm] * len(ins) + [pl.BlockSpec(memory_space=pltpu.SMEM)],
        out_specs=[in_vmem] * len(mids),
        scratch_shapes=scratch,
        compiler_params=pltpu.CompilerParams(
            collective_id=0, has_side_effects=True, vmem_limit_bytes=56 * 2**20
        ),
    )(*ins, lengths)
    outs = (
        sds((rows, width), B16), sds((rows, width), F32), sds((1, width), F32),
        sds(w_in.shape, F32), sds(w_out.shape, F32), sds(conv_w.shape, F32), sds(conv_b.shape, F32),
        sds(w_xt.shape, F32), sds(w_dt.shape, F32), sds(dt_bias.shape, F32), sds(a_log.shape, F32),
        sds(d_skip.shape, F32),
    )
    res = pl.pallas_call(
        functools.partial(finish, (w_xt.shape[1], rank, state)),
        out_shape=outs,
        in_specs=[in_vmem] * len(mids),
        out_specs=[in_hbm] * len(outs),
        scratch_shapes=[vm(x.shape, x.dtype) for x in outs[2:]] + [pltpu.SemaphoreType.DMA((len(outs),))],
        compiler_params=pltpu.CompilerParams(vmem_limit_bytes=8 * 2**20),
    )(*sums)
    return (res[0], res[1], res[2].reshape(width)) + tuple(res[3:7]) + (jnp.swapaxes(res[7], 1, 2),) + tuple(res[8:])


def solution(mesh):
    d1, d2 = P("dir", None), P("dir", None, None)
    return jax.shard_map(
        functools.partial(on_device, mesh.shape["seq"]),
        mesh=mesh,
        in_specs=(P("seq", None), P(), P(), P(), d2, d1, d2, d2, d1, d2, d1, P(), P("seq", None)),
        out_specs=(P("seq", None), P("seq", None), P(), P(), P(), d2, d1, d2, d2, d1, d2, d1),
        check_vma=False,
    )
```

```python
import functools

import jax
import jax.numpy as jnp
from jax import lax
from jax.experimental import pallas as pl
from jax.experimental.pallas import tpu as pltpu
from jax.sharding import PartitionSpec as P

F32 = jnp.float32
B16 = jnp.bfloat16
MESH = pl.DeviceIdType.MESH
NORM_EPS = 1e-05
LOG2E = 1.4426950408889634
RESET = 1e6
HALO = 16
LANES = 128
E_TWO, X_TWO, O_TWO = (True, True, False), (True, False, False), (True, True, True)


def dot(a, b, ca=1, cb=0):
    return lax.dot_general(a, b, (((ca,), (cb,)), ((), ())), preferred_element_type=F32)


def silu_grad(v, sigma):
    return sigma * (1.0 + v * (1.0 - sigma))


def softplus(v):
    u = jnp.exp(-jnp.abs(v))
    s = u / (2.0 + u)
    q = s * s
    p = 1.0 / 13.0
    for k in (11.0, 9.0, 7.0, 5.0, 3.0):
        p = p * q + 1.0 / k
    return jnp.maximum(v, 0.0) + 2.0 * s * (p * q + 1.0)


def log_split(n):
    inner = 1
    while inner * inner * 4 <= n:
        inner *= 2
    return inner, n // inner


class Ring:
    def __init__(self, ssem, rsem, size):
        self.ssem, self.rsem, self.next, self.size = ssem, rsem, 0, size
        self.sent, self.edges = [], []

    def take(self, count):
        base = self.next
        self.next += count
        assert self.next <= self.size
        return base

    def copy(self, src, dst, s, r, dev):
        return pltpu.make_async_remote_copy(
            src_ref=src, dst_ref=dst, send_sem=self.ssem.at[s], recv_sem=self.rsem.at[r],
            device_id=dev, device_id_type=MESH,
        )


class Exchange:
    def __init__(self, ring, size, me, dev):
        self.ring, self.size, self.me, self.dev = ring, size, me, dev
        self.base = ring.take(size)

    def start(self, src, dst):
        self.src, self.dst = src, dst
        for r in range(1, self.size):
            peer = lax.rem(self.me + r, self.size)
            c = self.ring.copy(src(peer), dst(self.me), self.base + r, self.base + self.me, self.dev(peer))
            c.start()
            self.ring.sent.append(c)

    def wait_one(self, r):
        peer = lax.rem(self.me + r, self.size)
        self.ring.copy(
            self.src(peer), self.dst(peer), self.base + r, self.base + peer, self.dev(peer)
        ).wait_recv()

    def wait(self):
        for r in range(1, self.size):
            self.wait_one(r)


def flip(a, mask):
    for b in range(4):
        if mask >> b & 1:
            a = a + (1 << b) * (1 - 2 * lax.rem(a // (1 << b), 2))
    return a


class Sum:
    def __init__(self, ring, n, seq, dirn, own, total, send, recv, over, blocks, two):
        self.ring, self.own, self.total, self.send, self.over = ring, own, total, send, over
        self.blocks, self.k, self.g3 = blocks, total.shape[0] // 16, n // 16
        self.me, hi = lax.rem(seq, 16), seq // 16
        self.hi = hi
        base = seq - self.me
        self.dev = lambda p: (dirn, base + p)
        self.lo, self.mid = lax.rem(self.me, 4), self.me // 4
        self.peers = [flip(self.me, m) for m in range(15, 0, -1)]
        self.out_two, self.back_two, self.far_first = two
        near = lambda p: self.dev(self.me - lax.rem(self.me, 4) + p)
        far = lambda p: self.dev(p * 4 + lax.rem(self.me, 4))
        if self.far_first:
            near, far, self.lo, self.mid = far, near, self.mid, self.lo
        if self.out_two:
            self.recv, self.send2, self.recv2 = recv
            self.ex1, self.ex2 = Exchange(ring, 4, self.lo, near), Exchange(ring, 4, self.mid, far)
        else:
            (self.recv,) = recv
            self.s1 = ring.take(16)
        if self.back_two:
            self.back2, self.back1 = Exchange(ring, 4, self.mid, far), Exchange(ring, 4, self.lo, near)
        else:
            self.s2 = ring.take(16)
        self.top = Exchange(ring, self.g3, hi, lambda p: (dirn, seq + (p - hi) * 16)) if self.g3 > 1 else None

    def block(self, p):
        if (self.out_two or self.back_two) and not self.far_first:
            return lax.rem(p, 4) * 4 + p // 4
        return p if self.blocks == 16 else lax.rem(p + 12, 16)

    def at(self, b, count=1):
        size = self.k * count
        return pl.ds(pl.multiple_of(b * size, size), size)

    def owns(self, p, body):
        if self.blocks < 16:
            pl.when(self.block(p) < self.blocks)(body)
        else:
            body()

    def go(self, c, owner):
        self.owns(owner, c.start)
        if self.blocks < 16:
            self.ring.edges.append((c, self.block(owner) < self.blocks))
        else:
            self.ring.sent.append(c)

    def scatter(self):
        self.send[...] = self.own(slice(None)).astype(B16)
        if self.out_two:
            self.ex1.start(lambda p: self.send.at[self.at(p, 4)], lambda s: self.recv.at[s])
            return
        for r, p in enumerate(self.peers):
            src = self.send.at[self.at(self.block(p))]
            self.go(self.ring.copy(src, self.recv.at[self.me], self.s1 + r, self.s1 + self.me, self.dev(p)), p)

    def scatter2(self):
        self.recv[self.lo] = jnp.zeros(self.recv.shape[1:], B16)
        self.ex1.wait()
        acc = self.own(self.at(self.lo, 4))
        for j in range(4):
            acc = acc + self.recv[j].astype(F32)
        self.send2[...] = acc.astype(B16)
        self.ex2.start(lambda p: self.send2.at[self.at(p)], lambda s: self.recv2.at[s])

    def add(self):
        if self.out_two:
            self.recv2[self.mid] = jnp.zeros(self.recv2.shape[1:], B16)
            self.ex2.wait()
            parts, count = self.recv2, 4
            acc = self.send2[self.at(self.mid)].astype(F32)
        else:
            self.recv[self.me] = jnp.zeros(self.recv.shape[1:], B16)
            for r, p in reversed(list(enumerate(self.peers))):
                there = self.send.at[pl.ds(0, self.k)]
                self.ring.copy(there, self.recv.at[p], self.s1 + r, self.s1 + p, self.dev(p)).wait_recv()
            parts, count = self.recv, 16
            acc = self.own(self.at(self.block(self.me)))
        for j in range(count):
            acc = acc + parts[j].astype(F32)
        if self.top is not None:
            self.over[self.hi] = acc.astype(B16)
            self.top.start(lambda p: self.over.at[self.hi], lambda s: self.over.at[s])
            self.top.wait()
            for _ in range(1, self.g3):
                self.ring.sent.pop().wait_send()
            acc = self.over[0].astype(F32)
            for j in range(1, self.g3):
                acc = acc + self.over[j].astype(F32)
        self.total[self.at(self.block(self.me))] = acc.astype(B16)

    def gather(self):
        self.owns(self.me, self.add)
        mine = self.total.at[self.at(self.block(self.me))]
        if self.back_two:
            there = lambda s: self.total.at[self.at(self.lo * 4 + s)]
            self.back2.start(lambda p: there(self.mid), there)
            return
        for r, p in enumerate(self.peers):
            self.go(self.ring.copy(mine, mine, self.s2 + r, self.s2 + self.me, self.dev(p)), self.me)

    def gather1(self):
        self.back2.wait()
        there = lambda s: self.total.at[self.at(s, 4)]
        self.back1.start(lambda p: there(self.lo), there)

    def took(self, p):
        there = self.total.at[self.at(self.block(p))]
        self.owns(p, self.ring.copy(there, there, self.s2, self.s2 + p, self.dev(p)).wait_recv)

    def finish(self):
        for p in reversed(self.peers):
            self.took(p)

    def mirror(self, other, sibling):
        copies = []

        def on(quarter):
            s = self.ring.take(1)
            rows = self.at(quarter, 4)
            c = self.ring.copy(self.total.at[rows], other.at[rows], s, s, sibling)
            c.start()
            self.ring.sent.append(c)
            copies.append(c)

        if self.back_two:
            for r in range(4):
                p = lax.rem(self.lo + r, 4)
                if r > 0:
                    self.back1.wait_one(r)
                on(p)
        else:
            by_lo = self.out_two and not self.far_first
            for r in range(4):
                quarter = lax.rem((self.lo if by_lo else self.mid) + r, 4)
                for x in range(4):
                    other_at = lax.rem((self.mid if by_lo else self.lo) + x, 4)
                    p = other_at * 4 + quarter if by_lo else quarter * 4 + other_at
                    if r + x > 0:
                        self.took(p)
                on(quarter)
        return copies


def kernel(n, nsem, *refs):
    (tok_h, gain_h, win_h, wout_h, cw_h, cb_h, wx_h, wdt_h, bias_h, alog_h, skip_h, cot_h, len_r,
     out_r, ing_r, etotal, esib, xtotal, xsib, ototal, gsib,
     tok_r, gain_r, win_r, wout_r, cw_r, cb_r, wx_r, wdt_r, bias_r, alog_r, skip_r, cot_r, lsem,
     tail_s, halo, picked, bcr, dref, cpr, hs, pr, sdr, sar, gyr, xpad, taps, later, gpad, gext, ghsend, ghrecv,
     sgr, cgr, zgr, gsr, skr, gyq, yl, ntx, woutf,
     xin1, xsend2, xin2, yr, adjr, dtar, bsend, brecv, vsend, vrecv,
     epair, eprecv, esend, *rest) = refs
    erecv, rest = rest[:3 if E_TWO[0] else 1], rest[3 if E_TWO[0] else 1:]
    eover, xpair, xprecv, xsend, *rest = rest
    xrecv, rest = rest[:3 if X_TWO[0] else 1], rest[3 if X_TWO[0] else 1:]
    xover, opart, osend, *rest = rest
    orecv, rest = rest[:3 if O_TWO[0] else 1], rest[3 if O_TWO[0] else 1:]
    oover, ssem, rsem = rest
    rows, width = tok_r.shape
    inner = wout_r.shape[0]
    state = alog_r.shape[1]
    chunks = inner // LANES
    dirn = lax.axis_index("dir")
    seq = lax.axis_index("seq")
    place = seq + dirn * (n - 1 - 2 * seq)
    seq_at = lambda p: p + dirn * (n - 1 - 2 * p)
    dev_at = lambda p: (dirn, seq_at(p))
    sibling = (1 - dirn, seq)
    g_in, g_out = log_split(n)
    lo = lax.rem(place, g_in)
    hi = place // g_in
    ring = Ring(ssem, rsem, nsem)
    up = lax.rem(place + 1, n)
    down = lax.rem(place + n - 1, n)

    barrier = pltpu.get_barrier_semaphore()
    line, s_hi = lax.rem(seq, 16), seq // 16
    peers = [sibling, dev_at(up), dev_at(down)]
    if all(E_TWO[:2] + X_TWO[:2] + O_TWO[:2]):
        near, far = lax.rem(line, 4), line // 4
        peers += [(dirn, seq - near + lax.rem(near + r, 4)) for r in range(1, 4)]
        peers += [(dirn, seq + (lax.rem(far + r, 4) - far) * 4) for r in range(1, 4)]
    else:
        peers += [(dirn, seq - line + lax.rem(line + r, 16)) for r in range(1, 16)]
    if n != 16:
        peers += [(dirn, seq + (lax.rem(s_hi + r, n // 16) - s_hi) * 16) for r in range(1, n // 16)]
        peers += [dev_at(hi * g_in + lax.rem(lo + r, g_in)) for r in range(1, g_in)]
        peers += [dev_at(lax.rem(hi + r, g_out) * g_in + lo) for r in range(1, g_out)]
    for dev in peers:
        pl.semaphore_signal(barrier, inc=1, device_id=dev, device_id_type=MESH)

    loads = {}
    pairs = [(tok_h, tok_r), (gain_h, gain_r), (win_h, win_r), (cot_h, cot_r), (wout_h, wout_r), (cw_h, cw_r),
             (cb_h, cb_r), (wx_h, wx_r), (wdt_h, wdt_r), (bias_h, bias_r), (alog_h, alog_r), (skip_h, skip_r)]
    for i, (a, b) in enumerate(pairs):
        loads[i] = pltpu.make_async_copy(a, b, lsem.at[i])
        loads[i].start()

    def turn(size):
        r = lax.broadcasted_iota(jnp.int32, (size, size), 0)
        c = lax.broadcasted_iota(jnp.int32, (size, size), 1)
        return jnp.where(c == r + dirn * (size - 1 - 2 * r), 1.0, 0.0).astype(B16)

    turn_t, turn_f = turn(rows), turn(width)
    turned = lambda v, tt: dot(dot(tt, v).astype(B16), turn_f)

    total = n * rows
    q = lax.broadcasted_iota(jnp.int32, (rows + 2 * HALO, LANES), 0) + (place * rows - HALO)
    dist = jnp.full(q.shape, 1 << 30, jnp.int32)
    before = jnp.int32(0)
    for w in range(len_r.shape[0]):
        after = before + len_r[w]
        delta = q - (before + dirn * (total - after - before))
        dist = jnp.where((delta >= 0) & (delta < dist), delta, dist)
        before = after
    over_lanes = lambda v: jnp.concatenate([v] * (inner // v.shape[1]), axis=1)
    for k in range(1, 4):
        later[k - 1] = jnp.where((dist >= k) & (q < total), 1.0, 0.0)
    dist_own = over_lanes(dist[HALO:HALO + rows])

    def normalise(v):
        inv = lax.rsqrt(jnp.mean(v * v, axis=1, keepdims=True) + NORM_EPS)
        vr = v * inv
        return inv, vr, (vr * gain_r[...]).astype(B16)

    for i in range(3):
        loads[i].wait()
    tok = turned(tok_r[...], turn_t)
    inv, vr, normed = normalise(tok)
    proj = dot(normed, win_r[...])
    xi_b = proj[:, :inner].astype(B16)
    xi = xi_b.astype(F32)
    zgate = proj[:, inner:]
    xpad[pl.ds(0, HALO)] = jnp.zeros((HALO, inner), F32)
    xpad[pl.ds(HALO, rows)] = xi
    tail_s[:, :inner] = xi_b[rows - HALO:]
    tail_s[:, inner:] = tok[rows - HALO:].astype(B16)

    pl.semaphore_wait(barrier, len(peers))
    b0 = ring.take(1)
    tok_copy = ring.copy(tail_s, halo, b0, b0, dev_at(up))
    ring.edges.append((tok_copy, place < n - 1))

    @pl.when(place < n - 1)
    def _():
        tok_copy.start()

    @pl.when(place == 0)
    def _():
        halo[...] = jnp.zeros(halo.shape, B16)

    for i in range(3, len(pairs)):
        loads[i].wait()
    cot = turned(cot_r[...], turn_t).astype(B16)
    sig_z = jax.nn.sigmoid(zgate)
    gate = zgate * sig_z
    gmix = dot(cot, wout_r[...], 1, 1)
    gy = gmix * gate
    gyr[...] = gy
    rate = -jnp.exp(alog_r[0])
    rate2 = rate * LOG2E
    cut = lambda v: [v[:, c * LANES:(c + 1) * LANES] for c in range(chunks)]
    a2 = cut(rate2)
    a1 = cut(rate)

    def drive(count):
        conv = xpad[pl.ds(HALO, count)] * cw_r[0, 0:1] + cb_r[...]
        for k in range(1, 4):
            tap = jnp.where(dist_own[:count] >= k, xpad[pl.ds(HALO - k, count)], 0.0)
            conv = conv + tap * cw_r[0, k:k + 1]
        sig_c = jax.nn.sigmoid(conv)
        act_b = (conv * sig_c).astype(B16)
        low_t = dot(wx_r[0, pl.ds(0, state)], act_b, 1, 1).astype(B16)
        bc = dot(act_b, wx_r[0, pl.ds(state, 2 * state)], 1, 1)
        pre = dot(low_t, wdt_r[0], 0, 0) + bias_r[...]
        step = softplus(pre)
        sd = jnp.where(dist_own[:count] == 0, RESET, step)
        sdr[pl.ds(0, count)] = sd
        sar[pl.ds(0, count)] = step * act_b.astype(F32)
        return conv, sig_c, act_b, low_t, pre, step, sd, bc

    wide = 2 * state
    lane_k = lax.broadcasted_iota(jnp.int32, (state, LANES), 1)
    row_k = lax.broadcasted_iota(jnp.int32, (state, LANES), 0)
    own_k = jnp.where((lane_k < 2 * wide) & (lax.rem(lane_k, state) == row_k), 1.0, 0.0)
    fan_r = lax.rem(lax.broadcasted_iota(jnp.int32, (LANES, 2 * LANES), 0), wide) // state
    fan_c = lax.broadcasted_iota(jnp.int32, (LANES, 2 * LANES), 1) // LANES
    fan = jnp.where(fan_r == fan_c, 1.0, 0.0).astype(B16)

    def spread(bc, first):
        count = bc.shape[0]
        top = bc.astype(B16).astype(F32)
        none = jnp.zeros((count, LANES - 2 * wide), F32)
        both = jnp.concatenate([top, bc - top, none], axis=1)
        for t in range(count):
            picked[pl.ds((first + t) * state, state)] = (both[t:t + 1] * own_k).astype(B16)
        at = pl.ds(first * state, count * state)
        bcr[at] = dot(picked[at], fan)

    def summarise(g, carry):
        h, p, l = [list(x) for x in carry]
        at8 = pl.ds(pl.multiple_of(g * 8, 8), 8)
        sd8, sa8, gy8 = sdr[at8], sar[at8], gyr[at8]
        for c in range(chunks):
            lane = slice(c * LANES, (c + 1) * LANES)
            for j in range(8):
                at = pl.ds(pl.multiple_of((g * 8 + j) * state, state), state)
                br, cr = bcr[at, :LANES], bcr[at, LANES:]
                d = jnp.exp2(sd8[j:j + 1, lane] * a2[c])
                dref[at, lane] = d
                h[c] = d * h[c] + sa8[j:j + 1, lane] * br
                p[c] = p[c] * d
                l[c] = l[c] + p[c] * (gy8[j:j + 1, lane] * cr)
        return tuple(h), tuple(p), tuple(l)

    zero = tuple(jnp.zeros((state, LANES), F32) for _ in range(chunks))
    one = tuple(jnp.ones((state, LANES), F32) for _ in range(chunks))
    join = lambda v: jnp.concatenate(v, axis=1)
    head = HALO // 8

    whole = drive(rows)
    spread(whole[7][HALO:], HALO)
    h_late, p_late, l_late = lax.fori_loop(head, rows // 8, summarise, (zero, one, zero), unroll=2)

    @pl.when(place > 0)
    def _():
        tok_copy.wait_recv()

    xpad[pl.ds(0, HALO)] = halo[:, :inner].astype(F32)
    start = drive(HALO)
    low_first = jnp.concatenate([start[3].astype(F32), jnp.zeros((state, rows - HALO), F32)], axis=1)
    lane_low = lax.broadcasted_iota(jnp.int32, low_first.shape, 1)
    dt_low = jnp.where(lane_low < HALO, low_first, whole[3].astype(F32)).astype(B16)
    patch = lambda i: jnp.concatenate([start[i], whole[i][HALO:]], axis=0)
    conv, sig_c, act_b, pre, step, sd = [patch(i) for i in (0, 1, 2, 4, 5, 6)]
    act = act_b.astype(F32)
    spread(start[7], 0)
    h_first, p_first, l_first = lax.fori_loop(0, head, summarise, (zero, one, zero), unroll=2)
    h_sum = join(h_late) + join(p_late) * join(h_first)
    l_sum = join(l_first) + join(p_first) * join(l_late)

    def pair_rows(v):
        top = v.astype(B16).astype(F32)
        both = cut(top) + cut(v - top) + [jnp.zeros((16 - 2 * chunks, LANES), F32)]
        return jnp.concatenate(both, axis=0).astype(B16)

    blk_s = chunks * state
    stack = lambda v: jnp.concatenate(cut(v), axis=0).astype(B16)
    unstack = lambda v, at: join([v[at + c * state:at + (c + 1) * state].astype(F32) for c in range(chunks)])
    def unpair1(v):
        r = v[blk_s:blk_s + 16].astype(F32)
        return join([r[c:c + 1] + r[chunks + c:chunks + c + 1] for c in range(chunks)])
    xin1[lo, pl.ds(0, blk_s)] = stack(h_sum)
    xin1[lo, pl.ds(blk_s, 16)] = pair_rows(jnp.sum(sd, axis=0, keepdims=True))
    xin1[lo, pl.ds(blk_s + 16, blk_s)] = stack(l_sum)
    ex1 = Exchange(ring, g_in, lo, lambda p: dev_at(hi * g_in + p))
    ex1.start(lambda p: xin1.at[lo], lambda s: xin1.at[s])

    sub = lax.broadcasted_iota(jnp.int32, (8, LANES), 0)
    lane_at = lax.broadcasted_iota(jnp.int32, (state, LANES), 1)

    def sum_rows(v):
        for bit in (1, 2, 4):
            mine = lax.rem(sub // bit, 2) == 0
            v = [
                jnp.where(mine, a, b) + pltpu.roll(jnp.where(mine, b, a), bit, 0)
                for a, b in zip(v[::2], v[1::2])
            ]
        return v[0]

    halve = lambda v: v[:8] + v[8:]
    hs[pl.ds(0, state)] = jnp.zeros((state, inner), F32)
    pr[pl.ds(0, state)] = jnp.ones((state, inner), F32)

    def prepare(g, carry):
        h, p = list(carry[0]), list(carry[1])
        at8 = pl.ds(pl.multiple_of(g * 8, 8), 8)
        sa8 = sar[at8]
        for c in range(chunks):
            lane = slice(c * LANES, (c + 1) * LANES)
            ys = []
            for j in range(8):
                at = pl.ds(pl.multiple_of((g * 8 + j) * state, state), state)
                nxt = pl.ds(pl.multiple_of((g * 8 + j + 1) * state, state), state)
                d, cr = dref[at, lane], bcr[at, LANES:]
                h[c] = d * h[c] + sa8[j:j + 1, lane] * bcr[at, :LANES]
                p[c] = p[c] * d
                hs[nxt, lane] = h[c]
                pr[nxt, lane] = p[c]
                cpr[at, lane] = p[c] * cr
                ys.append(halve(h[c] * cr))
            yl[at8, lane] = sum_rows(ys)
        return tuple(h), tuple(p)

    lax.fori_loop(0, rows // 8, prepare, (zero, one), unroll=2)

    ex1.wait()
    sums = [unpair1(xin1[j]) for j in range(g_in)]
    fwd = bwd = fwd_all = bwd_all = jnp.zeros((state, inner), F32)
    s_fwd = s_bwd = s_all = jnp.zeros((1, inner), F32)
    for j in range(g_in):
        fade = jnp.exp2(rate2 * sums[j])
        fwd_all = fade * fwd_all + unstack(xin1[j], 0)
        fwd = jnp.where(j < lo, fwd_all, fwd)
        s_all = s_all + sums[j]
        s_fwd = jnp.where(j < lo, s_all, s_fwd)
    for j in reversed(range(g_in)):
        fade = jnp.exp2(rate2 * sums[j])
        bwd_all = fade * bwd_all + unstack(xin1[j], blk_s + 16)
        bwd = jnp.where(j > lo, bwd_all, bwd)
        s_bwd = jnp.where(j > lo, s_bwd + sums[j], s_bwd)
    s_pair = pair_rows(s_all)
    for k, v in enumerate((fwd_all, bwd_all)):
        xsend2[k, pl.ds(0, blk_s)] = stack(v)
        xsend2[k, pl.ds(blk_s, 16)] = s_pair
    xin2[hi] = jnp.zeros(xin2.shape[1:], B16)
    ex2 = Exchange(ring, g_out, hi, lambda p: dev_at(p * g_in + lo))
    ex2.start(lambda p: xsend2.at[jnp.where(p > hi, 0, 1)], lambda s: xin2.at[s])
    _, vr_h, normed_h = normalise(halo[:, inner:].astype(F32))
    for k in range(1, 4):
        taps[k - 1] = jnp.where(dist_own >= k, xpad[pl.ds(HALO - k, rows)], 0.0)
    ntx[...] = jnp.concatenate([normed, normed_h], axis=0).T
    sgr[...] = jax.nn.sigmoid(pre)
    cgr[...] = silu_grad(conv, sig_c)
    zgr[...] = gmix * silu_grad(zgate, sig_z)
    gsr[...] = gy * skip_r[...]
    skr[...] = skip_r[...] * act
    woutf[...] = dot(wout_r[...], turn_f).astype(B16)
    gskip = jnp.sum(gy * act, axis=0, keepdims=True)
    gpad[pl.ds(0, 8)] = jnp.zeros((8, inner), F32)
    gpad[pl.ds(8, rows)] = gy
    gyq[...] = gpad[pl.ds(7, rows)]

    ex2.wait()
    h_in = l_in = jnp.zeros((state, inner), F32)
    for k in range(g_out):
        new = jnp.exp2(rate2 * unpair1(xin2[k])) * h_in
        h_in = jnp.where(k < hi, new + unstack(xin2[k], 0), h_in)
    for k in reversed(range(g_out)):
        new = jnp.exp2(rate2 * unpair1(xin2[k])) * l_in
        l_in = jnp.where(k > hi, new + unstack(xin2[k], 0), l_in)
    h_in = jnp.exp2(rate2 * s_fwd) * h_in + fwd
    l_in = jnp.exp2(rate2 * s_bwd) * l_in + bwd

    hin = cut(h_in)

    def forward(g, carry):
        at8 = pl.ds(pl.multiple_of(g * 8, 8), 8)
        for c in range(chunks):
            lane = slice(c * LANES, (c + 1) * LANES)
            ys = []
            for j in range(8):
                at = pl.ds(pl.multiple_of((g * 8 + j) * state, state), state)
                ys.append(halve(cpr[at, lane] * hin[c]))
            yr[at8, lane] = yl[at8, lane] + sum_rows(ys)
        return carry

    lax.fori_loop(0, rows // 8, forward, 0, unroll=4)
    none = jnp.zeros((state, rows), F32)
    y = yr[...] + skr[...]
    mixed = (y * gate).astype(B16)
    gz = (zgr[...] * y).astype(B16)

    epair[0] = dot(ntx[:, :rows], gz).astype(B16)
    gwo = dot(mixed, cot, 0, 0).astype(B16)
    epair[1, :, :width] = gwo[:width]
    epair[1, :, width:] = gwo[width:]
    be = ring.take(1)
    e_copy = ring.copy(epair.at[1 - dirn], eprecv, be, be, sibling)
    e_copy.start()
    ring.sent.append(e_copy)

    def backward(i, carry):
        m, acc, gb, gc = list(carry[0]), list(carry[1]), carry[2], carry[3]
        g = rows // 8 - 1 - i
        at8 = pl.ds(pl.multiple_of(g * 8, 8), 8)
        sd8, gy8, sa8, gq8 = sdr[at8], gyr[at8], sar[at8], gyq[at8]
        over_b, over_c = [None] * 8, [None] * 8
        for c in range(chunks):
            lane = slice(c * LANES, (c + 1) * LANES)
            adjs, dts = [None] * 8, [None] * 8
            for j in reversed(range(8)):
                at = pl.ds(pl.multiple_of((g * 8 + j) * state, state), state)
                lam = m[c] + gy8[j:j + 1, lane] * bcr[at, LANES:]
                m[c] = dref[at, lane] * lam
                h = hs[at, lane] + pr[at, lane] * hin[c]
                r = m[c] * h * a1[c]
                acc[c] = acc[c] + r * sd8[j:j + 1, lane]
                adjs[j] = halve(lam * bcr[at, :LANES])
                dts[j] = halve(r)
                new_b, new_c = lam * sa8[j:j + 1, lane], h * gq8[j:j + 1, lane]
                over_b[j] = new_b if c == 0 else over_b[j] + new_b
                over_c[j] = new_c if c == 0 else over_c[j] + new_c
            adjr[at8, lane] = sum_rows(adjs)
            dtar[at8, lane] = sum_rows(dts)
        for j in range(8):
            t = g * 8 + j
            gb = jnp.where(lane_at == t, jnp.sum(over_b[j], axis=1, keepdims=True), gb)
            gc = jnp.where(lane_at == t - 1, jnp.sum(over_c[j], axis=1, keepdims=True), gc)
        return tuple(m), tuple(acc), gb, gc

    h_out = hs[pl.ds(rows * state, state)] + pr[pl.ds(rows * state, state)] * h_in
    g_last = jnp.sum(h_out * gyr[pl.ds(rows - 1, 1)], axis=1, keepdims=True)
    none_c = jnp.where(lane_at == rows - 1, g_last, none)
    carry = lax.fori_loop(0, 6, backward, (tuple(cut(l_in)), zero, none, none_c), unroll=6)
    e_own = lambda at: epair[dirn, at].astype(F32) + eprecv[at].astype(F32)
    early = Sum(ring, n, seq, dirn, e_own, etotal, esend, erecv, eover, 16, E_TWO)
    e_copy.wait_recv()
    early.scatter()
    _, galog, g_b, g_c = lax.fori_loop(6, rows // 8, backward, carry, unroll=5)
    galog = join(galog)
    adj = adjr[...]
    gpre = (dtar[...] + adj * act) * sgr[...]
    gbias = jnp.sum(gpre, axis=0, keepdims=True)
    gpre = gpre.astype(B16)
    glow = dot(gpre, wdt_r[0], 1, 1).astype(B16)
    gbc = jnp.concatenate([g_b, g_c], axis=0).astype(B16)
    gact = gsr[...] + adj * step + dot(gbc, wx_r[0, pl.ds(state, 2 * state)], 0, 0)
    gact = gact + dot(glow, wx_r[0, pl.ds(0, state)])
    gconv_b = (gact * cgr[...]).astype(B16)
    gconv = gconv_b.astype(F32)

    gpad[pl.ds(0, rows)] = gconv
    gpad[pl.ds(rows, HALO)] = jnp.zeros((HALO, inner), F32)
    gext[pl.ds(0, HALO)] = jnp.zeros((HALO, inner), F32)
    gext[pl.ds(HALO, HALO)] = gconv[:HALO]
    gxi = gconv * cw_r[0, 0:1]
    gxe = jnp.zeros((HALO, inner), F32)
    for k in range(1, 4):
        w = cw_r[0, k:k + 1]
        gxi = gxi + gpad[pl.ds(k, rows)] * over_lanes(later[k - 1, pl.ds(HALO + k, rows)]) * w
        gxe = gxe + gext[pl.ds(k, HALO)] * over_lanes(later[k - 1, pl.ds(k, HALO)]) * w
    gxi_b = jnp.concatenate([gxi, gxe], axis=0).astype(B16)
    gwx_half = dot(ntx[...], gxi_b).astype(B16)
    hw = inner // 2
    xpair[0] = gwx_half[:, :hw]
    xpair[1] = gwx_half[:, hw:]
    bx = ring.take(1)
    x_copy = ring.copy(xpair.at[1 - dirn], xprecv, bx, bx, sibling)
    x_copy.start()
    ring.sent.append(x_copy)
    ghsend[...] = gconv_b[:HALO]
    bh = ring.take(1)
    h_copy = ring.copy(ghsend, ghrecv, bh, bh, dev_at(down))
    ring.edges.append((h_copy, place > 0))

    @pl.when(place > 0)
    def _():
        h_copy.start()

    gwx_t = jnp.concatenate([dot(glow, act_b, 0, 0), dot(gbc, act_b)], axis=0)
    gwdt = dot(dt_low, gpre)
    gn_x = dot(gxi_b, win_r[:, :inner], 1, 1)
    gn_z = dot(gz, win_r[:, inner:], 1, 1)
    ggain = jnp.sum((gn_x[:rows] + gn_z) * vr, axis=0, keepdims=True)
    ggain = ggain + jnp.sum(gn_x[rows:] * vr_h, axis=0, keepdims=True)
    gcb = jnp.sum(gconv, axis=0, keepdims=True)
    gcw = [jnp.sum(gconv * (xi if k == 0 else taps[k - 1]), axis=0, keepdims=True) for k in range(4)]
    pad_gain = jnp.concatenate([ggain, jnp.zeros((1, inner - width), F32)], axis=1)
    tail = jnp.concatenate(gcw + [gcb, gbias, gskip, pad_gain], axis=0)
    row = 0
    for part in (gwx_t, gwdt, galog, tail):
        k = part.shape[0]
        opart[pl.ds(row, k)] = part[:, :hw]
        opart[pl.ds(row + k, k)] = part[:, hw:]
        row += 2 * k
    opart[pl.ds(row, opart.shape[0] - row)] = jnp.zeros((opart.shape[0] - row, hw), F32)
    own = Sum(ring, n, seq, dirn, lambda at: opart[at], ototal, osend, orecv, oover, 16 if any(O_TWO[:2]) else -(-row // 16), O_TWO)
    own.scatter()
    x_own = lambda at: xpair[dirn, at].astype(F32) + xprecv[at].astype(F32)
    xlate = Sum(ring, n, seq, dirn, x_own, xtotal, xsend, xrecv, xover, 16, X_TWO)
    x_copy.wait_recv()
    xlate.scatter()
    if E_TWO[0]:
        early.scatter2()
    for v, two in ((own, O_TWO), (xlate, X_TWO)):
        if two[0]:
            v.scatter2()
    bsend[...] = dot(dot(turn_t, mixed).astype(B16), woutf[...])
    bb = ring.take(1)
    b_copy = ring.copy(bsend, brecv, bb, bb, sibling)
    b_copy.start()
    ring.sent.append(b_copy)

    early.gather()

    @pl.when(place < n - 1)
    def _():
        h_copy.wait_recv()
        gpad[pl.ds(rows, HALO)] = ghrecv[...].astype(F32)

    edge_x = gpad[pl.ds(rows - HALO, HALO)] * cw_r[0, 0:1]
    for k in range(1, 4):
        ok = over_lanes(later[k - 1, pl.ds(rows + k, HALO)])
        edge_x = edge_x + gpad[pl.ds(rows - HALO + k, HALO)] * ok * cw_r[0, k:k + 1]
    gn_edge = dot(edge_x.astype(B16), win_r[:, :inner], 1, 1)
    gn = jnp.concatenate([gn_x[:rows - HALO], gn_edge], axis=0) + gn_z
    scaled = gn * gain_r[...]
    gv = inv * (scaled - vr * jnp.mean(scaled * vr, axis=1, keepdims=True))
    vsend[...] = turned(gv.astype(B16), turn_t).astype(B16)
    bv = ring.take(1)
    v_copy = ring.copy(vsend, vrecv, bv, bv, sibling)
    v_copy.start()
    ring.sent.append(v_copy)

    own.gather()
    xlate.gather()
    b_copy.wait_recv()
    out_r[...] = (tok_r[...].astype(F32) + (bsend[...] + brecv[...])).astype(B16)
    v_copy.wait_recv()
    ing_r[...] = cot_r[...].astype(F32) + (vsend[...].astype(F32) + vrecv[...].astype(F32))
    for v, two in ((early, E_TWO), (own, O_TWO), (xlate, X_TWO)):
        if two[1]:
            v.gather1()
    if O_TWO[1]:
        own.back1.wait()
    else:
        own.finish()
    bo = ring.take(1)
    gat = pl.ds(row - 16, 16)
    os_copy = ring.copy(ototal.at[gat], gsib, bo, bo, sibling)
    os_copy.start()
    ring.sent.append(os_copy)
    copies = xlate.mirror(xsib, sibling)
    copies += early.mirror(esib, sibling)
    for c in copies:
        c.wait_recv()
    os_copy.wait_recv()
    done_edges(ring)
    for c in ring.sent:
        c.wait_send()


def finish(sizes, *refs):
    (out_v, ing_v, etotal, esib, xtotal, xsib, ototal, gsib,
     out_h, ing_h, ggain_h, gwin_h, gwout_h, gcw_h, gcb_h, gwx_h, gwdt_h, gbias_h, galog_h, gskip_h,
     ggain, gwin, gwout, gcw, gcb, gwx, gwdt, gbias, galog, gskip, sems) = refs
    nx, ns, state = sizes
    dirn = lax.axis_index("dir")
    width = ing_v.shape[1]
    hw = xtotal.shape[1]
    inner = 2 * hw
    started = []

    def write(src, dst):
        c = pltpu.make_async_copy(src, dst, sems.at[len(started)])
        c.start()
        started.append(c)

    write(out_v, out_h)
    write(ing_v, ing_h)

    def halves(mine, other):
        a, b = mine[...].astype(F32), other[...].astype(F32)
        return jnp.where(dirn == 0, a, b), jnp.where(dirn == 0, b, a)

    gz, go = halves(etotal, esib)
    gwout[pl.ds(0, width)] = go[:, :width]
    gwout[pl.ds(width, width)] = go[:, width:]
    write(gwout, gwout_h)
    gwin[:, inner:] = gz
    left, right = halves(xtotal, xsib)
    gwin[:, :hw] = left
    gwin[:, hw:inner] = right
    write(gwin, gwin_h)
    row = 0
    parts = []
    for k in (nx, ns, state, 8):
        both = ototal[pl.ds(row, 2 * k)].astype(F32)
        parts.append(jnp.concatenate([both[:k], both[k:]], axis=1))
        row += 2 * k
    tail = parts[3]
    gwx[0], gwdt[0], galog[0] = parts[:3]
    gcw[0] = tail[0:4]
    gcb[...], gbias[...], gskip[...] = tail[4:5], tail[5:6], tail[6:7]
    both = ototal[pl.ds(row - 16, 16)].astype(F32) + gsib[...].astype(F32)
    ggain[...] = both[7:8, :width]
    for a, b in ((gwx, gwx_h), (gwdt, gwdt_h), (galog, galog_h), (gcw, gcw_h), (gcb, gcb_h),
                 (gbias, gbias_h), (gskip, gskip_h), (ggain, ggain_h)):
        write(a, b)
    for c in started:
        c.wait()


def done_edges(ring):
    for c, cond in ring.edges:
        @pl.when(cond)
        def _():
            c.wait_send()


def on_device(n, tokens, gain, w_in, w_out, conv_w, conv_b, w_x, w_dt, dt_bias, a_log, d_skip, lengths, cotangent):
    rows, width = tokens.shape
    inner = w_out.shape[0]
    state = a_log.shape[1]
    rank = w_dt.shape[1]
    g_in, g_out = log_split(n)
    g3 = max(n // 16, 1)
    hw = inner // 2
    cells = state * inner // LANES
    gain = gain.reshape(1, width)
    w_xt = jnp.swapaxes(w_x, 1, 2)
    nsem = 24 + g_in + g_out + 3 * 32 + 3 * g3
    vm = pltpu.VMEM
    sds = jax.ShapeDtypeStruct
    ins = (tokens, gain, w_in, w_out, conv_w, conv_b, w_xt, w_dt, dt_bias, a_log, d_skip, cotangent)
    def bufs(two, k, lanes):
        if two[0]:
            return [vm((4, 4 * k, lanes), B16), vm((4 * k, lanes), B16), vm((4, k, lanes), B16)]
        return [vm((16, k, lanes), B16)]

    k = width // 16
    scratch = [vm(x.shape, x.dtype) for x in ins] + [
        pltpu.SemaphoreType.DMA((len(ins),)),
        vm((HALO, inner + width), B16), vm((HALO, inner + width), B16),
        vm((rows * state, LANES), B16), vm((rows * state, 2 * LANES), F32),
        *[vm((rows * state, inner), F32)] * 2, *[vm(((rows + 1) * state, inner), F32)] * 2,
        vm((rows, inner), F32), vm((rows, inner), F32), vm((rows, inner), F32),
        vm((HALO + rows, inner), F32), vm((3, rows, inner), F32), vm((3, rows + 2 * HALO, LANES), F32),
        vm((rows + HALO, inner), F32), vm((2 * HALO, inner), F32),
        vm((HALO, inner), B16), vm((HALO, inner), B16),
        *[vm((rows, inner), F32)] * 7, vm((width, rows + HALO), B16), vm((inner, width), B16),
        vm((g_in, 2 * cells + 16, LANES), B16), vm((2, cells + 16, LANES), B16),
        vm((g_out, cells + 16, LANES), B16),
        vm((rows, inner), F32), vm((rows, inner), F32), vm((rows, inner), F32),
        vm((rows, width), F32), vm((rows, width), F32),
        vm((rows, width), B16), vm((rows, width), B16),
        vm((2, width, inner), B16), vm((width, inner), B16), vm((width, inner), B16), *bufs(E_TWO, k, inner), vm((g3, k, inner), B16),
        vm((2, width, hw), B16), vm((width, hw), B16),
        vm((width, hw), B16), *bufs(X_TWO, k, hw), vm((g3, k, hw), B16),
        vm((256, hw), F32), vm((256, hw), B16), *bufs(O_TWO, 16, hw), vm((g3, 16, hw), B16),
        pltpu.SemaphoreType.DMA((nsem,)), pltpu.SemaphoreType.DMA((nsem,)),
    ]
    mids = [
        vm((rows, width), B16), vm((rows, width), F32), vm((width, inner), B16), vm((width, inner), B16),
        vm((width, hw), B16), vm((width, hw), B16), vm((256, hw), B16), vm((16, hw), B16),
    ]
    in_vmem = pl.BlockSpec(memory_space=pltpu.VMEM)
    in_hbm = pl.BlockSpec(memory_space=pltpu.HBM)
    sums = pl.pallas_call(
        functools.partial(kernel, n, nsem),
        out_shape=mids,
        in_specs=[in_hbm] * len(ins) + [pl.BlockSpec(memory_space=pltpu.SMEM)],
        out_specs=[in_vmem] * len(mids),
        scratch_shapes=scratch,
        compiler_params=pltpu.CompilerParams(
            collective_id=0, has_side_effects=True, vmem_limit_bytes=56 * 2**20
        ),
    )(*ins, lengths)
    outs = (
        sds((rows, width), B16), sds((rows, width), F32), sds((1, width), F32),
        sds(w_in.shape, F32), sds(w_out.shape, F32), sds(conv_w.shape, F32), sds(conv_b.shape, F32),
        sds(w_xt.shape, F32), sds(w_dt.shape, F32), sds(dt_bias.shape, F32), sds(a_log.shape, F32),
        sds(d_skip.shape, F32),
    )
    res = pl.pallas_call(
        functools.partial(finish, (w_xt.shape[1], rank, state)),
        out_shape=outs,
        in_specs=[in_vmem] * len(mids),
        out_specs=[in_hbm] * len(outs),
        scratch_shapes=[vm(x.shape, x.dtype) for x in outs[2:]] + [pltpu.SemaphoreType.DMA((len(outs),))],
        compiler_params=pltpu.CompilerParams(vmem_limit_bytes=8 * 2**20),
    )(*sums)
    return (res[0], res[1], res[2].reshape(width)) + tuple(res[3:7]) + (jnp.swapaxes(res[7], 1, 2),) + tuple(res[8:])


def solution(mesh):
    d1, d2 = P("dir", None), P("dir", None, None)
    return jax.shard_map(
        functools.partial(on_device, mesh.shape["seq"]),
        mesh=mesh,
        in_specs=(P("seq", None), P(), P(), P(), d2, d1, d2, d2, d1, d2, d1, P(), P("seq", None)),
        out_specs=(P("seq", None), P("seq", None), P(), P(), P(), d2, d1, d2, d2, d1, d2, d1),
        check_vma=False,
    )
```
